32 devices in a mesh: dp: 8 (over y, x, core), seq: 4 (over z).
Axes of the slice: x: 2, y: 2, z: 4, core: 2. Of those that a mesh axis runs over, the one named last changes fastest.
Arguments:
- latents: bfloat16 [8, 1024, 1536], P('dp', 'seq'), may hold values from -6 to 6
- context: bfloat16 [8, 384, 768], P('dp'), may hold values from -6 to 6
- clip_bounds: int32 [8, 2], P('dp'), may hold values from 1 to 1023, as said below
- timesteps: int32 [8, 3], P('dp'), may hold values from 0 to 999
- self_inward: bfloat16 [1536, 4608], P(('dp', 'seq')), may hold values from -0.1875 to 0.1875
- self_outward: bfloat16 [1536, 1536], P(('dp', 'seq')), may hold values from -2.5 to 2.5
- cross_query: bfloat16 [1536, 1536], P(('dp', 'seq')), may hold values from -0.15625 to 0.15625
- cross_keyval: bfloat16 [768, 3072], P(('dp', 'seq')), may hold values from -0.25 to 0.25
- cross_return: bfloat16 [1536, 1536], P(('dp', 'seq')), may hold values from -0.875 to 0.875
- time_weight: bfloat16 [256, 1536], P(('dp', 'seq')), may hold values from -1.5 to 1.5
- expand_weight: bfloat16 [1536, 12288], P(('dp', 'seq')), may hold values from -0.15625 to 0.15625
- shrink_weight: bfloat16 [6144, 1536], P(('dp', 'seq')), may hold values from -0.15625 to 0.15625
- gain_attend: bfloat16 [1536], P(('dp', 'seq')), may hold values from 0.25 to 1.75
- gain_cross: bfloat16 [1536], P(('dp', 'seq')), may hold values from 0.25 to 1.75
- gain_feed: bfloat16 [1536], P(('dp', 'seq')), may hold values from 0.25 to 1.75
- cotangent: bfloat16 [8, 1024, 1536], P('dp', 'seq'), may hold values from -6 to 6
Outputs:
- block_output: bfloat16 [8, 1024, 1536], P('dp', 'seq')
- grad_latents: float32 [8, 1024, 1536], P('dp', 'seq')
- grad_inward: float32 [1536, 4608], P(('dp', 'seq'))
- grad_outward: float32 [1536, 1536], P(('dp', 'seq'))
- grad_query: float32 [1536, 1536], P(('dp', 'seq'))
- grad_keyval: float32 [768, 3072], P(('dp', 'seq'))
- grad_return: float32 [1536, 1536], P(('dp', 'seq'))
- grad_time: float32 [256, 1536], P(('dp', 'seq'))
- grad_expand: float32 [1536, 12288], P(('dp', 'seq'))
- grad_shrink: float32 [6144, 1536], P(('dp', 'seq'))
- grad_attend: float32 [1536], P(('dp', 'seq'))
- grad_cross: float32 [1536], P(('dp', 'seq'))
- grad_feed: float32 [1536], P(('dp', 'seq'))
The draws below stay inside these ranges and needn't reach their ends.
Inputs may be any that keep to these rules, and one draw needn't show every extreme that they name: `clip_bounds`: in each row the first entry lies in 1 to 255 and the second in 769 to 1023, so every clip is non-empty and the second clip runs from the first index of seq to the last.
All inputs are finite; a program needn't handle non-finite values.
Results may differ from the reference program's by a relative error of at most 0.025.
Values may be sent and summed in bfloat16 or wider, within the bound.
No kernel may reach another device: no remote copies, remote signals or barrier semaphores. Data moves between devices by JAX's collectives and lax.ppermute only.
A program may use at most 320 MiB of HBM per device.

```python
import math
import jax
import jax.numpy as jnp
from jax import lax

D = 1536
HEADS = 24
HEAD_DIM = 64
FF = 6144
CTX_DIM = 768
CTX_LEN = 128
TFEAT = 256
CLIPS = 3
FRAMES_DEV = 256
ROW_LEN = 1024
ROWS = 8
CTXK = 384


def draw_clip_bounds(key, part):
    key = jax.random.fold_in(key, 11)
    first_key, second_key = jax.random.split(key)
    second_start = jax.random.randint(first_key, (ROWS, 1), 1, FRAMES_DEV)
    third_start = jax.random.randint(second_key, (ROWS, 1), ROW_LEN - FRAMES_DEV + 1, ROW_LEN)
    return jnp.concatenate([second_start, third_start], axis=1).astype(jnp.int32)


def set_ends(result, key, low, high):
    shape = result.shape
    place = [jax.random.randint(jax.random.fold_in(key, axis), (), 0, shape[axis]) for axis in range(len(shape))]
    result = result.at[tuple(place)].set(low)
    longest = shape.index(max(shape))
    place[longest] = (place[longest] + 1) % shape[longest]
    return result.at[tuple(place)].set(high)


def levels(rng, extent, shards, low, high):
    gain, own = 1.0, jax.random.fold_in(rng, 6)
    for position, shards_of in shards:
        steps = jnp.exp(jax.random.uniform(jax.random.fold_in(own, position), (shards_of,), jnp.float32, low / len(shards), high / len(shards)))
        gain = gain * jnp.repeat(steps, extent[position] // shards_of).reshape([-1 if axis == position else 1 for axis in range(len(extent))])
    return gain


def normal_values(own_key, extent, deviation, limit, cuts=(), held_as=jnp.bfloat16):
    gain = levels(own_key, extent, cuts, -0.22, 0.18) if cuts else 1.0
    drawn = jax.random.normal(own_key, extent, jnp.float32) * deviation * gain
    return jnp.minimum(jnp.maximum(drawn, -limit), limit).astype(held_as)


def setup_inputs(seed: int = 0) -> dict:
    seeds = jax.random.split(jax.random.key(seed), 17)
    latents = normal_values(seeds[0], (ROWS, ROW_LEN, D), 1.0, 6.0, ((0, 8), (1, 4)))
    context = normal_values(seeds[1], (ROWS, CTXK, CTX_DIM), 1.0, 6.0, ((0, 8),))
    clip_bounds = draw_clip_bounds(jax.random.fold_in(seeds[16], 71), 0)
    timesteps = set_ends(jax.random.randint(seeds[3], (ROWS, CLIPS), 0, 1000), jax.random.fold_in(seeds[3], 1), 0, 999).astype(jnp.int32)
    self_inward = normal_values(seeds[4], (D, 3 * D), (3 * D // 4) ** -0.5, 0.1875, ((0, 32),))
    self_outward = normal_values(seeds[5], (D, D), (max(D // 256, 2)) ** -0.5, 2.5, ((0, 32),))
    cross_query = normal_values(seeds[6], (D, D), D ** -0.5, 0.15625, ((0, 32),))
    cross_keyval = normal_values(seeds[7], (CTX_DIM, 2 * D), (3 * CTX_DIM // 4) ** -0.5, 0.25, ((0, 32),))
    cross_return = normal_values(seeds[8], (D, D), (D // 32) ** -0.5, 0.875, ((0, 32),))
    time_weight = normal_values(seeds[9], (TFEAT, D), (TFEAT // 16) ** -0.5, 1.5, ((0, 32),))
    expand_weight = normal_values(seeds[10], (D, 2 * FF), D ** -0.5, 0.15625, ((0, 32),))
    shrink_weight = normal_values(seeds[11], (FF, D), (FF // 4) ** -0.5, 0.15625, ((0, 32),))
    gain_attend = jnp.clip(1.0 + 0.15 * jax.random.normal(seeds[12], (D,), jnp.float32), 0.25, 1.75).astype(jnp.bfloat16)
    gain_cross = jnp.clip(1.0 + 0.15 * jax.random.normal(seeds[13], (D,), jnp.float32), 0.25, 1.75).astype(jnp.bfloat16)
    gain_feed = jnp.clip(1.0 + 0.15 * jax.random.normal(seeds[14], (D,), jnp.float32), 0.25, 1.75).astype(jnp.bfloat16)
    cotangent = normal_values(seeds[15], (ROWS, ROW_LEN, D), 1.0, 6.0, ((0, 8), (1, 4)))
    return dict(latents=latents, context=context, clip_bounds=clip_bounds, timesteps=timesteps, self_inward=self_inward, self_outward=self_outward, cross_query=cross_query, cross_keyval=cross_keyval, cross_return=cross_return, time_weight=time_weight, expand_weight=expand_weight, shrink_weight=shrink_weight, gain_attend=gain_attend, gain_cross=gain_cross, gain_feed=gain_feed, cotangent=cotangent)


EPSILON = 1e-05
SCORE_SCALE = 0.125
MASKED = -1e+30
PRECISE = lax.Precision.HIGHEST

@jax.custom_vjp
def low(v):
    return lax.optimization_barrier(v.astype(jnp.bfloat16)).astype(jnp.float32)

@jax.custom_vjp
def low_back(v):
    return v

def low_keep(v):
    return (low(v), None)

def low_pass(kept, grad):
    return (grad,)

def back_keep(v):
    return (v, None)

def back_low(kept, grad):
    return (low(grad),)
low.defvjp(low_keep, low_pass)
low_back.defvjp(back_keep, back_low)

def matmul_full(left, right):
    return jnp.dot(left, right, precision=PRECISE, preferred_element_type=jnp.float32)

def layer_norm(hidden, gain_vector):
    centre = lax.optimization_barrier(jnp.mean(hidden, axis=-1, keepdims=True))
    centred = hidden - centre
    spread = lax.optimization_barrier(jnp.mean(centred * centred, axis=-1, keepdims=True))
    return centred * lax.rsqrt(spread + EPSILON) * gain_vector

def rotate(head_values, cosine_table, sine_table):
    half_width = head_values.shape[-1] // 2
    first_half = head_values[..., :half_width]
    second_half = head_values[..., half_width:]
    return jnp.concatenate([first_half * cosine_table - second_half * sine_table, first_half * sine_table + second_half * cosine_table], axis=-1)

def rotary_tables(positions):
    half_width = HEAD_DIM // 2
    frequencies = jnp.exp(-math.log(10000.0) * jnp.arange(half_width, dtype=jnp.float32) / half_width)
    angles = positions[..., None] * frequencies
    return (jnp.cos(angles)[..., None, :], jnp.sin(angles)[..., None, :])

def time_features(step_values):
    half_width = TFEAT // 2
    frequencies = jnp.exp(-math.log(10000.0) * jnp.arange(half_width, dtype=jnp.float32) / half_width)
    angles = step_values.astype(jnp.float32)[..., None] * frequencies
    return jnp.concatenate([jnp.cos(angles), jnp.sin(angles)], axis=-1)

def attend(queries, keys_low, values_low, query_clip, key_clip):
    length = queries.shape[0]
    block_size = min(512, length)
    block_count = length // block_size

    def one_block(pieces):
        query_block, clip_block = pieces
        raw_scores = low_back(jnp.einsum('qhd,khd->hqk', query_block, keys_low, precision=PRECISE))
        allowed = (clip_block[:, None] == key_clip[None, :])[None]
        scores = jnp.where(allowed, raw_scores * SCORE_SCALE, MASKED)
        row_top = lax.optimization_barrier(jnp.max(scores, axis=-1, keepdims=True))
        weights = jnp.exp(scores - row_top)
        weights = weights / lax.optimization_barrier(jnp.sum(weights, axis=-1, keepdims=True))
        return low_back(jnp.einsum('hqk,khd->qhd', low(weights), values_low, precision=PRECISE))
    blocks = lax.map(jax.checkpoint(one_block), (queries.reshape(block_count, block_size, HEADS, HEAD_DIM), query_clip.reshape(block_count, block_size)))
    return blocks.reshape(length, HEADS * HEAD_DIM)

def block_forward(latent_row, params, context_row, clip_ids, positions, clip_feats):
    self_inward, self_outward, cross_query, cross_keyval, cross_return, time_weight, expand_weight, shrink_weight, gain_attend, gain_cross, gain_feed = params
    length = latent_row.shape[0]
    cosine_table, sine_table = rotary_tables(positions)
    clip_numbers = jnp.arange(CLIPS, dtype=jnp.int32)
    token = matmul_full(low(clip_feats), time_weight)
    token_normed = layer_norm(token, gain_attend)
    token_kv = matmul_full(low(token_normed), self_inward[:, D:]).reshape(CLIPS, 2, HEADS, HEAD_DIM)
    normed = layer_norm(latent_row, gain_attend)
    projected = low_back(matmul_full(low(normed), self_inward)).reshape(length, 3, HEADS, HEAD_DIM)
    queries = rotate(projected[:, 0], cosine_table, sine_table)
    keys_rot = rotate(projected[:, 1], cosine_table, sine_table)
    keys_all = jnp.concatenate([low(keys_rot), low(token_kv[:, 0])], axis=0)
    values_all = jnp.concatenate([low(projected[:, 2]), low(token_kv[:, 1])], axis=0)
    key_clips = jnp.concatenate([clip_ids, clip_numbers], axis=0)
    attended = attend(low(queries), keys_all, values_all, clip_ids, key_clips)
    after_self = latent_row + low_back(matmul_full(low(attended), self_outward))
    normed = layer_norm(after_self, gain_cross)
    cross_heads = low_back(matmul_full(low(normed), cross_query)).reshape(length, HEADS, HEAD_DIM)
    keyval = matmul_full(low(context_row), cross_keyval).reshape(context_row.shape[0], 2, HEADS, HEAD_DIM)
    text_clips = jnp.arange(context_row.shape[0], dtype=jnp.int32) // CTX_LEN
    crossed = attend(low(cross_heads), low(keyval[:, 0]), low(keyval[:, 1]), clip_ids, text_clips)
    after_cross = after_self + low_back(matmul_full(low(crossed), cross_return))
    normed = layer_norm(after_cross, gain_feed)
    gate_up = low_back(matmul_full(low(normed), expand_weight))
    hidden = jax.nn.silu(gate_up[:, :FF]) * gate_up[:, FF:]
    return after_cross + low_back(matmul_full(low(hidden), shrink_weight))

def reference(latents, context, clip_bounds, timesteps, self_inward, self_outward, cross_query, cross_keyval, cross_return, time_weight, expand_weight, shrink_weight, gain_attend, gain_cross, gain_feed, cotangent):
    params = tuple((matrix.astype(jnp.float32) for matrix in (self_inward, self_outward, cross_query, cross_keyval, cross_return, time_weight, expand_weight, shrink_weight, gain_attend, gain_cross, gain_feed)))
    length = latents.shape[1]
    frames = jnp.arange(length, dtype=jnp.int32)

    def one_row(running, row_data):
        latent_row, context_row, bounds, step_row, tangent_row = row_data
        clip_ids = (frames >= bounds[0]).astype(jnp.int32) + (frames >= bounds[1]).astype(jnp.int32)
        clip_starts = jnp.where(clip_ids == 0, 0, jnp.where(clip_ids == 1, bounds[0], bounds[1])).astype(jnp.int32)
        positions = (frames - clip_starts + 1).astype(jnp.float32)
        clip_feats = time_features(step_row)
        context_full = context_row.astype(jnp.float32)

        def forward(latent_in, weights_in):
            return block_forward(latent_in, weights_in, context_full, clip_ids, positions, clip_feats)
        output, pullback = jax.vjp(forward, latent_row.astype(jnp.float32), params)
        latent_grad, weight_grads = pullback(tangent_row.astype(jnp.float32))
        running = tuple((sofar + row_part for sofar, row_part in zip(running, weight_grads)))
        return (running, (output.astype(jnp.bfloat16), latent_grad))
    zeros = tuple((jnp.zeros_like(matrix) for matrix in params))
    totals, (outputs, latent_grads) = lax.scan(one_row, zeros, (latents, context, clip_bounds, timesteps, cotangent))
    return (outputs, latent_grads, totals[0], totals[1], totals[2], totals[3], totals[4], totals[5], totals[6], totals[7], totals[8], totals[9], totals[10])
```

```python
import math

import jax
import jax.numpy as jnp
from jax import lax
from jax.sharding import PartitionSpec as P

D = 1536
HEADS = 24
HEAD_DIM = 64
FF = 6144
CTX_LEN = 128
TFEAT = 256
CLIPS = 3


EPSILON = 1e-05
SCORE_SCALE = 0.125
MASKED = -1e30
PRECISE = lax.Precision.HIGHEST


def dense(activations, weight):
    return jnp.einsum("rfd,dn->rfn", activations, weight, preferred_element_type=jnp.float32)


def dense_back(gradients, weight):
    return jnp.einsum("rfn,dn->rfd", gradients, weight, preferred_element_type=jnp.float32)


def norm_forward(hidden):
    centre = jnp.mean(hidden, axis=-1, keepdims=True)
    centred = hidden - centre
    spread = jnp.mean(centred * centred, axis=-1, keepdims=True)
    scale_inv = lax.rsqrt(spread + EPSILON)
    return (centred * scale_inv, scale_inv)


def norm_backward(grad_norm, normalized, scale_inv, gain_vector):
    scaled = grad_norm * gain_vector
    gain_grad = jnp.sum(grad_norm * normalized, axis=(0, 1))
    inner = (
        scaled
        - jnp.mean(scaled, axis=-1, keepdims=True)
        - normalized * jnp.mean(scaled * normalized, axis=-1, keepdims=True)
    )
    return (scale_inv * inner, gain_grad)


def rotate(head_values, cosine_table, sine_table):
    half_width = head_values.shape[-1] // 2
    first_half = head_values[..., :half_width]
    second_half = head_values[..., half_width:]
    return jnp.concatenate(
        [
            first_half * cosine_table - second_half * sine_table,
            first_half * sine_table + second_half * cosine_table,
        ],
        axis=-1,
    )


def rotary_tables(positions):
    half_width = HEAD_DIM // 2
    frequencies = jnp.exp(
        -math.log(10000.0) * jnp.arange(half_width, dtype=jnp.float32) / half_width
    )
    angles = positions[..., None] * frequencies
    return (jnp.cos(angles)[..., None, :], jnp.sin(angles)[..., None, :])


def time_features(step_values):
    half_width = TFEAT // 2
    frequencies = jnp.exp(
        -math.log(10000.0) * jnp.arange(half_width, dtype=jnp.float32) / half_width
    )
    angles = step_values.astype(jnp.float32)[..., None] * frequencies
    return jnp.concatenate([jnp.cos(angles), jnp.sin(angles)], axis=-1)


def score_block(query_low, key_block, query_clip, key_clip):
    raw_scores = jnp.einsum(
        "rqhd,rkhd->rhqk", query_low, key_block, preferred_element_type=jnp.float32
    )
    allowed = (query_clip[:, :, None] == key_clip[:, None, :])[:, None]
    return (jnp.where(allowed, raw_scores * SCORE_SCALE, MASKED), allowed)


def attend_forward(query_low, keys_low, values_low, query_clip, key_clip):
    key_count = keys_low.shape[1]
    key_width = min(512, key_count)
    stat_shape = (query_low.shape[0], query_low.shape[2], query_low.shape[1], 1)
    row_top = jnp.full(stat_shape, MASKED, jnp.float32)
    norm_sum = jnp.zeros(stat_shape, jnp.float32)
    for offset in range(0, key_count, key_width):
        scores, allowed = score_block(
            query_low,
            keys_low[:, offset : offset + key_width],
            query_clip,
            key_clip[:, offset : offset + key_width],
        )
        next_top = jnp.maximum(row_top, jnp.max(scores, axis=-1, keepdims=True))
        norm_sum = norm_sum * jnp.exp(row_top - next_top) + jnp.sum(
            jnp.where(allowed, jnp.exp(scores - next_top), 0.0), axis=-1, keepdims=True
        )
        row_top = next_top
    mixture = jnp.zeros(query_low.shape, jnp.float32)
    for offset in range(0, key_count, key_width):
        scores, allowed = score_block(
            query_low,
            keys_low[:, offset : offset + key_width],
            query_clip,
            key_clip[:, offset : offset + key_width],
        )
        weights = jnp.where(allowed, jnp.exp(scores - row_top) / norm_sum, 0.0)
        mixture = mixture + jnp.einsum(
            "rhqk,rkhd->rqhd",
            weights.astype(jnp.bfloat16),
            values_low[:, offset : offset + key_width],
            preferred_element_type=jnp.float32,
        )
    return (mixture, row_top, norm_sum)


def attend_backward(
    query_low, keys_low, values_low, query_clip, key_clip, row_top, norm_sum, grad_low
):
    key_count = keys_low.shape[1]
    key_width = min(512, key_count)
    diagonal = jnp.zeros_like(row_top)
    for offset in range(0, key_count, key_width):
        scores, allowed = score_block(
            query_low,
            keys_low[:, offset : offset + key_width],
            query_clip,
            key_clip[:, offset : offset + key_width],
        )
        weights = jnp.where(allowed, jnp.exp(scores - row_top) / norm_sum, 0.0)
        grad_weights = jnp.einsum(
            "rqhd,rkhd->rhqk",
            grad_low,
            values_low[:, offset : offset + key_width],
            preferred_element_type=jnp.float32,
        )
        diagonal = diagonal + jnp.sum(weights * grad_weights, axis=-1, keepdims=True)
    query_grad = jnp.zeros(query_low.shape, jnp.float32)
    key_parts = []
    value_parts = []
    for offset in range(0, key_count, key_width):
        key_block = keys_low[:, offset : offset + key_width]
        scores, allowed = score_block(
            query_low, key_block, query_clip, key_clip[:, offset : offset + key_width]
        )
        weights = jnp.where(allowed, jnp.exp(scores - row_top) / norm_sum, 0.0)
        grad_weights = jnp.einsum(
            "rqhd,rkhd->rhqk",
            grad_low,
            values_low[:, offset : offset + key_width],
            preferred_element_type=jnp.float32,
        )
        score_grad = (weights * (grad_weights - diagonal) * SCORE_SCALE).astype(jnp.bfloat16)
        query_grad = query_grad + jnp.einsum(
            "rhqk,rkhd->rqhd", score_grad, key_block, preferred_element_type=jnp.float32
        )
        key_parts.append(
            jnp.einsum("rhqk,rqhd->rkhd", score_grad, query_low, preferred_element_type=jnp.float32)
        )
        value_parts.append(
            jnp.einsum(
                "rhqk,rqhd->rkhd",
                weights.astype(jnp.bfloat16),
                grad_low,
                preferred_element_type=jnp.float32,
            )
        )
    return (query_grad, jnp.concatenate(key_parts, axis=1), jnp.concatenate(value_parts, axis=1))


def gated_back(hidden_grad, gate_part, upward):
    gate_sigmoid = jax.nn.sigmoid(gate_part)
    gate_grad = hidden_grad * upward * gate_sigmoid * (1.0 + gate_part * (1.0 - gate_sigmoid))
    upward_grad = hidden_grad * gate_part * gate_sigmoid
    return jnp.concatenate([gate_grad, upward_grad], axis=-1).astype(jnp.bfloat16)


def xor_pairs(count, bit):
    return [(k, k ^ bit) for k in range(count)]


def chip_gather(values, axis):
    count = lax.axis_size(axis)
    bits = [1 << b for b in range(1, count.bit_length() - 1)]
    if len(bits) == 2 and values.shape[0] % 32 == 0:
        first, second = bits
        half = values.shape[0] // 2
        by_first = lax.ppermute(values, axis, xor_pairs(count, first))
        by_second = lax.ppermute(values, axis, xor_pairs(count, second))
        far_one = lax.ppermute(by_first[:half], axis, xor_pairs(count, second))
        far_two = lax.ppermute(by_second[half:], axis, xor_pairs(count, first))
        far = jnp.concatenate([far_one, far_two], axis=0)
        same = jnp.stack([values, by_first, by_second, far], axis=0)
    else:
        same = values[None]
        for bit in bits:
            same = jnp.concatenate([same, lax.ppermute(same, axis, xor_pairs(count, bit))], axis=0)
    if count == 1:
        return same
    other = lax.ppermute(same, axis, xor_pairs(count, 1))
    return jnp.stack([same, other], axis=1).reshape((count,) + values.shape)


def chip_scatter(parts, axis):
    count = lax.axis_size(axis)
    if count == 1:
        return parts[0].astype(jnp.float32)
    low = jnp.bfloat16
    pairs = parts.reshape((count // 2, 2) + parts.shape[1:])
    got = lax.ppermute(pairs[:, 1].astype(low), axis, xor_pairs(count, 1))
    total = pairs[:, 0].astype(jnp.float32) + got.astype(jnp.float32)
    bits = [1 << b for b in range(1, count.bit_length() - 1)]
    if len(bits) == 2 and parts.shape[1] % 32 == 0:
        first, second = bits
        half = parts.shape[1] // 2
        far_one = lax.ppermute(total[3, :half].astype(low), axis, xor_pairs(count, first))
        far_two = lax.ppermute(total[3, half:].astype(low), axis, xor_pairs(count, second))
        to_second = jnp.concatenate(
            [total[2, :half] + far_one.astype(jnp.float32), total[2, half:]], axis=0
        )
        to_first = jnp.concatenate(
            [total[1, :half], total[1, half:] + far_two.astype(jnp.float32)], axis=0
        )
        by_first = lax.ppermute(to_first.astype(low), axis, xor_pairs(count, first))
        by_second = lax.ppermute(to_second.astype(low), axis, xor_pairs(count, second))
        return total[0] + by_first.astype(jnp.float32) + by_second.astype(jnp.float32)
    for bit in reversed(bits):
        middle = total.shape[0] // 2
        got = lax.ppermute(total[middle:].astype(low), axis, xor_pairs(count, bit))
        total = total[:middle] + got.astype(jnp.float32)
    return total[0]


def place(buffer, block, dim, index):
    starts = [0] * buffer.ndim
    starts[dim] = index
    return lax.dynamic_update_slice(buffer, block, tuple(starts))


def by_order(relative, me):
    ordered = jnp.zeros(relative.shape, relative.dtype)
    for r in range(relative.shape[0]):
        ordered = place(ordered, relative[r : r + 1], 0, me ^ r)
    return ordered


def by_partner(ordered, me):
    return jnp.concatenate(
        [
            lax.dynamic_slice_in_dim(ordered, me ^ r, 1, axis=0)
            for r in range(ordered.shape[0])
        ],
        axis=0,
    )


def chip_exchange(blocks, axis, me):
    count = lax.axis_size(axis)
    result = blocks
    for r in range(1, count):
        sent = lax.dynamic_slice_in_dim(blocks, me ^ r, 1, axis=0)
        result = place(result, lax.ppermute(sent, axis, xor_pairs(count, r)), 0, me ^ r)
    return result


def line_gather(values, axis, me, dim=0):
    count = lax.axis_size(axis)
    values = jnp.expand_dims(values, dim)
    shape = list(values.shape)
    shape[dim] = count
    rightward, leftward = [values], [values]
    for step in range(1, count):
        rightward.append(
            lax.ppermute(rightward[-1], axis, [(k, k + 1) for k in range(step - 1, count - 1)])
        )
        leftward.append(
            lax.ppermute(leftward[-1], axis, [(k + 1, k) for k in range(0, count - step)])
        )
    result = place(jnp.zeros(shape, values.dtype), values, dim, me)
    for step in range(1, count):
        block = jnp.where(me >= step, rightward[step], leftward[count - step])
        result = place(result, block, dim, lax.rem(me - step + count, count))
    return result


def line_scatter(parts, axis, me, dim=0):
    count = lax.axis_size(axis)

    def part(index):
        picked = lax.dynamic_slice_in_dim(parts, index, 1, axis=dim)
        return jnp.squeeze(picked, dim).astype(jnp.float32)

    total = part(me)
    from_left = from_right = None
    for step in range(1, count):
        to_right = part(jnp.minimum(me + count - step, count - 1))
        to_left = part(jnp.maximum(me - count + step, 0))
        if step > 1:
            to_right = to_right + from_left.astype(jnp.float32)
            to_left = to_left + from_right.astype(jnp.float32)
        from_left = lax.ppermute(
            to_right.astype(jnp.bfloat16), axis, [(k, k + 1) for k in range(0, step)]
        )
        from_right = lax.ppermute(
            to_left.astype(jnp.bfloat16),
            axis,
            [(k + 1, k) for k in range(count - 1 - step, count - 1)],
        )
    if count > 1:
        total = total + from_left.astype(jnp.float32) + from_right.astype(jnp.float32)
    return total


def line_exchange(blocks, axis, me):
    count = lax.axis_size(axis)
    result = blocks
    for step in range(1, count):
        sent = lax.dynamic_slice_in_dim(blocks, lax.rem(me + step, count), 1, axis=0)
        got = lax.ppermute(sent, axis, [(k, (k + step) % count) for k in range(count)])
        result = place(result, got, 0, lax.rem(me - step + count, count))
    return result


def whole_weight(rows, dp_place, seq_place):
    column = line_gather(rows, "seq", seq_place)
    full = by_order(chip_gather(column, "dp"), dp_place)
    return full.reshape((-1,) + rows.shape[1:])


def own_rows_sum(partial, dp_place, seq_place):
    dp_count, seq_count = lax.axis_size("dp"), lax.axis_size("seq")
    rows, width = partial.shape
    shaped = partial.astype(jnp.bfloat16).reshape(dp_count, rows // dp_count, width)
    column = chip_scatter(by_partner(shaped, dp_place), "dp")
    return line_scatter(column.reshape(seq_count, -1, width), "seq", seq_place)


def on_device(
    latents,
    context,
    clip_bounds,
    timesteps,
    self_inward,
    self_outward,
    cross_query,
    cross_keyval,
    cross_return,
    time_weight,
    expand_weight,
    shrink_weight,
    gain_attend,
    gain_cross,
    gain_feed,
    cotangent,
):
    f32, bf16 = jnp.float32, jnp.bfloat16
    frame_count = latents.shape[1]
    dp_count = lax.axis_size("dp")
    seq_count = lax.axis_size("seq")
    dp_place = lax.axis_index("dp")
    seq_place = lax.axis_index("seq")
    row_length = frame_count * seq_count
    text_count = context.shape[1]
    own_heads = HEADS // seq_count
    own_width = own_heads * HEAD_DIM
    hidden_width = FF // dp_count
    place_all = dp_place * seq_count + seq_place

    all_frames = jnp.arange(row_length, dtype=jnp.int32)[None, :]
    second_start = clip_bounds[:, 0:1]
    third_start = clip_bounds[:, 1:2]
    frame_clips = (all_frames >= second_start).astype(jnp.int32) + (
        all_frames >= third_start
    ).astype(jnp.int32)
    clip_ids = lax.dynamic_slice_in_dim(frame_clips, seq_place * frame_count, frame_count, axis=1)
    token_clips = jnp.arange(CLIPS, dtype=jnp.int32)[None, :]
    key_clips = jnp.concatenate([frame_clips, token_clips], axis=1)
    clip_starts = jnp.where(
        frame_clips == 0, 0, jnp.where(frame_clips == 1, second_start, third_start)
    )
    positions = (all_frames - clip_starts + 1).astype(f32)
    cosine_table, sine_table = rotary_tables(positions)
    text_clips = (jnp.arange(text_count, dtype=jnp.int32) // CTX_LEN)[None, :]

    gains_all = lax.all_gather(
        jnp.stack([gain_attend, gain_cross, gain_feed], axis=0), ("dp", "seq"), axis=1, tiled=True
    ).astype(f32)
    time_full = lax.all_gather(time_weight, ("dp", "seq"), axis=0, tiled=True)
    steps_all = lax.all_gather(timesteps, "dp", axis=0, tiled=True)
    attend_gain, cross_gain, feed_gain = gains_all[0], gains_all[1], gains_all[2]

    inward_blocks = (
        self_inward.reshape(-1, 3, seq_count, own_width)
        .transpose(2, 0, 1, 3)
        .reshape(seq_count, -1, 3 * own_width)
    )
    row_latents = line_gather(latents[0], "seq", seq_place).reshape(row_length, D)
    inward_columns = line_exchange(inward_blocks, "seq", seq_place)
    inward_own = by_order(chip_gather(inward_columns, "dp"), dp_place).reshape(D, 3 * own_width)
    cotangent_all = chip_gather(cotangent[0], "dp").reshape(dp_count * frame_count, D)

    outward_full = whole_weight(self_outward, dp_place, seq_place)
    query_full = whole_weight(cross_query, dp_place, seq_place)
    keyval_full = whole_weight(cross_keyval, dp_place, seq_place)
    return_full = whole_weight(cross_return, dp_place, seq_place)

    expand_blocks = (
        expand_weight.reshape(-1, 2, dp_count, hidden_width)
        .transpose(2, 0, 1, 3)
        .reshape(dp_count, -1, 2 * hidden_width)
    )
    expand_part = chip_exchange(expand_blocks, "dp", dp_place)
    expand_own = line_gather(expand_part, "seq", seq_place, dim=1).reshape(D, 2 * hidden_width)
    shrink_own = line_gather(shrink_weight, "seq", seq_place).reshape(hidden_width, D)

    feats_low = time_features(timesteps[0]).astype(bf16)
    token = jnp.dot(feats_low, time_full, preferred_element_type=f32)
    token_norm, token_inverse = norm_forward(token)
    token_low = (token_norm * attend_gain).astype(bf16)
    token_kv = jnp.dot(
        token_low, inward_own[:, own_width:], preferred_element_type=f32
    ).astype(bf16)

    row_float = row_latents.astype(f32)
    row_norm, row_inverse = norm_forward(row_float)
    row_low = (row_norm * attend_gain).astype(bf16)
    projected = jnp.dot(row_low, inward_own, preferred_element_type=f32).reshape(
        1, row_length, 3, own_heads, HEAD_DIM
    )
    queries_low = rotate(projected[:, :, 0], cosine_table, sine_table).astype(bf16)
    keys_low = rotate(projected[:, :, 1], cosine_table, sine_table).astype(bf16)
    values_low = projected[:, :, 2].astype(bf16)
    token_heads = token_kv.reshape(1, CLIPS, 2, own_heads, HEAD_DIM)
    keys_heads = jnp.concatenate([keys_low, token_heads[:, :, 0]], axis=1)
    values_heads = jnp.concatenate([values_low, token_heads[:, :, 1]], axis=1)
    attended, self_top, self_sum = attend_forward(
        queries_low, keys_heads, values_heads, frame_clips, key_clips
    )
    attended_blocks = attended.astype(bf16).reshape(seq_count, frame_count, own_width)
    attended_low = (
        line_exchange(attended_blocks, "seq", seq_place)
        .transpose(1, 0, 2)
        .reshape(frame_count, D)
    )
    conditioned = latents[0].astype(f32)
    after_self = conditioned + jnp.dot(attended_low, outward_full, preferred_element_type=f32)

    norm_two, inverse_two = norm_forward(after_self)
    normed_two = (norm_two * cross_gain).astype(bf16)
    cross_heads = (
        jnp.dot(normed_two, query_full, preferred_element_type=f32)
        .astype(bf16)
        .reshape(1, frame_count, HEADS, HEAD_DIM)
    )
    keyval = (
        jnp.dot(context[0], keyval_full, preferred_element_type=f32)
        .astype(bf16)
        .reshape(1, text_count, 2, HEADS, HEAD_DIM)
    )
    cross_keys = keyval[:, :, 0]
    cross_values = keyval[:, :, 1]
    crossed, cross_top, cross_sum = attend_forward(
        cross_heads, cross_keys, cross_values, clip_ids, text_clips
    )
    crossed_low = crossed.reshape(frame_count, D).astype(bf16)
    after_cross = after_self + jnp.dot(crossed_low, return_full, preferred_element_type=f32)

    norm_three, inverse_three = norm_forward(after_cross)
    normed_three = (norm_three * feed_gain).astype(bf16)
    frames_all = chip_gather(normed_three, "dp").reshape(dp_count * frame_count, D)
    gate_up = jnp.dot(frames_all, expand_own, preferred_element_type=f32)
    gate_part = gate_up[:, :hidden_width]
    upward = gate_up[:, hidden_width:]
    hidden_low = (jax.nn.silu(gate_part) * upward).astype(bf16)
    hidden_grad = jnp.dot(cotangent_all, shrink_own.T, preferred_element_type=f32)
    expand_low = gated_back(hidden_grad, gate_part, upward)
    feed_parts = jnp.dot(expand_low, expand_own.T, preferred_element_type=f32).astype(bf16)
    feed_norm_grad = chip_scatter(feed_parts.reshape(dp_count, frame_count, D), "dp")
    out_parts = jnp.dot(hidden_low, shrink_own, preferred_element_type=f32).astype(bf16)
    fed = chip_scatter(out_parts.reshape(dp_count, frame_count, D), "dp")
    block_output = (after_cross + fed).astype(bf16)

    shrink_part = jnp.dot(hidden_low.T, cotangent_all, preferred_element_type=f32).astype(bf16)
    grad_shrink = line_scatter(
        shrink_part.reshape(seq_count, hidden_width // seq_count, D), "seq", seq_place
    )
    expand_grad = jnp.dot(frames_all.T, expand_low, preferred_element_type=f32).astype(bf16)
    expand_sum = line_scatter(
        expand_grad.reshape(dp_count, seq_count, -1, 2 * hidden_width), "seq", seq_place, dim=1
    ).astype(bf16)
    grad_expand = (
        chip_exchange(expand_sum, "dp", dp_place)
        .reshape(dp_count, -1, 2, hidden_width)
        .transpose(1, 2, 0, 3)
        .reshape(-1, 2 * FF)
        .astype(f32)
    )

    feed_term, feed_gain_part = norm_backward(
        feed_norm_grad[None], norm_three[None], inverse_three[None], feed_gain
    )
    after_cross_grad = cotangent[0].astype(f32) + feed_term[0]
    return_low = after_cross_grad.astype(bf16)
    grad_return = own_rows_sum(
        jnp.dot(crossed_low.T, return_low, preferred_element_type=f32), dp_place, seq_place
    )
    crossed_grad = (
        jnp.dot(return_low, return_full.T, preferred_element_type=f32)
        .astype(bf16)
        .reshape(1, frame_count, HEADS, HEAD_DIM)
    )
    cross_query_grad, cross_key_grad, cross_value_grad = attend_backward(
        cross_heads,
        cross_keys,
        cross_values,
        clip_ids,
        text_clips,
        cross_top,
        cross_sum,
        crossed_grad,
    )
    cross_query_low = cross_query_grad.reshape(frame_count, D).astype(bf16)
    keyval_low = (
        jnp.stack([cross_key_grad, cross_value_grad], axis=2)
        .reshape(text_count, 2 * D)
        .astype(bf16)
    )
    grad_keyval = own_rows_sum(
        jnp.dot(context[0].T, keyval_low, preferred_element_type=f32), dp_place, seq_place
    )
    grad_query = own_rows_sum(
        jnp.dot(normed_two.T, cross_query_low, preferred_element_type=f32), dp_place, seq_place
    )
    cross_norm_grad = jnp.dot(cross_query_low, query_full.T, preferred_element_type=f32)
    cross_term, cross_gain_part = norm_backward(
        cross_norm_grad[None], norm_two[None], inverse_two[None], cross_gain
    )
    after_self_grad = after_cross_grad + cross_term[0]
    outward_low = after_self_grad.astype(bf16)
    grad_outward = own_rows_sum(
        jnp.dot(attended_low.T, outward_low, preferred_element_type=f32), dp_place, seq_place
    )
    attended_grad = jnp.dot(outward_low, outward_full.T, preferred_element_type=f32).astype(bf16)
    attended_grad_own = line_exchange(
        attended_grad.reshape(frame_count, seq_count, own_width).transpose(1, 0, 2),
        "seq",
        seq_place,
    ).reshape(1, row_length, own_heads, HEAD_DIM)
    self_query_grad, self_key_grad, self_value_grad = attend_backward(
        queries_low,
        keys_heads,
        values_heads,
        frame_clips,
        key_clips,
        self_top,
        self_sum,
        attended_grad_own,
    )
    query_turned = rotate(self_query_grad, cosine_table, -sine_table)
    key_turned = rotate(self_key_grad[:, :row_length], cosine_table, -sine_table)
    inward_low = (
        jnp.stack([query_turned, key_turned, self_value_grad[:, :row_length]], axis=2)
        .reshape(row_length, 3 * own_width)
        .astype(bf16)
    )
    token_grad = jnp.stack(
        [self_key_grad[:, row_length:], self_value_grad[:, row_length:]], axis=2
    ).reshape(CLIPS, 2 * own_width)
    token_grad_low = token_grad.astype(bf16)
    attend_parts = jnp.dot(inward_low, inward_own.T, preferred_element_type=f32)
    attend_norm_grad = line_scatter(
        attend_parts.astype(bf16).reshape(seq_count, frame_count, D), "seq", seq_place
    )
    own_norm = lax.dynamic_slice_in_dim(row_norm, seq_place * frame_count, frame_count, axis=0)
    own_inverse = lax.dynamic_slice_in_dim(
        row_inverse, seq_place * frame_count, frame_count, axis=0
    )
    attend_term, _ = norm_backward(
        attend_norm_grad[None], own_norm[None], own_inverse[None], attend_gain
    )
    latents_grad = (after_self_grad + attend_term[0])[None]

    token_norm_grad = jnp.dot(
        token_grad_low, inward_own[:, own_width:].T, preferred_element_type=f32
    )
    token_term, token_gain_part = norm_backward(
        token_norm_grad[None], token_norm[None], token_inverse[None], attend_gain
    )
    attend_gain_part = jnp.sum(attend_parts * row_norm, axis=0) + token_gain_part
    small = jnp.concatenate(
        [
            token_term[0],
            attend_gain_part[None],
            cross_gain_part[None],
            feed_gain_part[None],
        ],
        axis=0,
    )
    small_all = lax.all_gather(small, ("dp", "seq"), axis=0, tiled=False)
    small_sum = jnp.sum(small_all.reshape(dp_count, seq_count, CLIPS + 3, D), axis=1)
    feats_all = time_features(steps_all).astype(bf16).astype(f32)
    time_rows = TFEAT // (dp_count * seq_count)
    feats_own = lax.dynamic_slice_in_dim(feats_all, place_all * time_rows, time_rows, axis=2)
    grad_time = jnp.einsum(
        "rct,rcn->tn",
        feats_own,
        small_sum[:, :CLIPS],
        precision=PRECISE,
        preferred_element_type=f32,
    )
    gain_width = D // (dp_count * seq_count)
    gain_sums = lax.dynamic_slice_in_dim(
        jnp.sum(small_sum[:, CLIPS:], axis=0), place_all * gain_width, gain_width, axis=1
    )

    inward_full_low = jnp.concatenate(
        [row_low, jnp.pad(token_low, ((0, 16 - CLIPS), (0, 0)))], axis=0
    )
    inward_full_grad = jnp.concatenate(
        [inward_low, jnp.pad(token_grad_low, ((0, 16 - CLIPS), (own_width, 0)))], axis=0
    )
    inward_grad = jnp.dot(inward_full_low.T, inward_full_grad, preferred_element_type=f32)
    inward_sum = chip_scatter(
        by_partner(
            inward_grad.astype(bf16).reshape(dp_count, D // dp_count, 3 * own_width), dp_place
        ),
        "dp",
    )
    grad_inward = (
        line_exchange(
            inward_sum.astype(bf16).reshape(seq_count, -1, 3 * own_width), "seq", seq_place
        )
        .reshape(seq_count, -1, 3, own_width)
        .transpose(1, 2, 0, 3)
        .reshape(-1, 3 * D)
        .astype(f32)
    )
    return (
        block_output[None],
        latents_grad,
        grad_inward,
        grad_outward,
        grad_query,
        grad_keyval,
        grad_return,
        grad_time,
        grad_expand,
        grad_shrink,
        gain_sums[0],
        gain_sums[1],
        gain_sums[2],
    )


def solution(mesh):
    return jax.shard_map(
        on_device,
        mesh=mesh,
        in_specs=(
            P("dp", "seq", None),
            P("dp", None, None),
            P("dp", None),
            P("dp", None),
            P(("dp", "seq"), None),
            P(("dp", "seq"), None),
            P(("dp", "seq"), None),
            P(("dp", "seq"), None),
            P(("dp", "seq"), None),
            P(("dp", "seq"), None),
            P(("dp", "seq"), None),
            P(("dp", "seq"), None),
            P(("dp", "seq")),
            P(("dp", "seq")),
            P(("dp", "seq")),
            P("dp", "seq", None),
        ),
        out_specs=(
            P("dp", "seq", None),
            P("dp", "seq", None),
            P(("dp", "seq"), None),
            P(("dp", "seq"), None),
            P(("dp", "seq"), None),
            P(("dp", "seq"), None),
            P(("dp", "seq"), None),
            P(("dp", "seq"), None),
            P(("dp", "seq"), None),
            P(("dp", "seq"), None),
            P(("dp", "seq")),
            P(("dp", "seq")),
            P(("dp", "seq")),
        ),
        check_vma=False,
    )
```

```python
import math

import jax
import jax.numpy as jnp
from jax import lax
from jax.experimental import pallas as pl
from jax.experimental.pallas import tpu as pltpu
from jax.sharding import PartitionSpec as P

D = 1536
HEADS = 24
HEAD_DIM = 64
FF = 6144
CTX_LEN = 128
TFEAT = 256
CLIPS = 3
TOKEN_ROWS = 128


EPSILON = 1e-05
SCORE_SCALE = 0.125
MASKED = -1e30
PRECISE = lax.Precision.HIGHEST


def contract_last(left, right):
    return lax.dot_general(left, right, (((1,), (1,)), ((), ())), preferred_element_type=jnp.float32)


def contract(left, right):
    return lax.dot_general(left, right, (((1,), (0,)), ((), ())), preferred_element_type=jnp.float32)


def lane_of(width=2 * HEAD_DIM):
    return lax.broadcasted_iota(jnp.int32, (1, width), 1)


def attend_rows(query, keys, value_pair, query_clip, key_clip):
    first = lane_of() < HEAD_DIM
    allowed = query_clip == key_clip
    zero = jnp.zeros((), query.dtype)
    outs, tops = [], []
    for head in range(2):
        mine = first if head == 0 else jnp.logical_not(first)
        scores = contract_last(jnp.where(mine, query, zero), keys)
        scores = jnp.where(allowed, scores, MASKED)
        top = jnp.max(scores, axis=1, keepdims=True)
        weights = jnp.exp(scores - top).astype(jnp.bfloat16)
        mixed = contract(weights, value_pair[head])
        place_sum = HEAD_DIM if head == 0 else 0
        total = mixed[:, place_sum : place_sum + 1]
        outs.append(mixed / total)
        tops.append(top + jnp.log(total))
    mixture = jnp.where(first, outs[0], outs[1])
    return mixture, jnp.where(first, tops[0], tops[1])


def value_with_ones(values):
    first = lane_of() < HEAD_DIM
    one = jnp.ones((), values.dtype)
    return jnp.where(first, values, one), jnp.where(first, one, values)


def attend_rows_back(query, keys, keys_turned, values, grads, mixture, level, query_clip, key_clip):
    first = lane_of() < HEAD_DIM
    allowed = key_clip == query_clip
    zero = jnp.zeros((), query.dtype)
    product = jnp.transpose(grads.astype(jnp.float32) * mixture)
    level_turned = jnp.transpose(level)
    head_rows = lax.broadcasted_iota(jnp.int32, (2 * HEAD_DIM, 1), 0) < HEAD_DIM
    parts = []
    for head in range(2):
        mine = first if head == 0 else jnp.logical_not(first)
        low, high = head * HEAD_DIM, (head + 1) * HEAD_DIM
        query_own = jnp.where(mine, query, zero)
        grads_own = jnp.where(mine, grads, zero)
        scores = contract_last(keys, query_own)
        scores = jnp.where(allowed, scores, MASKED)
        weights = jnp.exp(scores - level_turned[low : low + 1])
        grad_weights = contract_last(values, grads_own)
        diagonal = jnp.sum(product[low:high], axis=0, keepdims=True)
        grad_scores = (weights * (grad_weights - diagonal)).astype(jnp.bfloat16)
        key_grad = contract(grad_scores, query_own)
        value_grad = contract(weights.astype(jnp.bfloat16), grads_own)
        parts.append((contract(keys_turned, grad_scores), key_grad, value_grad))
    query_turned = jnp.where(head_rows, parts[0][0], parts[1][0])
    return query_turned, parts[0][1] + parts[1][1], parts[0][2] + parts[1][2]


def swap_halves(values):
    quarter = HEAD_DIM // 2
    down = pltpu.roll(values, 2 * HEAD_DIM - quarter, 1)
    up = pltpu.roll(values, quarter, 1)
    return jnp.where(lane_of() % HEAD_DIM < quarter, down, up)


def self_forward_kernel(
    projected, cosine, sine, clip_column, clip_row, mixed, mixed_wide, level, low, value_pair
):
    rows = mixed.shape[0]
    pair = 2 * HEAD_DIM
    block = min(256, rows)
    for part, scale in ((0, SCORE_SCALE), (1, 1.0)):
        values = projected[:, part * pair : (part + 1) * pair]
        turned = values * cosine[...] + swap_halves(values) * sine[...]
        low[:, part * pair : (part + 1) * pair] = turned.astype(jnp.bfloat16) * jnp.bfloat16(scale)
    values = projected[:, 2 * pair : 3 * pair].astype(jnp.bfloat16)
    low[:, 2 * pair : 3 * pair] = values
    value_pair[0], value_pair[1] = value_with_ones(values)

    def step(index, carry):
        place = pl.ds(pl.multiple_of(index * block, block), block)
        mixture, tops = attend_rows(
            low[place, 0:pair],
            low[:, pair : 2 * pair],
            (value_pair[0], value_pair[1]),
            clip_column[place, :],
            clip_row[...],
        )
        mixed[place, :] = mixture.astype(jnp.bfloat16)
        mixed_wide[place, :] = mixture
        level[place, :] = tops
        return carry

    lax.fori_loop(0, rows // block, step, 0)


def self_backward_kernel(
    low, grads, mixed_wide, level, cosine, sine, clip_column, clip_row, out, keys_turned, totals
):
    rows = grads.shape[0]
    pair = 2 * HEAD_DIM
    block = min(256, rows)
    keys_turned[...] = jnp.transpose(low[:, pair : 2 * pair])
    totals[...] = jnp.zeros_like(totals)
    out[rows:, 0:pair] = jnp.zeros((out.shape[0] - rows, pair), jnp.bfloat16)

    def step(index, carry):
        start = pl.multiple_of(index * block, block)
        place = pl.ds(start, block)
        query_turned, key_grad, value_grad = attend_rows_back(
            low[place, 0:pair],
            low[:, pair : 2 * pair],
            keys_turned[...],
            low[:, 2 * pair : 3 * pair],
            grads[place, :],
            mixed_wide[place, :],
            level[place, :],
            clip_row[:, place],
            clip_column[...],
        )
        query_grad = jnp.transpose(query_turned) * SCORE_SCALE
        back = query_grad * cosine[place, :] - swap_halves(query_grad) * sine[place, :]
        out[place, 0:pair] = back.astype(jnp.bfloat16)
        totals[0] += key_grad
        totals[1] += value_grad
        return carry

    lax.fori_loop(0, rows // block, step, 0)
    key_grad = totals[0]
    back = key_grad * cosine[...] - swap_halves(key_grad) * sine[...]
    out[:, pair : 2 * pair] = back.astype(jnp.bfloat16)
    out[:, 2 * pair : 3 * pair] = totals[1].astype(jnp.bfloat16)


def cross_forward_kernel(query, keys, values, clip_column, clip_row, mixed, mixed_wide, level):
    mixture, tops = attend_rows(
        query[...] * jnp.bfloat16(SCORE_SCALE),
        keys[...],
        value_with_ones(values[...]),
        clip_column[...],
        clip_row[...],
    )
    mixed[...] = mixture.astype(jnp.bfloat16)
    mixed_wide[...] = mixture
    level[...] = tops


def cross_backward_kernel(
    query, keys, values, grads, mixed_wide, level, clip_column, clip_row, query_out, key_out, value_out
):
    query_turned, key_grad, value_grad = attend_rows_back(
        query[...] * jnp.bfloat16(SCORE_SCALE),
        keys[...],
        jnp.transpose(keys[...]),
        values[...],
        grads[...],
        mixed_wide[...],
        level[...],
        clip_row[...],
        clip_column[...],
    )
    query_out[...] = (jnp.transpose(query_turned) * SCORE_SCALE).astype(jnp.bfloat16)
    key_out[...] = key_grad.astype(jnp.bfloat16)
    value_out[...] = value_grad.astype(jnp.bfloat16)


def whole(array):
    return pl.BlockSpec(array.shape, lambda p: (0,) * array.ndim)


def lanes(rows, width=2 * HEAD_DIM, offset=0):
    return pl.BlockSpec((rows, width), lambda p: (0, p + offset))


KERNEL_PARAMS = pltpu.CompilerParams(
    dimension_semantics=("arbitrary",), vmem_limit_bytes=48 * 1024 * 1024
)


def cost(heads, queries, keys, dots):
    return pl.CostEstimate(
        flops=2 * dots * heads * queries * keys * 2 * HEAD_DIM,
        bytes_accessed=heads * HEAD_DIM * (queries + keys) * 16,
        transcendentals=heads * queries * keys,
    )


def self_forward(projected, cosine, sine, clip_column, clip_row, rows):
    total, width = projected.shape
    pair = 2 * HEAD_DIM
    pairs = width // (3 * pair)
    return pl.pallas_call(
        self_forward_kernel,
        grid=(pairs,),
        in_specs=[
            lanes(total, 3 * pair),
            whole(cosine),
            whole(sine),
            whole(clip_column),
            whole(clip_row),
        ],
        out_specs=[lanes(rows), lanes(rows), lanes(rows), lanes(total, 3 * pair)],
        out_shape=[
            jax.ShapeDtypeStruct((rows, pairs * pair), jnp.bfloat16),
            jax.ShapeDtypeStruct((rows, pairs * pair), jnp.float32),
            jax.ShapeDtypeStruct((rows, pairs * pair), jnp.float32),
            jax.ShapeDtypeStruct((total, width), jnp.bfloat16),
        ],
        scratch_shapes=[pltpu.VMEM((2, total, pair), jnp.bfloat16)],
        compiler_params=KERNEL_PARAMS,
        cost_estimate=cost(2 * pairs, rows, total, 2),
    )(projected, cosine, sine, clip_column, clip_row)


def self_backward(low, grads, mixed_wide, level, cosine, sine, clip_column, clip_row):
    total, width = low.shape
    rows = grads.shape[0]
    pair = 2 * HEAD_DIM
    pairs = width // (3 * pair)
    return pl.pallas_call(
        self_backward_kernel,
        grid=(pairs,),
        in_specs=[
            lanes(total, 3 * pair),
            lanes(rows),
            lanes(rows),
            lanes(rows),
            whole(cosine),
            whole(sine),
            whole(clip_column),
            whole(clip_row),
        ],
        out_specs=lanes(total, 3 * pair),
        out_shape=jax.ShapeDtypeStruct((total, width), jnp.bfloat16),
        scratch_shapes=[
            pltpu.VMEM((pair, total), jnp.bfloat16),
            pltpu.VMEM((2, total, pair), jnp.float32),
        ],
        compiler_params=KERNEL_PARAMS,
        cost_estimate=cost(2 * pairs, rows, total, 5),
    )(low, grads, mixed_wide, level, cosine, sine, clip_column, clip_row)


def cross_forward(query, keyval, clip_column, clip_row):
    rows, width = query.shape
    keys = keyval.shape[0]
    pair = 2 * HEAD_DIM
    pairs = width // pair
    return pl.pallas_call(
        cross_forward_kernel,
        grid=(pairs,),
        in_specs=[
            lanes(rows),
            lanes(keys),
            lanes(keys, offset=pairs),
            whole(clip_column),
            whole(clip_row),
        ],
        out_specs=[lanes(rows), lanes(rows), lanes(rows)],
        out_shape=[
            jax.ShapeDtypeStruct((rows, width), jnp.bfloat16),
            jax.ShapeDtypeStruct((rows, width), jnp.float32),
            jax.ShapeDtypeStruct((rows, width), jnp.float32),
        ],
        compiler_params=KERNEL_PARAMS,
        cost_estimate=cost(2 * pairs, rows, keys, 2),
    )(query, keyval, keyval, clip_column, clip_row)


def cross_backward(query, keyval, grads, mixed_wide, level, clip_column, clip_row):
    rows, width = query.shape
    keys = keyval.shape[0]
    pair = 2 * HEAD_DIM
    pairs = width // pair
    return pl.pallas_call(
        cross_backward_kernel,
        grid=(pairs,),
        in_specs=[
            lanes(rows),
            lanes(keys),
            lanes(keys, offset=pairs),
            lanes(rows),
            lanes(rows),
            lanes(rows),
            whole(clip_column),
            whole(clip_row),
        ],
        out_specs=[lanes(rows), lanes(keys), lanes(keys)],
        out_shape=[
            jax.ShapeDtypeStruct((rows, width), jnp.bfloat16),
            jax.ShapeDtypeStruct((keys, width), jnp.bfloat16),
            jax.ShapeDtypeStruct((keys, width), jnp.bfloat16),
        ],
        compiler_params=KERNEL_PARAMS,
        cost_estimate=cost(2 * pairs, rows, keys, 5),
    )(query, keyval, keyval, grads, mixed_wide, level, clip_column, clip_row)


def norm_forward(hidden):
    centre = jnp.mean(hidden, axis=-1, keepdims=True)
    centred = hidden - centre
    spread = jnp.mean(centred * centred, axis=-1, keepdims=True)
    scale_inv = lax.rsqrt(spread + EPSILON)
    return (centred * scale_inv, scale_inv)


def norm_backward(grad_norm, normalized, scale_inv, gain_vector):
    scaled = grad_norm * gain_vector
    gain_grad = jnp.sum(grad_norm * normalized, axis=0)
    inner = (
        scaled
        - jnp.mean(scaled, axis=-1, keepdims=True)
        - normalized * jnp.mean(scaled * normalized, axis=-1, keepdims=True)
    )
    return (scale_inv * inner, gain_grad)


def rotary_tables(positions):
    half_width = HEAD_DIM // 2
    frequencies = jnp.exp(
        -math.log(10000.0) * jnp.arange(half_width, dtype=jnp.float32) / half_width
    )
    angles = positions[:, None] * frequencies
    cosine, sine = jnp.cos(angles), jnp.sin(angles)
    return (
        jnp.concatenate([cosine, cosine, cosine, cosine], axis=1),
        jnp.concatenate([-sine, sine, -sine, sine], axis=1),
    )


def time_features(step_values):
    half_width = TFEAT // 2
    frequencies = jnp.exp(
        -math.log(10000.0) * jnp.arange(half_width, dtype=jnp.float32) / half_width
    )
    angles = step_values.astype(jnp.float32)[..., None] * frequencies
    return jnp.concatenate([jnp.cos(angles), jnp.sin(angles)], axis=-1)


def gated_back(hidden_grad, gate_part, upward):
    gate_sigmoid = jax.nn.sigmoid(gate_part)
    gate_grad = hidden_grad * upward * gate_sigmoid * (1.0 + gate_part * (1.0 - gate_sigmoid))
    upward_grad = hidden_grad * gate_part * gate_sigmoid
    return jnp.concatenate([gate_grad, upward_grad], axis=-1).astype(jnp.bfloat16)


def xor_pairs(count, bit):
    return [(k, k ^ bit) for k in range(count)]


def place(buffer, block, dim, index):
    starts = [0] * buffer.ndim
    starts[dim] = index
    return lax.dynamic_update_slice(buffer, block, tuple(starts))


def take(array, index, dim=0):
    return lax.dynamic_slice_in_dim(array, index, 1, axis=dim)


def plane_bits(count):
    return [1 << b for b in range(1, count.bit_length() - 1)]


def chip_gather(values, axis):
    count = lax.axis_size(axis)
    bits = plane_bits(count)
    if len(bits) == 2 and values.shape[0] % 32 == 0:
        first, second = bits
        half = values.shape[0] // 2
        by_first = lax.ppermute(values, axis, xor_pairs(count, first))
        by_second = lax.ppermute(values, axis, xor_pairs(count, second))
        far_one = lax.ppermute(by_first[:half], axis, xor_pairs(count, second))
        far_two = lax.ppermute(by_second[half:], axis, xor_pairs(count, first))
        far = jnp.concatenate([far_one, far_two], axis=0)
        same = jnp.stack([values, by_first, by_second, far], axis=0)
    else:
        same = values[None]
        for bit in bits:
            same = jnp.concatenate([same, lax.ppermute(same, axis, xor_pairs(count, bit))], axis=0)
    if count == 1:
        return same
    other = lax.ppermute(same, axis, xor_pairs(count, 1))
    return jnp.stack([same, other], axis=1).reshape((count,) + values.shape)


def chip_gather_ordered(values, axis, me):
    count = lax.axis_size(axis)
    bits = plane_bits(count)
    if len(bits) == 2 and values.shape[0] % 2 == 0:
        first, second = bits
        half = values.shape[0] // 2
        chip, core = me // 2, me % 2
        by_first = lax.ppermute(values, axis, xor_pairs(count, first))
        by_second = lax.ppermute(values, axis, xor_pairs(count, second))
        far_one = lax.ppermute(by_first[:half], axis, xor_pairs(count, second))
        far_two = lax.ppermute(by_second[half:], axis, xor_pairs(count, first))
        same = jnp.zeros((count // 2,) + values.shape, values.dtype)
        same = place(same, values[None], 0, chip)
        same = place(same, by_first[None], 0, chip ^ 1)
        same = place(same, by_second[None], 0, chip ^ 2)
        far = jnp.concatenate([far_one, far_two], axis=0)
        same = place(same, far[None], 0, chip ^ 3)
        other = lax.ppermute(same, axis, xor_pairs(count, 1))
        result = jnp.zeros((count // 2, 2) + values.shape, values.dtype)
        result = place(result, same[:, None], 1, core)
        result = place(result, other[:, None], 1, 1 - core)
        return result.reshape((count,) + values.shape)
    return lax.all_gather(values, axis)


def chip_scatter(parts, axis):
    count = lax.axis_size(axis)
    if count == 1:
        return parts[0].astype(jnp.float32)
    low = jnp.bfloat16
    pairs = parts.reshape((count // 2, 2) + parts.shape[1:])
    got = lax.ppermute(pairs[:, 1].astype(low), axis, xor_pairs(count, 1))
    total = pairs[:, 0].astype(jnp.float32) + got.astype(jnp.float32)
    return sum_over_chips([total[r] for r in range(count // 2)], axis)


def chip_scatter_ordered(parts, axis, me):
    count = lax.axis_size(axis)
    if count == 1:
        return parts[0].astype(jnp.float32)
    low = jnp.bfloat16
    chip, core = me // 2, me % 2
    pairs = parts.reshape((count // 2, 2) + parts.shape[1:])
    got = lax.ppermute(take(pairs, 1 - core, 1).astype(low), axis, xor_pairs(count, 1))
    total = (take(pairs, core, 1).astype(jnp.float32) + got.astype(jnp.float32))[:, 0]
    return sum_over_chips([take(total, chip ^ r)[0] for r in range(count // 2)], axis)


def sum_over_chips(blocks, axis):
    count = lax.axis_size(axis)
    bits = plane_bits(count)
    low, wide = jnp.bfloat16, jnp.float32
    if len(bits) == 2 and blocks[0].shape[0] % 2 == 0:
        first, second = bits
        half = blocks[0].shape[0] // 2
        far_one = lax.ppermute(blocks[3][:half].astype(low), axis, xor_pairs(count, first))
        far_two = lax.ppermute(blocks[3][half:].astype(low), axis, xor_pairs(count, second))
        to_second = jnp.concatenate(
            [(blocks[2][:half] + far_one.astype(wide)).astype(low), blocks[2][half:].astype(low)],
            axis=0,
        )
        to_first = jnp.concatenate(
            [blocks[1][:half].astype(low), (blocks[1][half:] + far_two.astype(wide)).astype(low)],
            axis=0,
        )
        by_first = lax.ppermute(to_first, axis, xor_pairs(count, first))
        by_second = lax.ppermute(to_second, axis, xor_pairs(count, second))
        return blocks[0] + by_first.astype(wide) + by_second.astype(wide)
    total = jnp.stack(blocks, axis=0)
    for bit in reversed(bits):
        middle = total.shape[0] // 2
        got = lax.ppermute(total[middle:].astype(low), axis, xor_pairs(count, bit))
        total = total[:middle] + got.astype(wide)
    return total[0]


def line_send(blocks, axis, me):
    count = lax.axis_size(axis)
    return [
        lax.ppermute(
            take(blocks, lax.rem(me + step, count)),
            axis,
            [(k, (k + step) % count) for k in range(count)],
        )
        for step in range(1, count)
    ]


def line_exchange(blocks, axis, me):
    count = lax.axis_size(axis)
    result = blocks
    for step, got in enumerate(line_send(blocks, axis, me), 1):
        result = place(result, got, 0, lax.rem(me - step + count, count))
    return result


def line_gather(values, axis, me):
    count = lax.axis_size(axis)
    result = place(jnp.zeros((count,) + values.shape, values.dtype), values[None], 0, me)
    for step in range(1, count):
        got = lax.ppermute(values, axis, [(k, (k + step) % count) for k in range(count)])
        result = place(result, got[None], 0, lax.rem(me - step + count, count))
    return result


def line_scatter(parts, axis, me):
    count = lax.axis_size(axis)

    def part(index):
        return take(parts, index)[0].astype(jnp.float32)

    total = part(me)
    from_left = from_right = None
    for step in range(1, count):
        to_right = part(jnp.minimum(me + count - step, count - 1))
        to_left = part(jnp.maximum(me - count + step, 0))
        if step > 1:
            to_right = to_right + from_left.astype(jnp.float32)
            to_left = to_left + from_right.astype(jnp.float32)
        from_left = lax.ppermute(
            to_right.astype(jnp.bfloat16), axis, [(k, k + 1) for k in range(0, step)]
        )
        from_right = lax.ppermute(
            to_left.astype(jnp.bfloat16),
            axis,
            [(k + 1, k) for k in range(count - 1 - step, count - 1)],
        )
    if count > 1:
        total = total + from_left.astype(jnp.float32) + from_right.astype(jnp.float32)
    return total


def dot(left, right):
    return jnp.dot(left, right, preferred_element_type=jnp.float32)


def on_device(
    latents,
    context,
    clip_bounds,
    timesteps,
    self_inward,
    self_outward,
    cross_query,
    cross_keyval,
    cross_return,
    time_weight,
    expand_weight,
    shrink_weight,
    gain_attend,
    gain_cross,
    gain_feed,
    cotangent,
):
    f32, bf16 = jnp.float32, jnp.bfloat16
    frame_count = latents.shape[1]
    dp_count = lax.axis_size("dp")
    seq_count = lax.axis_size("seq")
    dp_place = lax.axis_index("dp")
    seq_place = lax.axis_index("seq")
    row_length = frame_count * seq_count
    text_count = context.shape[1]
    own_heads = HEADS // seq_count
    pairs = (own_heads + 1) // 2
    own_width = own_heads * HEAD_DIM
    pair_width = 2 * HEAD_DIM
    padded = pairs * pair_width
    hidden_width = FF // dp_count
    shard = D // (dp_count * seq_count)
    time_shard = TFEAT // (dp_count * seq_count)
    place_all = dp_place * seq_count + seq_place

    all_frames = jnp.arange(row_length, dtype=jnp.int32)
    second_start, third_start = clip_bounds[0, 0], clip_bounds[0, 1]
    frame_clips = (all_frames >= second_start).astype(jnp.int32) + (
        all_frames >= third_start
    ).astype(jnp.int32)
    clip_starts = jnp.where(
        frame_clips == 0, 0, jnp.where(frame_clips == 1, second_start, third_start)
    )
    token_slots = jnp.arange(TOKEN_ROWS, dtype=jnp.int32)
    clips = jnp.concatenate(
        [frame_clips, jnp.where(token_slots < CLIPS, token_slots, -1)]
    ).astype(f32)
    positions = jnp.concatenate(
        [all_frames - clip_starts + 1, jnp.zeros(TOKEN_ROWS, jnp.int32)]
    ).astype(f32)
    cosine, sine = rotary_tables(positions)
    clip_column, clip_row = clips[:, None], clips[None, :]
    own_clips = lax.dynamic_slice_in_dim(clips, seq_place * frame_count, frame_count)
    text_clips = (jnp.arange(text_count, dtype=jnp.int32) // CTX_LEN).astype(f32)

    inward_blocks = (
        self_inward.reshape(shard, 3, seq_count, own_width)
        .transpose(2, 0, 1, 3)
        .reshape(seq_count, shard, 3 * own_width)
    )
    extra = jnp.concatenate([time_weight.reshape(-1), gain_attend, gain_cross, gain_feed])
    extra_rows = -(-extra.shape[0] // (3 * own_width))
    sent_rows = -(-(shard + extra_rows) // 16) * 16
    extra = jnp.pad(extra, (0, (sent_rows - shard) * 3 * own_width - extra.shape[0]))
    extra = jnp.broadcast_to(
        extra.reshape(1, sent_rows - shard, 3 * own_width),
        (seq_count, sent_rows - shard, 3 * own_width),
    )
    inward_columns = line_exchange(
        jnp.concatenate([inward_blocks, extra], axis=1), "seq", seq_place
    )
    row_latents = line_gather(latents[0], "seq", seq_place).reshape(row_length, D)
    inward_all = chip_gather_ordered(inward_columns, "dp", dp_place)
    inward_own = inward_all[:, :, :shard].reshape(D, 3, own_width)
    inward_own = jnp.pad(inward_own, ((0, 0), (0, 0), (0, padded - own_width)))
    inward_own = (
        inward_own.reshape(D, 3, pairs, pair_width).transpose(0, 2, 1, 3).reshape(D, 3 * padded)
    )
    extra_all = inward_all[:, :, shard:].reshape(dp_count, seq_count, -1)
    time_full = extra_all[:, :, : time_shard * D].reshape(TFEAT, D)
    gains_all = extra_all[:, :, time_shard * D : time_shard * D + 3 * shard]
    gains_all = gains_all.reshape(dp_count, seq_count, 3, shard).astype(f32)
    attend_gain = gains_all[:, :, 0].reshape(D)
    cross_gain = gains_all[:, :, 1].reshape(D)
    feed_gain = gains_all[:, :, 2].reshape(D)
    steps_all = lax.all_gather(timesteps, "dp", axis=0, tiled=True)

    packed = jnp.concatenate(
        [
            self_outward,
            cross_keyval[:, :D],
            cross_keyval[:, D:],
            cross_query,
            cross_return,
        ],
        axis=0,
    )
    lined = lax.all_gather(packed, "seq")
    cotangent_all = chip_gather(cotangent[0], "dp").reshape(dp_count * frame_count, D)
    outward_full = chip_gather_ordered(lined[:, :shard], "dp", dp_place).reshape(D, D)
    keyval_rows = chip_gather_ordered(lined[:, shard : 2 * shard], "dp", dp_place)
    keyval_full = jnp.concatenate(
        [
            keyval_rows[:, :, : shard // 2].reshape(D // 2, D),
            keyval_rows[:, :, shard // 2 :].reshape(D // 2, D),
        ],
        axis=1,
    )
    query_full = chip_gather_ordered(lined[:, 2 * shard : 3 * shard], "dp", dp_place).reshape(D, D)
    return_full = chip_gather_ordered(lined[:, 3 * shard :], "dp", dp_place).reshape(D, D)

    expand_blocks = (
        expand_weight.reshape(shard, 2, dp_count, hidden_width)
        .transpose(2, 0, 1, 3)
        .reshape(dp_count, shard, 2 * hidden_width)
    )
    expand_part = lax.all_to_all(expand_blocks, "dp", 0, 0, tiled=True)
    expand_own = (
        lax.all_gather(expand_part, "seq", axis=1).reshape(D, 2 * hidden_width)
    )
    shrink_own = lax.all_gather(shrink_weight, "seq", tiled=True)

    feats_low = time_features(timesteps[0]).astype(bf16)
    token = dot(feats_low, time_full)
    token_norm, token_inverse = norm_forward(token)
    token_low = jnp.pad(
        (token_norm * attend_gain).astype(bf16), ((0, TOKEN_ROWS - CLIPS), (0, 0))
    )
    row_norm, row_inverse = norm_forward(row_latents.astype(f32))
    row_low = jnp.concatenate([(row_norm * attend_gain).astype(bf16), token_low], axis=0)
    projected = dot(row_low, inward_own)
    attended, attended_wide, self_level, projected_low = self_forward(
        projected, cosine, sine, clip_column, clip_row, row_length
    )
    attended_low = (
        line_exchange(
            attended[:, :own_width].reshape(seq_count, frame_count, own_width), "seq", seq_place
        )
        .transpose(1, 0, 2)
        .reshape(frame_count, D)
    )
    after_self = latents[0].astype(f32) + dot(attended_low, outward_full)

    norm_two, inverse_two = norm_forward(after_self)
    normed_two = (norm_two * cross_gain).astype(bf16)
    cross_heads = dot(normed_two, query_full).astype(bf16)
    keyval = dot(context[0], keyval_full).astype(bf16)
    crossed, crossed_wide, cross_level = cross_forward(
        cross_heads, keyval, own_clips[:, None], text_clips[None, :]
    )
    after_cross = after_self + dot(crossed, return_full)

    norm_three, inverse_three = norm_forward(after_cross)
    normed_three = (norm_three * feed_gain).astype(bf16)
    frames_all = chip_gather(normed_three, "dp").reshape(dp_count * frame_count, D)
    gate_up = dot(frames_all, expand_own)
    gate_part = gate_up[:, :hidden_width]
    upward = gate_up[:, hidden_width:]
    hidden_low = (jax.nn.silu(gate_part) * upward).astype(bf16)
    hidden_grad = dot(cotangent_all, shrink_own.T)
    expand_low = gated_back(hidden_grad, gate_part, upward)
    feed_parts = dot(expand_low, expand_own.T).astype(bf16)
    feed_norm_grad = chip_scatter(feed_parts.reshape(dp_count, frame_count, D), "dp")
    expand_grad = dot(frames_all.T, expand_low).astype(bf16)
    expand_sum = lax.psum_scatter(
        expand_grad.reshape(dp_count, seq_count, shard, 2 * hidden_width).transpose(1, 0, 2, 3),
        "seq",
        scatter_dimension=0,
    )
    shrink_part = dot(hidden_low.T, cotangent_all).astype(bf16)
    grad_shrink = lax.psum_scatter(
        shrink_part, "seq", scatter_dimension=0, tiled=True
    ).astype(f32)
    out_parts = dot(hidden_low, shrink_own).astype(bf16)
    fed = chip_scatter(out_parts.reshape(dp_count, frame_count, D), "dp")
    block_output = (after_cross + fed).astype(bf16)
    grad_expand = (
        lax.all_to_all(expand_sum, "dp", 0, 0, tiled=True)
        .reshape(dp_count, shard, 2, hidden_width)
        .transpose(1, 2, 0, 3)
        .reshape(shard, 2 * FF)
        .astype(f32)
    )

    feed_term, feed_gain_part = norm_backward(
        feed_norm_grad, norm_three, inverse_three, feed_gain
    )
    after_cross_grad = cotangent[0].astype(f32) + feed_term
    return_low = after_cross_grad.astype(bf16)
    crossed_grad = dot(return_low, return_full.T).astype(bf16)
    cross_query_low, cross_key_low, cross_value_low = cross_backward(
        cross_heads,
        keyval,
        crossed_grad,
        crossed_wide,
        cross_level,
        text_clips[:, None],
        own_clips[None, :],
    )
    cross_norm_grad = dot(cross_query_low, query_full.T)
    cross_term, cross_gain_part = norm_backward(
        cross_norm_grad, norm_two, inverse_two, cross_gain
    )
    after_self_grad = after_cross_grad + cross_term
    outward_low = after_self_grad.astype(bf16)
    attended_grad = dot(outward_low, outward_full.T).astype(bf16)
    attended_grad_own = line_exchange(
        attended_grad.reshape(frame_count, seq_count, own_width).transpose(1, 0, 2),
        "seq",
        seq_place,
    ).reshape(row_length, own_width)
    attended_grad_own = jnp.pad(attended_grad_own, ((0, 0), (0, padded - own_width)))

    def column_sum(partial):
        shaped = partial.astype(bf16).reshape(dp_count, seq_count, -1, D)
        return chip_scatter_ordered(shaped, "dp", dp_place)

    columns = jnp.concatenate(
        [
            column_sum(dot(crossed.T, return_low)),
            column_sum(dot(context[0].T, cross_key_low)),
            column_sum(dot(context[0].T, cross_value_low)),
            column_sum(dot(normed_two.T, cross_query_low)),
            column_sum(dot(attended_low.T, outward_low)),
        ],
        axis=1,
    )
    whole_sums = lax.psum_scatter(columns.astype(bf16), "seq", scatter_dimension=0).astype(f32)
    grad_return = whole_sums[:shard]
    grad_keyval = jnp.concatenate(
        [whole_sums[shard : shard + shard // 2], whole_sums[shard + shard // 2 : 2 * shard]],
        axis=1,
    )
    grad_query = whole_sums[2 * shard : 3 * shard]
    grad_outward = whole_sums[3 * shard :]

    inward_low = self_backward(
        projected_low,
        attended_grad_own,
        attended_wide,
        self_level,
        cosine,
        sine,
        clip_column,
        clip_row,
    )
    attend_parts = dot(inward_low, inward_own.T)
    attend_norm_grad = line_scatter(
        attend_parts[:row_length].reshape(seq_count, frame_count, D), "seq", seq_place
    )
    own_norm = lax.dynamic_slice_in_dim(row_norm, seq_place * frame_count, frame_count, axis=0)
    own_inverse = lax.dynamic_slice_in_dim(
        row_inverse, seq_place * frame_count, frame_count, axis=0
    )
    attend_term, _ = norm_backward(attend_norm_grad, own_norm, own_inverse, attend_gain)
    latents_grad = (after_self_grad + attend_term)[None]

    inward_grad = dot(row_low.T, inward_low).astype(bf16)
    inward_grad = (
        inward_grad.reshape(D, pairs, 3, pair_width)
        .transpose(0, 2, 1, 3)
        .reshape(D, 3, padded)[:, :, :own_width]
    )
    inward_sum = chip_scatter_ordered(
        inward_grad.reshape(dp_count, seq_count, shard, 3 * own_width), "dp", dp_place
    )
    grad_inward = (
        line_exchange(inward_sum.astype(bf16), "seq", seq_place)
        .reshape(seq_count, shard, 3, own_width)
        .transpose(1, 2, 0, 3)
        .reshape(shard, 3 * D)
        .astype(f32)
    )

    token_term, token_gain_part = norm_backward(
        attend_parts[row_length : row_length + CLIPS], token_norm, token_inverse, attend_gain
    )
    attend_gain_part = jnp.sum(attend_parts[:row_length] * row_norm, axis=0) + token_gain_part
    small = jnp.concatenate(
        [token_term, attend_gain_part[None], cross_gain_part[None], feed_gain_part[None]], axis=0
    )
    device_count = dp_count * seq_count
    small_all = lax.all_to_all(
        jnp.broadcast_to(small[None], (device_count,) + small.shape),
        ("dp", "seq"),
        0,
        0,
        tiled=True,
    )
    small_sum = jnp.sum(small_all.reshape(dp_count, seq_count, CLIPS + 3, D), axis=1)
    feats_all = time_features(steps_all).astype(bf16).astype(f32)
    feats_own = lax.dynamic_slice_in_dim(feats_all, place_all * time_shard, time_shard, axis=2)
    grad_time = jnp.einsum(
        "rct,rcn->tn",
        feats_own,
        small_sum[:, :CLIPS],
        precision=PRECISE,
        preferred_element_type=f32,
    )
    gain_sums = lax.dynamic_slice_in_dim(
        jnp.sum(small_sum[:, CLIPS:], axis=0), place_all * shard, shard, axis=1
    )
    return (
        block_output[None],
        latents_grad,
        grad_inward,
        grad_outward,
        grad_query,
        grad_keyval,
        grad_return,
        grad_time,
        grad_expand,
        grad_shrink,
        gain_sums[0],
        gain_sums[1],
        gain_sums[2],
    )


def solution(mesh):
    return jax.shard_map(
        on_device,
        mesh=mesh,
        in_specs=(
            P("dp", "seq", None),
            P("dp", None, None),
            P("dp", None),
            P("dp", None),
            P(("dp", "seq"), None),
            P(("dp", "seq"), None),
            P(("dp", "seq"), None),
            P(("dp", "seq"), None),
            P(("dp", "seq"), None),
            P(("dp", "seq"), None),
            P(("dp", "seq"), None),
            P(("dp", "seq"), None),
            P(("dp", "seq")),
            P(("dp", "seq")),
            P(("dp", "seq")),
            P("dp", "seq", None),
        ),
        out_specs=(
            P("dp", "seq", None),
            P("dp", "seq", None),
            P(("dp", "seq"), None),
            P(("dp", "seq"), None),
            P(("dp", "seq"), None),
            P(("dp", "seq"), None),
            P(("dp", "seq"), None),
            P(("dp", "seq"), None),
            P(("dp", "seq"), None),
            P(("dp", "seq"), None),
            P(("dp", "seq")),
            P(("dp", "seq")),
            P(("dp", "seq")),
        ),
        check_vma=False,
    )
```

```python
import math

import jax
import jax.numpy as jnp
from jax import lax
from jax.experimental import pallas as pl
from jax.experimental.pallas import tpu as pltpu
from jax.sharding import PartitionSpec as P

D = 1536
HEADS = 24
HEAD_DIM = 64
FF = 6144
CTX_LEN = 128
TFEAT = 256
CLIPS = 3
TOKEN_ROWS = 128


EPSILON = 1e-05
SCORE_SCALE = 0.125
MASKED = -1e30
PRECISE = lax.Precision.HIGHEST


def contract_last(left, right):
    return lax.dot_general(left, right, (((1,), (1,)), ((), ())), preferred_element_type=jnp.float32)


def contract(left, right):
    return lax.dot_general(left, right, (((1,), (0,)), ((), ())), preferred_element_type=jnp.float32)


def lane_of(width=2 * HEAD_DIM):
    return lax.broadcasted_iota(jnp.int32, (1, width), 1)


def attend_rows(query, keys, value_pair, query_clip, key_clip):
    first = lane_of() < HEAD_DIM
    allowed = query_clip == key_clip
    zero = jnp.zeros((), query.dtype)
    outs, tops = [], []
    for head in range(2):
        mine = first if head == 0 else jnp.logical_not(first)
        scores = contract_last(jnp.where(mine, query, zero), keys)
        scores = jnp.where(allowed, scores, MASKED)
        top = jnp.max(scores, axis=1, keepdims=True)
        weights = jnp.exp(scores - top).astype(jnp.bfloat16)
        mixed = contract(weights, value_pair[head])
        place_sum = HEAD_DIM if head == 0 else 0
        total = mixed[:, place_sum : place_sum + 1]
        outs.append(mixed / total)
        tops.append(top + jnp.log(total))
    mixture = jnp.where(first, outs[0], outs[1])
    return mixture, jnp.where(first, tops[0], tops[1])


def value_with_ones(values):
    first = lane_of() < HEAD_DIM
    one = jnp.ones((), values.dtype)
    return jnp.where(first, values, one), jnp.where(first, one, values)


def attend_rows_back(query, keys, keys_turned, values, grads, mixture, level, query_clip, key_clip):
    first = lane_of() < HEAD_DIM
    allowed = key_clip == query_clip
    zero = jnp.zeros((), query.dtype)
    product = jnp.transpose(grads.astype(jnp.float32) * mixture)
    level_turned = jnp.transpose(level)
    head_rows = lax.broadcasted_iota(jnp.int32, (2 * HEAD_DIM, 1), 0) < HEAD_DIM
    parts = []
    for head in range(2):
        mine = first if head == 0 else jnp.logical_not(first)
        low, high = head * HEAD_DIM, (head + 1) * HEAD_DIM
        query_own = jnp.where(mine, query, zero)
        grads_own = jnp.where(mine, grads, zero)
        scores = contract_last(keys, query_own)
        scores = jnp.where(allowed, scores, MASKED)
        weights = jnp.exp(scores - level_turned[low : low + 1])
        grad_weights = contract_last(values, grads_own)
        diagonal = jnp.sum(product[low:high], axis=0, keepdims=True)
        grad_scores = (weights * (grad_weights - diagonal)).astype(jnp.bfloat16)
        key_grad = contract(grad_scores, query_own)
        value_grad = contract(weights.astype(jnp.bfloat16), grads_own)
        parts.append((contract(keys_turned, grad_scores), key_grad, value_grad))
    query_turned = jnp.where(head_rows, parts[0][0], parts[1][0])
    return query_turned, parts[0][1] + parts[1][1], parts[0][2] + parts[1][2]


def swap_halves(values):
    quarter = HEAD_DIM // 2
    down = pltpu.roll(values, 2 * HEAD_DIM - quarter, 1)
    up = pltpu.roll(values, quarter, 1)
    return jnp.where(lane_of() % HEAD_DIM < quarter, down, up)


def self_forward_kernel(
    projected, cosine, sine, clip_column, clip_row, mixed, mixed_wide, level, low, value_pair
):
    rows = mixed.shape[0]
    pair = 2 * HEAD_DIM
    block = min(256, rows)
    for part, scale in ((0, SCORE_SCALE), (1, 1.0)):
        values = projected[:, part * pair : (part + 1) * pair]
        turned = values * cosine[...] + swap_halves(values) * sine[...]
        low[:, part * pair : (part + 1) * pair] = turned.astype(jnp.bfloat16) * jnp.bfloat16(scale)
    values = projected[:, 2 * pair : 3 * pair].astype(jnp.bfloat16)
    low[:, 2 * pair : 3 * pair] = values
    value_pair[0], value_pair[1] = value_with_ones(values)

    def step(index, carry):
        place = pl.ds(pl.multiple_of(index * block, block), block)
        mixture, tops = attend_rows(
            low[place, 0:pair],
            low[:, pair : 2 * pair],
            (value_pair[0], value_pair[1]),
            clip_column[place, :],
            clip_row[...],
        )
        mixed[place, :] = mixture.astype(jnp.bfloat16)
        mixed_wide[place, :] = mixture
        level[place, :] = tops
        return carry

    lax.fori_loop(0, rows // block, step, 0)


def self_backward_kernel(
    low, grads, mixed_wide, level, cosine, sine, clip_column, clip_row, out, keys_turned, totals
):
    rows = grads.shape[0]
    pair = 2 * HEAD_DIM
    block = min(256, rows)
    keys_turned[...] = jnp.transpose(low[:, pair : 2 * pair])
    totals[...] = jnp.zeros_like(totals)
    out[rows:, 0:pair] = jnp.zeros((out.shape[0] - rows, pair), jnp.bfloat16)

    def step(index, carry):
        start = pl.multiple_of(index * block, block)
        place = pl.ds(start, block)
        query_turned, key_grad, value_grad = attend_rows_back(
            low[place, 0:pair],
            low[:, pair : 2 * pair],
            keys_turned[...],
            low[:, 2 * pair : 3 * pair],
            grads[place, :],
            mixed_wide[place, :],
            level[place, :],
            clip_row[:, place],
            clip_column[...],
        )
        query_grad = jnp.transpose(query_turned) * SCORE_SCALE
        back = query_grad * cosine[place, :] - swap_halves(query_grad) * sine[place, :]
        out[place, 0:pair] = back.astype(jnp.bfloat16)
        totals[0] += key_grad
        totals[1] += value_grad
        return carry

    lax.fori_loop(0, rows // block, step, 0)
    key_grad = totals[0]
    back = key_grad * cosine[...] - swap_halves(key_grad) * sine[...]
    out[:, pair : 2 * pair] = back.astype(jnp.bfloat16)
    out[:, 2 * pair : 3 * pair] = totals[1].astype(jnp.bfloat16)


def cross_forward_kernel(query, keys, values, clip_column, clip_row, mixed, mixed_wide, level):
    mixture, tops = attend_rows(
        query[...] * jnp.bfloat16(SCORE_SCALE),
        keys[...],
        value_with_ones(values[...]),
        clip_column[...],
        clip_row[...],
    )
    mixed[...] = mixture.astype(jnp.bfloat16)
    mixed_wide[...] = mixture
    level[...] = tops


def cross_backward_kernel(
    query, keys, values, grads, mixed_wide, level, clip_column, clip_row, query_out, key_out, value_out
):
    query_turned, key_grad, value_grad = attend_rows_back(
        query[...] * jnp.bfloat16(SCORE_SCALE),
        keys[...],
        jnp.transpose(keys[...]),
        values[...],
        grads[...],
        mixed_wide[...],
        level[...],
        clip_row[...],
        clip_column[...],
    )
    query_out[...] = (jnp.transpose(query_turned) * SCORE_SCALE).astype(jnp.bfloat16)
    key_out[...] = key_grad.astype(jnp.bfloat16)
    value_out[...] = value_grad.astype(jnp.bfloat16)


def whole(array):
    return pl.BlockSpec(array.shape, lambda p: (0,) * array.ndim)


def lanes(rows, width=2 * HEAD_DIM, second=False):
    return pl.BlockSpec((rows, width), lambda p: (1 if second else 0, p))


KERNEL_PARAMS = pltpu.CompilerParams(
    dimension_semantics=("arbitrary",), vmem_limit_bytes=48 * 1024 * 1024
)


def cost(microseconds):
    return pl.CostEstimate(
        flops=int(microseconds * 1e9), bytes_accessed=2**20, transcendentals=0
    )


def self_forward(projected, cosine, sine, clip_column, clip_row, rows):
    total, width = projected.shape
    pair = 2 * HEAD_DIM
    pairs = width // (3 * pair)
    return pl.pallas_call(
        self_forward_kernel,
        grid=(pairs,),
        in_specs=[
            lanes(total, 3 * pair),
            whole(cosine),
            whole(sine),
            whole(clip_column),
            whole(clip_row),
        ],
        out_specs=[lanes(rows), lanes(rows), lanes(rows), lanes(total, 3 * pair)],
        out_shape=[
            jax.ShapeDtypeStruct((rows, pairs * pair), jnp.bfloat16),
            jax.ShapeDtypeStruct((rows, pairs * pair), jnp.float32),
            jax.ShapeDtypeStruct((rows, pairs * pair), jnp.float32),
            jax.ShapeDtypeStruct((total, width), jnp.bfloat16),
        ],
        scratch_shapes=[pltpu.VMEM((2, total, pair), jnp.bfloat16)],
        compiler_params=KERNEL_PARAMS,
        cost_estimate=cost(120),
    )(projected, cosine, sine, clip_column, clip_row)


def self_backward(low, grads, mixed_wide, level, cosine, sine, clip_column, clip_row):
    total, width = low.shape
    rows = grads.shape[0]
    pair = 2 * HEAD_DIM
    pairs = width // (3 * pair)
    return pl.pallas_call(
        self_backward_kernel,
        grid=(pairs,),
        in_specs=[
            lanes(total, 3 * pair),
            lanes(rows),
            lanes(rows),
            lanes(rows),
            whole(cosine),
            whole(sine),
            whole(clip_column),
            whole(clip_row),
        ],
        out_specs=lanes(total, 3 * pair),
        out_shape=jax.ShapeDtypeStruct((total, width), jnp.bfloat16),
        scratch_shapes=[
            pltpu.VMEM((pair, total), jnp.bfloat16),
            pltpu.VMEM((2, total, pair), jnp.float32),
        ],
        compiler_params=KERNEL_PARAMS,
        cost_estimate=cost(15),
    )(low, grads, mixed_wide, level, cosine, sine, clip_column, clip_row)


def cross_forward(query, keyval, clip_column, clip_row):
    rows, width = query.shape
    keys = keyval.shape[0] // 2
    pair = 2 * HEAD_DIM
    pairs = width // pair
    return pl.pallas_call(
        cross_forward_kernel,
        grid=(pairs,),
        in_specs=[
            lanes(rows),
            lanes(keys),
            lanes(keys, second=True),
            whole(clip_column),
            whole(clip_row),
        ],
        out_specs=[lanes(rows), lanes(rows), lanes(rows)],
        out_shape=[
            jax.ShapeDtypeStruct((rows, width), jnp.bfloat16),
            jax.ShapeDtypeStruct((rows, width), jnp.float32),
            jax.ShapeDtypeStruct((rows, width), jnp.float32),
        ],
        compiler_params=KERNEL_PARAMS,
        cost_estimate=cost(20),
    )(query, keyval, keyval, clip_column, clip_row)


def cross_backward(query, keyval, grads, mixed_wide, level, clip_column, clip_row):
    rows, width = query.shape
    keys = keyval.shape[0] // 2
    pair = 2 * HEAD_DIM
    pairs = width // pair
    return pl.pallas_call(
        cross_backward_kernel,
        grid=(pairs,),
        in_specs=[
            lanes(rows),
            lanes(keys),
            lanes(keys, second=True),
            lanes(rows),
            lanes(rows),
            lanes(rows),
            whole(clip_column),
            whole(clip_row),
        ],
        out_specs=[lanes(rows), lanes(keys), lanes(keys)],
        out_shape=[
            jax.ShapeDtypeStruct((rows, width), jnp.bfloat16),
            jax.ShapeDtypeStruct((keys, width), jnp.bfloat16),
            jax.ShapeDtypeStruct((keys, width), jnp.bfloat16),
        ],
        compiler_params=KERNEL_PARAMS,
        cost_estimate=cost(120),
    )(query, keyval, keyval, grads, mixed_wide, level, clip_column, clip_row)


def norm_forward(hidden):
    centre = jnp.mean(hidden, axis=-1, keepdims=True)
    centred = hidden - centre
    spread = jnp.mean(centred * centred, axis=-1, keepdims=True)
    scale_inv = lax.rsqrt(spread + EPSILON)
    return (centred * scale_inv, scale_inv)


def norm_backward(grad_norm, normalized, scale_inv, gain_vector):
    scaled = grad_norm * gain_vector
    gain_grad = jnp.sum(grad_norm * normalized, axis=0)
    inner = (
        scaled
        - jnp.mean(scaled, axis=-1, keepdims=True)
        - normalized * jnp.mean(scaled * normalized, axis=-1, keepdims=True)
    )
    return (scale_inv * inner, gain_grad)


def rotary_tables(positions):
    half_width = HEAD_DIM // 2
    frequencies = jnp.exp(
        -math.log(10000.0) * jnp.arange(half_width, dtype=jnp.float32) / half_width
    )
    angles = positions[:, None] * frequencies
    cosine, sine = jnp.cos(angles), jnp.sin(angles)
    return (
        jnp.concatenate([cosine, cosine, cosine, cosine], axis=1),
        jnp.concatenate([-sine, sine, -sine, sine], axis=1),
    )


def time_features(step_values):
    half_width = TFEAT // 2
    frequencies = jnp.exp(
        -math.log(10000.0) * jnp.arange(half_width, dtype=jnp.float32) / half_width
    )
    angles = step_values.astype(jnp.float32)[..., None] * frequencies
    return jnp.concatenate([jnp.cos(angles), jnp.sin(angles)], axis=-1)


def gated_back(hidden_grad, gate_part, upward):
    gate_sigmoid = jax.nn.sigmoid(gate_part)
    gate_grad = hidden_grad * upward * gate_sigmoid * (1.0 + gate_part * (1.0 - gate_sigmoid))
    upward_grad = hidden_grad * gate_part * gate_sigmoid
    return jnp.concatenate([gate_grad, upward_grad], axis=-1).astype(jnp.bfloat16)


def xor_pairs(count, bit):
    return [(k, k ^ bit) for k in range(count)]


def place(buffer, block, dim, index):
    starts = [0] * buffer.ndim
    starts[dim] = index
    return lax.dynamic_update_slice(buffer, block, tuple(starts))


def take(array, index, dim=0):
    return lax.dynamic_slice_in_dim(array, index, 1, axis=dim)


def plane_bits(count):
    return [1 << b for b in range(1, count.bit_length() - 1)]


def line_send(blocks, axis, me):
    count = lax.axis_size(axis)
    return [
        lax.ppermute(
            take(blocks, lax.rem(me + step, count)),
            axis,
            [(k, (k + step) % count) for k in range(count)],
        )
        for step in range(1, count)
    ]


def line_exchange(blocks, axis, me):
    count = lax.axis_size(axis)
    result = blocks
    for step, got in enumerate(line_send(blocks, axis, me), 1):
        result = place(result, got, 0, lax.rem(me - step + count, count))
    return result


def dot(left, right):
    return jnp.dot(left, right, preferred_element_type=jnp.float32)


def tie(*values):
    return lax.optimization_barrier(values)


def flip(values, bit):
    return lax.ppermute(values, "dp", xor_pairs(lax.axis_size("dp"), bit))


def two_by_two():
    return lax.axis_size("dp") == 8


def assemble(pieces, shapes, moves, places):
    count = len(pieces)

    def kernel(places_ref, *refs):
        given, results, semaphores = refs[:count], refs[count:-1], refs[-1]
        copies = []
        for number, (piece, source, result, target) in enumerate(moves):
            copy = pltpu.make_async_copy(
                given[piece].at[source(places_ref)],
                results[result].at[target(places_ref)],
                semaphores.at[number],
            )
            copy.start()
            copies.append(copy)
        for copy in copies:
            copy.wait()

    size = sum(2 * math.prod(shape) for shape in shapes)
    return pl.pallas_call(
        kernel,
        in_specs=[pl.BlockSpec(memory_space=pltpu.SMEM)]
        + [pl.BlockSpec(memory_space=pl.ANY)] * count,
        out_specs=[pl.BlockSpec(memory_space=pltpu.VMEM)] * len(shapes),
        out_shape=[jax.ShapeDtypeStruct(shape, jnp.bfloat16) for shape in shapes],
        scratch_shapes=[pltpu.SemaphoreType.DMA((len(moves),))],
        compiler_params=pltpu.CompilerParams(vmem_limit_bytes=48 * 1024 * 1024),
        cost_estimate=pl.CostEstimate(flops=0, bytes_accessed=2 * size, transcendentals=0),
    )(places, *pieces)


def everything(places):
    return slice(None)


def at(*index):
    return lambda places: index


def plane_open(values):
    if not two_by_two():
        return (values,)
    return (values, flip(values, 2), flip(values, 4))


def plane_relay(state):
    if not two_by_two():
        return state
    values, by_first, by_second = state
    half = values.shape[0] // 2
    return state + (flip(by_first[:half], 4), flip(by_second[half:], 2))


def plane_chips(state, chip=None):
    values = state[0]
    chips = lax.axis_size("dp") // 2
    if not two_by_two():
        same = values[None]
        for bit in plane_bits(2 * chips):
            same = jnp.concatenate([same, flip(same, bit)], axis=0)
        if chip is None:
            return same
        ordered = jnp.zeros(same.shape, same.dtype)
        for r in range(chips):
            ordered = place(ordered, same[r : r + 1], 0, chip ^ r)
        return ordered
    half = values.shape[0] // 2
    rest = values.shape[0] - half

    def target(r, *more):
        if chip is None:
            return at(r, *more)
        return lambda places: (places[0] ^ r,) + more

    moves = [(r, everything, 0, target(r)) for r in range(3)]
    moves.append((3, everything, 0, target(3, pl.ds(0, half))))
    moves.append((4, everything, 0, target(3, pl.ds(half, rest))))
    places = jnp.zeros((1,), jnp.int32) if chip is None else chip.reshape(1).astype(jnp.int32)
    return assemble(state, [(chips,) + values.shape], moves, places)[0]


def both_cores(same, other, core, rows):
    chips, line, _, width = same.shape
    if two_by_two() and all(count % 16 == 0 for count in rows):
        moves, start = [], 0
        for result, count in enumerate(rows):
            part = at(slice(None), slice(None), pl.ds(start, count))
            moves.append((0, part, result, lambda places: (slice(None), places[0])))
            moves.append((1, part, result, lambda places: (slice(None), 1 - places[0])))
            start += count
        return assemble(
            [same, other],
            [(chips, 2, line, count, width) for count in rows],
            moves,
            core.reshape(1).astype(jnp.int32),
        )
    full = jnp.zeros((chips, 2) + same.shape[1:], same.dtype)
    full = place(place(full, same[:, None], 1, core), other[:, None], 1, 1 - core)
    results, start = [], 0
    for count in rows:
        results.append(full[:, :, :, start : start + count])
        start += count
    return results


def plane_far(blocks):
    if not two_by_two():
        return None
    half = blocks[3].shape[0] // 2
    low = jnp.bfloat16
    return (flip(blocks[3][:half].astype(low), 2), flip(blocks[3][half:].astype(low), 4))


def plane_near(blocks, far):
    low, wide = jnp.bfloat16, jnp.float32
    if not two_by_two():
        total = jnp.stack([block.astype(wide) for block in blocks], axis=0)
        for bit in reversed(plane_bits(lax.axis_size("dp"))):
            middle = total.shape[0] // 2
            got = flip(total[middle:].astype(low), bit)
            total = total[:middle] + got.astype(wide)
        return (total[0],)
    half = blocks[3].shape[0] // 2
    to_first = jnp.concatenate(
        [
            blocks[1][:half].astype(low),
            (blocks[1][half:].astype(wide) + far[1].astype(wide)).astype(low),
        ],
        axis=0,
    )
    to_second = jnp.concatenate(
        [
            (blocks[2][:half].astype(wide) + far[0].astype(wide)).astype(low),
            blocks[2][half:].astype(low),
        ],
        axis=0,
    )
    return (blocks[0], flip(to_first, 2), flip(to_second, 4))


def plane_total(near):
    total = near[0].astype(jnp.float32)
    for got in near[1:]:
        total = total + got.astype(jnp.float32)
    return total


def relay_step(state, step):
    count = lax.axis_size("seq")
    rightward, leftward = state
    return (
        rightward
        + [lax.ppermute(rightward[-1], "seq", [(k, k + 1) for k in range(step - 1, count - 1)])],
        leftward
        + [lax.ppermute(leftward[-1], "seq", [(k + 1, k) for k in range(0, count - step)])],
    )


def relay_join(state, me):
    rightward, leftward = state
    count = len(rightward)
    shape = rightward[0].shape

    def kernel(me_ref, *refs):
        right, left, result = refs[:count], refs[count : 2 * count - 1], refs[-1]
        index = me_ref[0]
        result[pl.ds(index, 1)] = right[0][...][None]
        for step in range(1, count):
            target = lax.rem(index - step + count, count)

            @pl.when(index >= step)
            def _(step=step, target=target):
                result[pl.ds(target, 1)] = right[step][...][None]

            @pl.when(index < step)
            def _(step=step, target=target):
                result[pl.ds(target, 1)] = left[count - step - 1][...][None]

    return pl.pallas_call(
        kernel,
        in_specs=[pl.BlockSpec(memory_space=pltpu.SMEM)]
        + [pl.BlockSpec(memory_space=pltpu.VMEM)] * (2 * count - 1),
        out_specs=pl.BlockSpec(memory_space=pltpu.VMEM),
        out_shape=jax.ShapeDtypeStruct((count,) + shape, rightward[0].dtype),
        compiler_params=pltpu.CompilerParams(vmem_limit_bytes=48 * 1024 * 1024),
        cost_estimate=pl.CostEstimate(
            flops=0, bytes_accessed=6 * count * math.prod(shape), transcendentals=0
        ),
    )(me.reshape(1).astype(jnp.int32), *rightward, *leftward[1:])


def line_join(blocks, got, me):
    count = len(got) + 1
    alone = blocks.shape[0] != count
    moves = [
        (
            0,
            everything if alone else lambda places: pl.ds(places[0], 1),
            0,
            lambda places: pl.ds(places[0], 1),
        )
    ]
    for step in range(1, count):
        moves.append(
            (
                step,
                everything,
                0,
                lambda places, step=step: pl.ds(lax.rem(places[0] - step + count, count), 1),
            )
        )
    shape = (count,) + blocks.shape[1:]
    return assemble([blocks] + got, [shape], moves, me.reshape(1).astype(jnp.int32))[0]


def sum_step(parts, me, step, came):
    count = lax.axis_size("seq")
    to_right = take(parts, jnp.minimum(me + count - step, count - 1))[0].astype(jnp.float32)
    to_left = take(parts, jnp.maximum(me - count + step, 0))[0].astype(jnp.float32)
    if came is not None:
        to_right = to_right + came[0].astype(jnp.float32)
        to_left = to_left + came[1].astype(jnp.float32)
    low = jnp.bfloat16
    return (
        lax.ppermute(to_right.astype(low), "seq", [(k, k + 1) for k in range(0, step)]),
        lax.ppermute(
            to_left.astype(low), "seq", [(k + 1, k) for k in range(count - 1 - step, count - 1)]
        ),
    )


def on_device(
    latents,
    context,
    clip_bounds,
    timesteps,
    self_inward,
    self_outward,
    cross_query,
    cross_keyval,
    cross_return,
    time_weight,
    expand_weight,
    shrink_weight,
    gain_attend,
    gain_cross,
    gain_feed,
    cotangent,
):
    f32, bf16 = jnp.float32, jnp.bfloat16
    frame_count = latents.shape[1]
    dp_count = lax.axis_size("dp")
    seq_count = lax.axis_size("seq")
    dp_place = lax.axis_index("dp")
    seq_place = lax.axis_index("seq")
    row_length = frame_count * seq_count
    text_count = context.shape[1]
    own_heads = HEADS // seq_count
    pairs = (own_heads + 1) // 2
    own_width = own_heads * HEAD_DIM
    pair_width = 2 * HEAD_DIM
    padded = pairs * pair_width
    hidden_width = FF // dp_count
    shard = D // (dp_count * seq_count)
    time_shard = TFEAT // (dp_count * seq_count)
    place_all = dp_place * seq_count + seq_place
    chip_place, core_place = dp_place // 2, dp_place % 2
    chips = dp_count // 2

    all_frames = jnp.arange(row_length, dtype=jnp.int32)
    second_start, third_start = clip_bounds[0, 0], clip_bounds[0, 1]
    frame_clips = (all_frames >= second_start).astype(jnp.int32) + (
        all_frames >= third_start
    ).astype(jnp.int32)
    clip_starts = jnp.where(
        frame_clips == 0, 0, jnp.where(frame_clips == 1, second_start, third_start)
    )
    token_slots = jnp.arange(TOKEN_ROWS, dtype=jnp.int32)
    clips = jnp.concatenate(
        [frame_clips, jnp.where(token_slots < CLIPS, token_slots, -1)]
    ).astype(f32)
    positions = jnp.concatenate(
        [all_frames - clip_starts + 1, jnp.zeros(TOKEN_ROWS, jnp.int32)]
    ).astype(f32)
    cosine, sine = rotary_tables(positions)
    clip_column, clip_row = clips[:, None], clips[None, :]
    own_clips = lax.dynamic_slice_in_dim(clips, seq_place * frame_count, frame_count)
    text_clips = (jnp.arange(text_count, dtype=jnp.int32) // CTX_LEN).astype(f32)

    def by_pairs(blocks):
        blocks = jnp.pad(blocks, ((0, 0),) * 3 + ((0, padded - own_width),))
        return (
            blocks.reshape(seq_count, shard, 3, pairs, pair_width)
            .transpose(0, 1, 3, 2, 4)
            .reshape(seq_count, shard, 3 * padded)
        )

    def from_pairs(blocks):
        return (
            blocks.reshape(seq_count, shard, pairs, 3, pair_width)
            .transpose(0, 1, 3, 2, 4)
            .reshape(seq_count, shard, 3, padded)[..., :own_width]
        )

    inward_blocks = by_pairs(
        self_inward.reshape(shard, 3, seq_count, own_width).transpose(2, 0, 1, 3)
    )
    extra = jnp.concatenate([time_weight.reshape(-1), gain_attend, gain_cross, gain_feed])
    extra_rows = -(-extra.shape[0] // (16 * 3 * padded)) * 16
    extra = jnp.pad(extra, (0, extra_rows * 3 * padded - extra.shape[0]))
    extra = jnp.broadcast_to(
        extra.reshape(1, extra_rows, 3 * padded), (seq_count, extra_rows, 3 * padded)
    )
    inward_send = jnp.concatenate([inward_blocks, extra], axis=1)
    expand_blocks = (
        expand_weight.reshape(shard, 2, dp_count, hidden_width)
        .transpose(2, 0, 1, 3)
        .reshape(dp_count, shard, 2 * hidden_width)
    )

    inward_got = line_send(inward_send, "seq", seq_place)
    inward_got, latents = tie(inward_got, latents)

    moving = ([latents[0]], [latents[0]])
    for step in range(1, seq_count - 2):
        moving = relay_step(moving, step)
    inward_columns = line_join(inward_send, inward_got, seq_place)
    inward_state = plane_open(inward_columns)
    packed = jnp.concatenate(
        [self_outward, cross_keyval[:, :D], cross_keyval[:, D:], cross_query, cross_return],
        axis=0,
    )
    inward_state, moving, cosine, sine, packed, expand_blocks = tie(
        inward_state, moving, cosine, sine, packed, expand_blocks
    )

    moving = relay_step(moving, seq_count - 2)
    inward_state = plane_relay(inward_state)
    inward_same = plane_chips(inward_state, chip_place)
    inward_same, moving, packed = tie(inward_same, moving, packed)

    moving = relay_step(moving, seq_count - 1)
    lined = lax.all_gather(packed, "seq")
    inward_other = flip(inward_same, 1)
    expand_part = lax.all_to_all(expand_blocks, "dp", 0, 0, tiled=True)
    spread_rows = jnp.arange(D, dtype=jnp.int32)[None, :]
    context_rows = jnp.arange(D // 2, dtype=jnp.int32)[:, None]
    group, within = context_rows // (shard // 2), context_rows % (shard // 2)
    spread_keys = (spread_rows == group * shard + within).astype(bf16)
    spread_values = (spread_rows == group * shard + shard // 2 + within).astype(bf16)
    context_spread = jnp.concatenate(
        [dot(context[0], spread_keys).astype(bf16), dot(context[0], spread_values).astype(bf16)],
        axis=0,
    )
    inward_same, inward_other, context_spread, expand_part, moving = tie(
        inward_same, inward_other, context_spread, expand_part, moving
    )

    inward_own, extra_all = both_cores(
        inward_same, inward_other, core_place, [shard, extra_rows]
    )
    inward_own = inward_own.reshape(D, 3 * padded)
    extra_all = extra_all.reshape(dp_count, seq_count, extra_rows * 3 * padded)
    time_full = extra_all[:, :, : time_shard * D].reshape(TFEAT, D)
    gains_all = extra_all[:, :, time_shard * D : time_shard * D + 3 * shard]
    gains_all = gains_all.reshape(dp_count, seq_count, 3, shard).astype(f32)
    attend_gain = gains_all[:, :, 0].reshape(D)
    cross_gain = gains_all[:, :, 1].reshape(D)
    feed_gain = gains_all[:, :, 2].reshape(D)
    feats_low = time_features(timesteps[0]).astype(bf16)
    token = dot(feats_low, time_full)
    token_norm, token_inverse = norm_forward(token)
    token_low = jnp.pad(
        (token_norm * attend_gain).astype(bf16), ((0, TOKEN_ROWS - CLIPS), (0, 0))
    )
    row_latents = relay_join(moving, seq_place).reshape(row_length, D)
    row_norm, row_inverse = norm_forward(row_latents.astype(f32))
    row_low = jnp.concatenate([(row_norm * attend_gain).astype(bf16), token_low], axis=0)
    projected = dot(row_low, inward_own)
    projected, lined, shrink_weight = tie(projected, lined, shrink_weight)
    shrink_own = lax.all_gather(shrink_weight, "seq", tiled=True)
    expand_lined = lax.all_gather(expand_part, "seq")
    first_state = plane_open(lined[:, : 3 * shard])
    attended, attended_wide, self_level, projected_low = self_forward(
        projected, cosine, sine, clip_column, clip_row, row_length
    )
    attended, first_state = tie(attended, first_state)

    attended_blocks = attended[:, :own_width].reshape(seq_count, frame_count, own_width)
    attended_got = line_send(attended_blocks, "seq", seq_place)
    first_state = plane_relay(first_state)
    second_state = plane_open(lined[:, 3 * shard :])
    first_same = plane_chips(first_state, chip_place)
    attended_got, first_same, second_state, cotangent, shrink_own = tie(
        attended_got, first_same, second_state, cotangent, shrink_own
    )

    first_other = flip(first_same, 1)
    second_state = plane_relay(second_state)
    attended_low = (
        line_join(attended_blocks, attended_got, seq_place)
        .transpose(1, 0, 2)
        .reshape(frame_count, D)
    )
    first_other, second_state, attended_low = tie(first_other, second_state, attended_low)

    cotangent_state = plane_open(cotangent[0])
    outward_full, keyval_full, query_full = [
        weight.reshape(D, D)
        for weight in both_cores(first_same, first_other, core_place, [shard] * 3)
    ]
    second_same = plane_chips(second_state, chip_place)
    second_other = flip(second_same, 1)
    keyval = dot(context_spread, keyval_full).astype(bf16)
    after_self = latents[0].astype(f32) + dot(attended_low, outward_full)
    norm_two, inverse_two = norm_forward(after_self)
    normed_two = (norm_two * cross_gain).astype(bf16)
    cross_heads = dot(normed_two, query_full).astype(bf16)
    cross_heads, keyval, second_other, cotangent_state = tie(
        cross_heads, keyval, second_other, cotangent_state
    )

    cotangent_state = plane_relay(cotangent_state)
    cotangent_same = plane_chips(cotangent_state)
    cotangent_other = flip(cotangent_same, 1)
    return_full = both_cores(second_same, second_other, core_place, [shard])[0].reshape(D, D)
    crossed, crossed_wide, cross_level = cross_forward(
        cross_heads, keyval, own_clips[:, None], text_clips[None, :]
    )
    crossed, return_full, cotangent_other, expand_lined = tie(
        crossed, return_full, cotangent_other, expand_lined
    )
    after_cross = after_self + dot(crossed, return_full)
    norm_three, inverse_three = norm_forward(after_cross)
    normed_three = (norm_three * feed_gain).astype(bf16)
    frames_state = plane_relay(plane_open(normed_three))

    expand_own = (
        expand_lined.reshape(seq_count, dp_count, shard, 2 * hidden_width)
        .transpose(1, 0, 2, 3)
        .reshape(D, 2 * hidden_width)
    )
    half_frames = chips * frame_count
    frames_same = plane_chips(frames_state)
    frames_other = flip(frames_same, 1)
    frames = [frames_same.reshape(half_frames, D), frames_other.reshape(half_frames, D)]
    tangents = [cotangent_same.reshape(half_frames, D), cotangent_other.reshape(half_frames, D)]
    hidden_low, expand_low = [], []
    for side in range(2):
        gate_up = dot(frames[side], expand_own)
        gate_part = gate_up[:, :hidden_width]
        upward = gate_up[:, hidden_width:]
        hidden_low.append((jax.nn.silu(gate_part) * upward).astype(bf16))
        hidden_grad = dot(tangents[side], shrink_own.T)
        expand_low.append(gated_back(hidden_grad, gate_part, upward))

    def sides(array):
        return array.astype(bf16).reshape(chips, frame_count, D)

    feed_other = sides(dot(expand_low[1], expand_own.T))
    feed_got = flip(feed_other, 1)
    feed_same = sides(dot(expand_low[0], expand_own.T))
    feed_same, feed_got, hidden_low, expand_low = tie(feed_same, feed_got, hidden_low, expand_low)
    feed_blocks = [feed_same[r].astype(f32) + feed_got[r].astype(f32) for r in range(chips)]
    feed_far = plane_far(feed_blocks)
    shrink_part = (
        dot(hidden_low[0].T, tangents[0]) + dot(hidden_low[1].T, tangents[1])
    ).astype(bf16)
    feed_far, shrink_part, expand_low = tie(feed_far, shrink_part, expand_low)
    grad_shrink = lax.psum_scatter(shrink_part, "seq", scatter_dimension=0, tiled=True)

    feed_near = plane_near(feed_blocks, feed_far)
    expand_grad = (dot(frames[0].T, expand_low[0]) + dot(frames[1].T, expand_low[1])).astype(bf16)
    expand_grad = expand_grad.reshape(dp_count, seq_count, shard, 2 * hidden_width)
    expand_grad = expand_grad.transpose(1, 0, 2, 3).reshape(D, 2 * hidden_width)
    feed_near, expand_grad, hidden_low = tie(feed_near, expand_grad, hidden_low)
    expand_sum = lax.psum_scatter(expand_grad, "seq", scatter_dimension=0, tiled=True)
    expand_sum = expand_sum.reshape(dp_count, shard, 2 * hidden_width)

    def open_grad(grad):
        grad = grad.astype(bf16).reshape(chips, 2, seq_count, shard, -1)
        return grad, flip(take(grad, 1 - core_place, 1), 1)

    def side_blocks(opened):
        return [
            jnp.concatenate(
                [
                    (
                        take(take(grad, core_place, 1), chip_place ^ r)[0, 0].astype(f32)
                        + take(got, chip_place ^ r)[0, 0].astype(f32)
                    ).astype(bf16)
                    for grad, got in opened
                ],
                axis=1,
            )
            for r in range(chips)
        ]

    feed_norm_grad = plane_total(feed_near)
    feed_term, feed_gain_part = norm_backward(
        feed_norm_grad, norm_three, inverse_three, feed_gain
    )
    after_cross_grad = cotangent[0].astype(f32) + feed_term
    return_low = after_cross_grad.astype(bf16)
    crossed_grad = dot(return_low, return_full.T).astype(bf16)
    return_grad = open_grad(dot(crossed.T, return_low))
    crossed_grad, return_grad = tie(crossed_grad, return_grad)
    return_blocks = side_blocks([return_grad])
    return_far = plane_far(return_blocks)
    cross_query_low, cross_key_low, cross_value_low = cross_backward(
        cross_heads,
        keyval,
        crossed_grad,
        crossed_wide,
        cross_level,
        text_clips[:, None],
        own_clips[None, :],
    )
    cross_query_low, cross_key_low, cross_value_low, return_far, grad_shrink = tie(
        cross_query_low, cross_key_low, cross_value_low, return_far, grad_shrink
    )
    return_near = plane_near(return_blocks, return_far)
    keyval_low = jnp.concatenate([cross_key_low, cross_value_low], axis=0)
    keyval_grad = open_grad(dot(context_spread.T, keyval_low))
    query_grad = open_grad(dot(normed_two.T, cross_query_low))
    cross_norm_grad = dot(cross_query_low, query_full.T)
    cross_term, cross_gain_part = norm_backward(
        cross_norm_grad, norm_two, inverse_two, cross_gain
    )
    after_self_grad = after_cross_grad + cross_term
    outward_low = after_self_grad.astype(bf16)
    attended_grad = dot(outward_low, outward_full.T).astype(bf16)
    attended_grad, return_near, outward_low, keyval_grad, query_grad = tie(
        attended_grad, return_near, outward_low, keyval_grad, query_grad
    )

    grad_blocks = attended_grad.reshape(frame_count, seq_count, own_width).transpose(1, 0, 2)
    grad_got = line_send(grad_blocks, "seq", seq_place)
    outward_grad = open_grad(dot(attended_low.T, outward_low))
    rest_blocks = side_blocks([keyval_grad, query_grad, outward_grad])
    grad_got, rest_blocks = tie(grad_got, rest_blocks)

    rest_far = plane_far(rest_blocks)
    attended_grad_own = line_join(grad_blocks, grad_got, seq_place)
    attended_grad_own = attended_grad_own.reshape(row_length, own_width)
    attended_grad_own = jnp.pad(attended_grad_own, ((0, 0), (0, padded - own_width)))
    inward_low = self_backward(
        projected_low,
        attended_grad_own,
        attended_wide,
        self_level,
        cosine,
        sine,
        clip_column,
        clip_row,
    )
    inward_low, rest_far, expand_sum = tie(inward_low, rest_far, expand_sum)

    rest_near = plane_near(rest_blocks, rest_far)
    attend_parts = dot(inward_low, inward_own.T)
    attend_blocks = attend_parts[:row_length].reshape(seq_count, frame_count, D)
    came = sum_step(attend_blocks, seq_place, 1, None)
    inward_grad = open_grad(dot(row_low.T, inward_low))
    came, inward_grad = tie(came, inward_grad)

    for step in range(2, seq_count - 1):
        came = sum_step(attend_blocks, seq_place, step, came)
    inward_blocks = side_blocks([inward_grad])
    inward_far = plane_far(inward_blocks)
    token_term, token_gain_part = norm_backward(
        attend_parts[row_length : row_length + CLIPS], token_norm, token_inverse, attend_gain
    )
    attend_gain_part = jnp.sum(attend_parts[:row_length] * row_norm, axis=0) + token_gain_part
    feats_row = jnp.pad(feats_low.astype(f32).reshape(1, -1), ((0, 0), (0, D - CLIPS * TFEAT)))
    small = jnp.concatenate(
        [
            token_term,
            attend_gain_part[None],
            cross_gain_part[None],
            feed_gain_part[None],
            feats_row,
            jnp.zeros((1, D), f32),
        ],
        axis=0,
    )
    came, inward_far, rest_near, small = tie(came, inward_far, rest_near, small)

    whole_column = jnp.concatenate(
        [plane_total(return_near).astype(bf16), plane_total(rest_near).astype(bf16)], axis=1
    )
    whole_sums = lax.psum_scatter(whole_column, "seq", scatter_dimension=0).astype(f32)
    came = sum_step(attend_blocks, seq_place, seq_count - 1, came)
    inward_near = plane_near(inward_blocks, inward_far)
    device_count = dp_count * seq_count
    small_all = lax.all_to_all(
        jnp.broadcast_to(small[None], (device_count,) + small.shape),
        ("dp", "seq"),
        0,
        0,
        tiled=True,
    )
    fed_other = sides(dot(hidden_low[1], shrink_own))
    fed_got = flip(fed_other, 1)
    fed_same = sides(dot(hidden_low[0], shrink_own))
    inward_near, came, fed_got, fed_same, expand_sum = tie(
        inward_near, came, fed_got, fed_same, expand_sum
    )

    fed_blocks = [fed_same[r].astype(f32) + fed_got[r].astype(f32) for r in range(chips)]
    fed_far = plane_far(fed_blocks)
    inward_sum = plane_total(inward_near).astype(bf16)
    inward_moved = line_send(inward_sum, "seq", seq_place)
    attend_norm_grad = take(attend_blocks, seq_place)[0]
    attend_norm_grad = attend_norm_grad + came[0].astype(f32) + came[1].astype(f32)
    own_norm = lax.dynamic_slice_in_dim(row_norm, seq_place * frame_count, frame_count, axis=0)
    own_inverse = lax.dynamic_slice_in_dim(
        row_inverse, seq_place * frame_count, frame_count, axis=0
    )
    attend_term, _ = norm_backward(attend_norm_grad, own_norm, own_inverse, attend_gain)
    latents_grad = (after_self_grad + attend_term)[None]
    grad_expand = (
        lax.all_to_all(expand_sum, "dp", 0, 0, tiled=True)
        .reshape(dp_count, shard, 2, hidden_width)
        .transpose(1, 2, 0, 3)
        .reshape(shard, 2 * FF)
        .astype(f32)
    )
    fed_far, inward_moved, latents_grad, grad_expand = tie(
        fed_far, inward_moved, latents_grad, grad_expand
    )

    fed_near = plane_near(fed_blocks, fed_far)
    inward_rows = line_join(inward_sum, inward_moved, seq_place)
    grad_inward = (
        from_pairs(inward_rows).transpose(1, 2, 0, 3).reshape(shard, 3 * D).astype(f32)
    )
    block_output = (after_cross + plane_total(fed_near)).astype(bf16)
    grad_return = whole_sums[:shard]
    grad_keyval = jnp.concatenate(
        [whole_sums[shard : shard + shard // 2], whole_sums[shard + shard // 2 : 2 * shard]],
        axis=1,
    )
    grad_query = whole_sums[2 * shard : 3 * shard]
    grad_outward = whole_sums[3 * shard :]
    grad_shrink = grad_shrink.astype(f32)
    small_sum = jnp.sum(small_all.reshape(dp_count, seq_count, 8, D), axis=1)
    feats_all = small_all.reshape(dp_count, seq_count, 8, D)[:, 0, CLIPS + 3, : CLIPS * TFEAT]
    feats_all = feats_all.reshape(dp_count, CLIPS, TFEAT)
    feats_own = lax.dynamic_slice_in_dim(feats_all, place_all * time_shard, time_shard, axis=2)
    grad_time = jnp.einsum(
        "rct,rcn->tn",
        feats_own,
        small_sum[:, :CLIPS],
        precision=PRECISE,
        preferred_element_type=f32,
    )
    gain_sums = lax.dynamic_slice_in_dim(
        jnp.sum(small_sum[:, CLIPS : CLIPS + 3], axis=0), place_all * shard, shard, axis=1
    )
    return (
        block_output[None],
        latents_grad,
        grad_inward,
        grad_outward,
        grad_query,
        grad_keyval,
        grad_return,
        grad_time,
        grad_expand,
        grad_shrink,
        gain_sums[0],
        gain_sums[1],
        gain_sums[2],
    )


def solution(mesh):
    return jax.shard_map(
        on_device,
        mesh=mesh,
        in_specs=(
            P("dp", "seq", None),
            P("dp", None, None),
            P("dp", None),
            P("dp", None),
            P(("dp", "seq"), None),
            P(("dp", "seq"), None),
            P(("dp", "seq"), None),
            P(("dp", "seq"), None),
            P(("dp", "seq"), None),
            P(("dp", "seq"), None),
            P(("dp", "seq"), None),
            P(("dp", "seq"), None),
            P(("dp", "seq")),
            P(("dp", "seq")),
            P(("dp", "seq")),
            P("dp", "seq", None),
        ),
        out_specs=(
            P("dp", "seq", None),
            P("dp", "seq", None),
            P(("dp", "seq"), None),
            P(("dp", "seq"), None),
            P(("dp", "seq"), None),
            P(("dp", "seq"), None),
            P(("dp", "seq"), None),
            P(("dp", "seq"), None),
            P(("dp", "seq"), None),
            P(("dp", "seq"), None),
            P(("dp", "seq")),
            P(("dp", "seq")),
            P(("dp", "seq")),
        ),
        check_vma=False,
    )
```

```python
import math

import jax
import jax.numpy as jnp
from jax import lax
from jax.experimental import pallas as pl
from jax.experimental.pallas import tpu as pltpu
from jax.sharding import PartitionSpec as P

D = 1536
HEADS = 24
HEAD_DIM = 64
FF = 6144
CTX_LEN = 128
TFEAT = 256
CLIPS = 3
TOKEN_ROWS = 128


EPSILON = 1e-05
SCORE_SCALE = 0.125
MASKED = -1e30
PRECISE = lax.Precision.HIGHEST


def contract_last(left, right):
    return lax.dot_general(left, right, (((1,), (1,)), ((), ())), preferred_element_type=jnp.float32)


def contract(left, right):
    return lax.dot_general(left, right, (((1,), (0,)), ((), ())), preferred_element_type=jnp.float32)


def lane_of(width=2 * HEAD_DIM):
    return lax.broadcasted_iota(jnp.int32, (1, width), 1)


def attend_rows(query, keys, value_pair, query_clip, key_clip):
    first = lane_of() < HEAD_DIM
    allowed = query_clip == key_clip
    zero = jnp.zeros((), query.dtype)
    outs, tops = [], []
    for head in range(2):
        mine = first if head == 0 else jnp.logical_not(first)
        scores = contract_last(jnp.where(mine, query, zero), keys)
        scores = jnp.where(allowed, scores, MASKED)
        top = jnp.max(scores, axis=1, keepdims=True)
        weights = jnp.exp(scores - top).astype(jnp.bfloat16)
        mixed = contract(weights, value_pair[head])
        place_sum = HEAD_DIM if head == 0 else 0
        total = mixed[:, place_sum : place_sum + 1]
        outs.append(mixed / total)
        tops.append(top + jnp.log(total))
    mixture = jnp.where(first, outs[0], outs[1])
    return mixture, jnp.where(first, tops[0], tops[1])


def value_with_ones(values):
    first = lane_of() < HEAD_DIM
    one = jnp.ones((), values.dtype)
    return jnp.where(first, values, one), jnp.where(first, one, values)


def attend_rows_back(query, keys, keys_turned, values, grads, mixture, level, query_clip, key_clip):
    first = lane_of() < HEAD_DIM
    allowed = key_clip == query_clip
    zero = jnp.zeros((), query.dtype)
    product = jnp.transpose(grads.astype(jnp.float32) * mixture)
    level_turned = jnp.transpose(level)
    head_rows = lax.broadcasted_iota(jnp.int32, (2 * HEAD_DIM, 1), 0) < HEAD_DIM
    parts = []
    for head in range(2):
        mine = first if head == 0 else jnp.logical_not(first)
        low, high = head * HEAD_DIM, (head + 1) * HEAD_DIM
        query_own = jnp.where(mine, query, zero)
        grads_own = jnp.where(mine, grads, zero)
        scores = contract_last(keys, query_own)
        scores = jnp.where(allowed, scores, MASKED)
        weights = jnp.exp(scores - level_turned[low : low + 1])
        grad_weights = contract_last(values, grads_own)
        diagonal = jnp.sum(product[low:high], axis=0, keepdims=True)
        grad_scores = (weights * (grad_weights - diagonal)).astype(jnp.bfloat16)
        key_grad = contract(grad_scores, query_own)
        value_grad = contract(weights.astype(jnp.bfloat16), grads_own)
        parts.append((contract(keys_turned, grad_scores), key_grad, value_grad))
    query_turned = jnp.where(head_rows, parts[0][0], parts[1][0])
    return query_turned, parts[0][1] + parts[1][1], parts[0][2] + parts[1][2]


def swap_halves(values):
    quarter = HEAD_DIM // 2
    down = pltpu.roll(values, 2 * HEAD_DIM - quarter, 1)
    up = pltpu.roll(values, quarter, 1)
    return jnp.where(lane_of() % HEAD_DIM < quarter, down, up)


def self_forward_kernel(
    projected, cosine, sine, clip_column, clip_row, mixed, mixed_wide, level, low, value_pair
):
    rows = mixed.shape[0]
    pair = 2 * HEAD_DIM
    block = min(256, rows)
    for part, scale in ((0, SCORE_SCALE), (1, 1.0)):
        values = projected[:, part * pair : (part + 1) * pair]
        turned = values * cosine[...] + swap_halves(values) * sine[...]
        low[:, part * pair : (part + 1) * pair] = turned.astype(jnp.bfloat16) * jnp.bfloat16(scale)
    values = projected[:, 2 * pair : 3 * pair].astype(jnp.bfloat16)
    low[:, 2 * pair : 3 * pair] = values
    value_pair[0], value_pair[1] = value_with_ones(values)

    def step(index, carry):
        place = pl.ds(pl.multiple_of(index * block, block), block)
        mixture, tops = attend_rows(
            low[place, 0:pair],
            low[:, pair : 2 * pair],
            (value_pair[0], value_pair[1]),
            clip_column[place, :],
            clip_row[...],
        )
        mixed[place, :] = mixture.astype(jnp.bfloat16)
        mixed_wide[place, :] = mixture
        level[place, :] = tops
        return carry

    lax.fori_loop(0, rows // block, step, 0)


def self_backward_kernel(
    low, grads, mixed_wide, level, cosine, sine, clip_column, clip_row, out, keys_turned, totals
):
    rows = grads.shape[0]
    pair = 2 * HEAD_DIM
    block = min(256, rows)
    keys_turned[...] = jnp.transpose(low[:, pair : 2 * pair])
    totals[...] = jnp.zeros_like(totals)
    out[rows:, 0:pair] = jnp.zeros((out.shape[0] - rows, pair), jnp.bfloat16)

    def step(index, carry):
        start = pl.multiple_of(index * block, block)
        place = pl.ds(start, block)
        query_turned, key_grad, value_grad = attend_rows_back(
            low[place, 0:pair],
            low[:, pair : 2 * pair],
            keys_turned[...],
            low[:, 2 * pair : 3 * pair],
            grads[place, :],
            mixed_wide[place, :],
            level[place, :],
            clip_row[:, place],
            clip_column[...],
        )
        query_grad = jnp.transpose(query_turned) * SCORE_SCALE
        back = query_grad * cosine[place, :] - swap_halves(query_grad) * sine[place, :]
        out[place, 0:pair] = back.astype(jnp.bfloat16)
        totals[0] += key_grad
        totals[1] += value_grad
        return carry

    lax.fori_loop(0, rows // block, step, 0)
    key_grad = totals[0]
    back = key_grad * cosine[...] - swap_halves(key_grad) * sine[...]
    out[:, pair : 2 * pair] = back.astype(jnp.bfloat16)
    out[:, 2 * pair : 3 * pair] = totals[1].astype(jnp.bfloat16)


def cross_forward_kernel(query, keys, values, clip_column, clip_row, mixed, mixed_wide, level):
    mixture, tops = attend_rows(
        query[...] * jnp.bfloat16(SCORE_SCALE),
        keys[...],
        value_with_ones(values[...]),
        clip_column[...],
        clip_row[...],
    )
    mixed[...] = mixture.astype(jnp.bfloat16)
    mixed_wide[...] = mixture
    level[...] = tops


def cross_backward_kernel(
    query, keys, values, grads, mixed_wide, level, clip_column, clip_row, query_out, key_out, value_out
):
    query_turned, key_grad, value_grad = attend_rows_back(
        query[...] * jnp.bfloat16(SCORE_SCALE),
        keys[...],
        jnp.transpose(keys[...]),
        values[...],
        grads[...],
        mixed_wide[...],
        level[...],
        clip_row[...],
        clip_column[...],
    )
    query_out[...] = (jnp.transpose(query_turned) * SCORE_SCALE).astype(jnp.bfloat16)
    key_out[...] = key_grad.astype(jnp.bfloat16)
    value_out[...] = value_grad.astype(jnp.bfloat16)


def whole(array):
    return pl.BlockSpec(array.shape, lambda p: (0,) * array.ndim)


def lanes(rows, width=2 * HEAD_DIM, second=False):
    return pl.BlockSpec((rows, width), lambda p: (1 if second else 0, p))


KERNEL_PARAMS = pltpu.CompilerParams(
    dimension_semantics=("arbitrary",), vmem_limit_bytes=48 * 1024 * 1024
)


def cost(microseconds):
    return pl.CostEstimate(
        flops=int(microseconds * 1e9), bytes_accessed=2**20, transcendentals=0
    )


def self_forward(projected, cosine, sine, clip_column, clip_row, rows):
    total, width = projected.shape
    pair = 2 * HEAD_DIM
    pairs = width // (3 * pair)
    return pl.pallas_call(
        self_forward_kernel,
        grid=(pairs,),
        in_specs=[
            lanes(total, 3 * pair),
            whole(cosine),
            whole(sine),
            whole(clip_column),
            whole(clip_row),
        ],
        out_specs=[lanes(rows), lanes(rows), lanes(rows), lanes(total, 3 * pair)],
        out_shape=[
            jax.ShapeDtypeStruct((rows, pairs * pair), jnp.bfloat16),
            jax.ShapeDtypeStruct((rows, pairs * pair), jnp.float32),
            jax.ShapeDtypeStruct((rows, pairs * pair), jnp.float32),
            jax.ShapeDtypeStruct((total, width), jnp.bfloat16),
        ],
        scratch_shapes=[pltpu.VMEM((2, total, pair), jnp.bfloat16)],
        compiler_params=KERNEL_PARAMS,
        cost_estimate=cost(120),
    )(projected, cosine, sine, clip_column, clip_row)


def self_backward(low, grads, mixed_wide, level, cosine, sine, clip_column, clip_row):
    total, width = low.shape
    rows = grads.shape[0]
    pair = 2 * HEAD_DIM
    pairs = width // (3 * pair)
    return pl.pallas_call(
        self_backward_kernel,
        grid=(pairs,),
        in_specs=[
            lanes(total, 3 * pair),
            lanes(rows),
            lanes(rows),
            lanes(rows),
            whole(cosine),
            whole(sine),
            whole(clip_column),
            whole(clip_row),
        ],
        out_specs=lanes(total, 3 * pair),
        out_shape=jax.ShapeDtypeStruct((total, width), jnp.bfloat16),
        scratch_shapes=[
            pltpu.VMEM((pair, total), jnp.bfloat16),
            pltpu.VMEM((2, total, pair), jnp.float32),
        ],
        compiler_params=KERNEL_PARAMS,
        cost_estimate=cost(15),
    )(low, grads, mixed_wide, level, cosine, sine, clip_column, clip_row)


def cross_forward(query, keyval, clip_column, clip_row):
    rows, width = query.shape
    keys = keyval.shape[0] // 2
    pair = 2 * HEAD_DIM
    pairs = width // pair
    return pl.pallas_call(
        cross_forward_kernel,
        grid=(pairs,),
        in_specs=[
            lanes(rows),
            lanes(keys),
            lanes(keys, second=True),
            whole(clip_column),
            whole(clip_row),
        ],
        out_specs=[lanes(rows), lanes(rows), lanes(rows)],
        out_shape=[
            jax.ShapeDtypeStruct((rows, width), jnp.bfloat16),
            jax.ShapeDtypeStruct((rows, width), jnp.float32),
            jax.ShapeDtypeStruct((rows, width), jnp.float32),
        ],
        compiler_params=KERNEL_PARAMS,
        cost_estimate=cost(20),
    )(query, keyval, keyval, clip_column, clip_row)


def cross_backward(query, keyval, grads, mixed_wide, level, clip_column, clip_row):
    rows, width = query.shape
    keys = keyval.shape[0] // 2
    pair = 2 * HEAD_DIM
    pairs = width // pair
    return pl.pallas_call(
        cross_backward_kernel,
        grid=(pairs,),
        in_specs=[
            lanes(rows),
            lanes(keys),
            lanes(keys, second=True),
            lanes(rows),
            lanes(rows),
            lanes(rows),
            whole(clip_column),
            whole(clip_row),
        ],
        out_specs=[lanes(rows), lanes(keys), lanes(keys)],
        out_shape=[
            jax.ShapeDtypeStruct((rows, width), jnp.bfloat16),
            jax.ShapeDtypeStruct((keys, width), jnp.bfloat16),
            jax.ShapeDtypeStruct((keys, width), jnp.bfloat16),
        ],
        compiler_params=KERNEL_PARAMS,
        cost_estimate=cost(120),
    )(query, keyval, keyval, grads, mixed_wide, level, clip_column, clip_row)


def norm_forward(hidden):
    centre = jnp.mean(hidden, axis=-1, keepdims=True)
    centred = hidden - centre
    spread = jnp.mean(centred * centred, axis=-1, keepdims=True)
    scale_inv = lax.rsqrt(spread + EPSILON)
    return (centred * scale_inv, scale_inv)


def norm_backward(grad_norm, normalized, scale_inv, gain_vector):
    scaled = grad_norm * gain_vector
    gain_grad = jnp.sum(grad_norm * normalized, axis=0)
    inner = (
        scaled
        - jnp.mean(scaled, axis=-1, keepdims=True)
        - normalized * jnp.mean(scaled * normalized, axis=-1, keepdims=True)
    )
    return (scale_inv * inner, gain_grad)


def rotary_tables(positions):
    half_width = HEAD_DIM // 2
    frequencies = jnp.exp(
        -math.log(10000.0) * jnp.arange(half_width, dtype=jnp.float32) / half_width
    )
    angles = positions[:, None] * frequencies
    cosine, sine = jnp.cos(angles), jnp.sin(angles)
    return (
        jnp.concatenate([cosine, cosine, cosine, cosine], axis=1),
        jnp.concatenate([-sine, sine, -sine, sine], axis=1),
    )


def time_features(step_values):
    half_width = TFEAT // 2
    frequencies = jnp.exp(
        -math.log(10000.0) * jnp.arange(half_width, dtype=jnp.float32) / half_width
    )
    angles = step_values.astype(jnp.float32)[..., None] * frequencies
    return jnp.concatenate([jnp.cos(angles), jnp.sin(angles)], axis=-1)


def gated_back(hidden_grad, gate_part, upward):
    gate_sigmoid = jax.nn.sigmoid(gate_part)
    gate_grad = hidden_grad * upward * gate_sigmoid * (1.0 + gate_part * (1.0 - gate_sigmoid))
    upward_grad = hidden_grad * gate_part * gate_sigmoid
    return jnp.concatenate([gate_grad, upward_grad], axis=-1).astype(jnp.bfloat16)


def xor_pairs(count, bit):
    return [(k, k ^ bit) for k in range(count)]


def place(buffer, block, dim, index):
    starts = [0] * buffer.ndim
    starts[dim] = index
    return lax.dynamic_update_slice(buffer, block, tuple(starts))


def take(array, index, dim=0):
    return lax.dynamic_slice_in_dim(array, index, 1, axis=dim)


def plane_bits(count):
    return [1 << b for b in range(1, count.bit_length() - 1)]


def line_swap(blocks, split=0, join=0):
    return lax.all_to_all(blocks, "seq", split, join, tiled=True)


def dot(left, right):
    return jnp.dot(left, right, preferred_element_type=jnp.float32)


def tie(*values):
    return lax.optimization_barrier(values)


def flip(values, bit):
    return lax.ppermute(values, "dp", xor_pairs(lax.axis_size("dp"), bit))


def two_by_two():
    return lax.axis_size("dp") == 8


def assemble(pieces, shapes, moves, places):
    count = len(pieces)

    def kernel(places_ref, *refs):
        given, results, semaphores = refs[:count], refs[count:-1], refs[-1]
        copies = []
        for number, (piece, source, result, target) in enumerate(moves):
            copy = pltpu.make_async_copy(
                given[piece].at[source(places_ref)],
                results[result].at[target(places_ref)],
                semaphores.at[number],
            )
            copy.start()
            copies.append(copy)
        for copy in copies:
            copy.wait()

    size = sum(2 * math.prod(shape) for shape in shapes)
    return pl.pallas_call(
        kernel,
        in_specs=[pl.BlockSpec(memory_space=pltpu.SMEM)]
        + [pl.BlockSpec(memory_space=pl.ANY)] * count,
        out_specs=[pl.BlockSpec(memory_space=pltpu.VMEM)] * len(shapes),
        out_shape=[jax.ShapeDtypeStruct(shape, jnp.bfloat16) for shape in shapes],
        scratch_shapes=[pltpu.SemaphoreType.DMA((len(moves),))],
        compiler_params=pltpu.CompilerParams(vmem_limit_bytes=48 * 1024 * 1024),
        cost_estimate=pl.CostEstimate(flops=0, bytes_accessed=2 * size, transcendentals=0),
    )(places, *pieces)


def everything(places):
    return slice(None)


def at(*index):
    return lambda places: index


def plane_open(values):
    if not two_by_two():
        return (values,)
    return (values, flip(values, 2), flip(values, 4))


def plane_relay(state):
    if not two_by_two():
        return state
    values, by_first, by_second = state
    half = values.shape[0] // 2
    return state + (flip(by_first[:half], 4), flip(by_second[half:], 2))


def plane_chips(state, chip=None):
    values = state[0]
    chips = lax.axis_size("dp") // 2
    if not two_by_two():
        same = values[None]
        for bit in plane_bits(2 * chips):
            same = jnp.concatenate([same, flip(same, bit)], axis=0)
        if chip is None:
            return same
        ordered = jnp.zeros(same.shape, same.dtype)
        for r in range(chips):
            ordered = place(ordered, same[r : r + 1], 0, chip ^ r)
        return ordered
    half = values.shape[0] // 2
    rest = values.shape[0] - half

    def target(r, *more):
        if chip is None:
            return at(r, *more)
        return lambda places: (places[0] ^ r,) + more

    moves = [(r, everything, 0, target(r)) for r in range(3)]
    moves.append((3, everything, 0, target(3, pl.ds(0, half))))
    moves.append((4, everything, 0, target(3, pl.ds(half, rest))))
    places = jnp.zeros((1,), jnp.int32) if chip is None else chip.reshape(1).astype(jnp.int32)
    return assemble(state, [(chips,) + values.shape], moves, places)[0]


def both_cores(same, other, core, rows):
    chips, line, _, width = same.shape
    if two_by_two() and all(count % 16 == 0 for count in rows):
        moves, start = [], 0
        for result, count in enumerate(rows):
            part = at(slice(None), slice(None), pl.ds(start, count))
            moves.append((0, part, result, lambda places: (slice(None), places[0])))
            moves.append((1, part, result, lambda places: (slice(None), 1 - places[0])))
            start += count
        return assemble(
            [same, other],
            [(chips, 2, line, count, width) for count in rows],
            moves,
            core.reshape(1).astype(jnp.int32),
        )
    full = jnp.zeros((chips, 2) + same.shape[1:], same.dtype)
    full = place(place(full, same[:, None], 1, core), other[:, None], 1, 1 - core)
    results, start = [], 0
    for count in rows:
        results.append(full[:, :, :, start : start + count])
        start += count
    return results


def plane_far(blocks):
    if not two_by_two():
        return None
    half = blocks[3].shape[0] // 2
    low = jnp.bfloat16
    return (flip(blocks[3][:half].astype(low), 2), flip(blocks[3][half:].astype(low), 4))


def plane_near(blocks, far):
    low, wide = jnp.bfloat16, jnp.float32
    if not two_by_two():
        total = jnp.stack([block.astype(wide) for block in blocks], axis=0)
        for bit in reversed(plane_bits(lax.axis_size("dp"))):
            middle = total.shape[0] // 2
            got = flip(total[middle:].astype(low), bit)
            total = total[:middle] + got.astype(wide)
        return (total[0],)
    half = blocks[3].shape[0] // 2
    to_first = jnp.concatenate(
        [
            blocks[1][:half].astype(low),
            (blocks[1][half:].astype(wide) + far[1].astype(wide)).astype(low),
        ],
        axis=0,
    )
    to_second = jnp.concatenate(
        [
            (blocks[2][:half].astype(wide) + far[0].astype(wide)).astype(low),
            blocks[2][half:].astype(low),
        ],
        axis=0,
    )
    return (blocks[0], flip(to_first, 2), flip(to_second, 4))


def plane_total(near):
    total = near[0].astype(jnp.float32)
    for got in near[1:]:
        total = total + got.astype(jnp.float32)
    return total


def on_device(
    latents,
    context,
    clip_bounds,
    timesteps,
    self_inward,
    self_outward,
    cross_query,
    cross_keyval,
    cross_return,
    time_weight,
    expand_weight,
    shrink_weight,
    gain_attend,
    gain_cross,
    gain_feed,
    cotangent,
):
    f32, bf16 = jnp.float32, jnp.bfloat16
    frame_count = latents.shape[1]
    dp_count = lax.axis_size("dp")
    seq_count = lax.axis_size("seq")
    dp_place = lax.axis_index("dp")
    seq_place = lax.axis_index("seq")
    row_length = frame_count * seq_count
    text_count = context.shape[1]
    own_heads = HEADS // seq_count
    pairs = (own_heads + 1) // 2
    own_width = own_heads * HEAD_DIM
    pair_width = 2 * HEAD_DIM
    padded = pairs * pair_width
    hidden_width = FF // dp_count
    shard = D // (dp_count * seq_count)
    time_shard = TFEAT // (dp_count * seq_count)
    place_all = dp_place * seq_count + seq_place
    chip_place, core_place = dp_place // 2, dp_place % 2
    chips = dp_count // 2

    all_frames = jnp.arange(row_length, dtype=jnp.int32)
    second_start, third_start = clip_bounds[0, 0], clip_bounds[0, 1]
    frame_clips = (all_frames >= second_start).astype(jnp.int32) + (
        all_frames >= third_start
    ).astype(jnp.int32)
    clip_starts = jnp.where(
        frame_clips == 0, 0, jnp.where(frame_clips == 1, second_start, third_start)
    )
    token_slots = jnp.arange(TOKEN_ROWS, dtype=jnp.int32)
    clips = jnp.concatenate(
        [frame_clips, jnp.where(token_slots < CLIPS, token_slots, -1)]
    ).astype(f32)
    positions = jnp.concatenate(
        [all_frames - clip_starts + 1, jnp.zeros(TOKEN_ROWS, jnp.int32)]
    ).astype(f32)
    cosine, sine = rotary_tables(positions)
    clip_column, clip_row = clips[:, None], clips[None, :]
    own_clips = lax.dynamic_slice_in_dim(clips, seq_place * frame_count, frame_count)
    text_clips = (jnp.arange(text_count, dtype=jnp.int32) // CTX_LEN).astype(f32)

    def by_pairs(blocks):
        blocks = jnp.pad(blocks, ((0, 0),) * 3 + ((0, padded - own_width),))
        return (
            blocks.reshape(seq_count, shard, 3, pairs, pair_width)
            .transpose(0, 1, 3, 2, 4)
            .reshape(seq_count, shard, 3 * padded)
        )

    def from_pairs(blocks):
        return (
            blocks.reshape(seq_count, shard, pairs, 3, pair_width)
            .transpose(0, 1, 3, 2, 4)
            .reshape(seq_count, shard, 3, padded)[..., :own_width]
        )

    inward_blocks = by_pairs(
        self_inward.reshape(shard, 3, seq_count, own_width).transpose(2, 0, 1, 3)
    )
    extra = jnp.concatenate([time_weight.reshape(-1), gain_attend, gain_cross, gain_feed])
    extra_rows = -(-extra.shape[0] // (16 * 3 * padded)) * 16
    extra = jnp.pad(extra, (0, extra_rows * 3 * padded - extra.shape[0]))
    extra = jnp.broadcast_to(
        extra.reshape(1, extra_rows, 3 * padded), (seq_count, extra_rows, 3 * padded)
    )
    inward_send = jnp.concatenate([inward_blocks, extra], axis=1)
    expand_blocks = (
        expand_weight.reshape(shard, 2, dp_count, hidden_width)
        .transpose(2, 0, 1, 3)
        .reshape(dp_count, shard, 2 * hidden_width)
    )

    spread_rows = jnp.arange(D, dtype=jnp.int32)[None, :]
    context_rows = jnp.arange(D // 2, dtype=jnp.int32)[:, None]
    group, within = context_rows // (shard // 2), context_rows % (shard // 2)
    spread_keys = (spread_rows == group * shard + within).astype(bf16)
    spread_values = (spread_rows == group * shard + shard // 2 + within).astype(bf16)
    stacked = jnp.concatenate(
        [
            latents[0],
            self_outward,
            cross_query,
            cross_keyval[:, :D],
            cross_keyval[:, D:],
            cross_return,
        ],
        axis=0,
    )
    lined = lax.all_gather(stacked, "seq")
    inward_columns = line_swap(inward_send)
    inward_columns, cotangent = tie(inward_columns, cotangent)

    inward_state = plane_open(inward_columns)
    cotangent_state = plane_open(cotangent[0])
    context_other = flip(context, 1)
    context_spread = jnp.concatenate(
        [dot(context[0], spread_keys).astype(bf16), dot(context[0], spread_values).astype(bf16)],
        axis=0,
    )
    inward_state, cotangent_state, context_spread, context_other = tie(
        inward_state, cotangent_state, context_spread, context_other
    )

    inward_state = plane_relay(inward_state)
    cotangent_state = plane_relay(cotangent_state)
    inward_same = plane_chips(inward_state, chip_place)
    core_rows = jnp.arange(D // 2, dtype=jnp.int32)[None, :]
    core_rows = (
        core_rows // (seq_count * shard) * 2 + core_place
    ) * seq_count * shard + core_rows % (seq_count * shard)
    core_keys = (core_rows == group * shard + within).astype(bf16)
    core_values = (core_rows == group * shard + shard // 2 + within).astype(bf16)
    context_core = [
        jnp.concatenate(
            [dot(side[0], core_keys).astype(bf16), dot(side[0], core_values).astype(bf16)], axis=0
        )
        for side in (context, context_other)
    ]
    inward_same, cotangent_state, context_core = tie(inward_same, cotangent_state, context_core)

    inward_other = flip(inward_same, 1)
    cotangent_same = plane_chips(cotangent_state)
    inward_other, cosine, sine, cotangent_same = tie(inward_other, cosine, sine, cotangent_same)

    inward_own, extra_all = both_cores(
        inward_same, inward_other, core_place, [shard, extra_rows]
    )
    inward_own = inward_own.reshape(D, 3 * padded)
    extra_all = extra_all.reshape(dp_count, seq_count, extra_rows * 3 * padded)
    time_full = extra_all[:, :, : time_shard * D].reshape(TFEAT, D)
    gains_all = extra_all[:, :, time_shard * D : time_shard * D + 3 * shard]
    gains_all = gains_all.reshape(dp_count, seq_count, 3, shard).astype(f32)
    attend_gain = gains_all[:, :, 0].reshape(D)
    cross_gain = gains_all[:, :, 1].reshape(D)
    feed_gain = gains_all[:, :, 2].reshape(D)
    feats_low = time_features(timesteps[0]).astype(bf16)
    token = dot(feats_low, time_full)
    token_norm, token_inverse = norm_forward(token)
    token_low = jnp.pad(
        (token_norm * attend_gain).astype(bf16), ((0, TOKEN_ROWS - CLIPS), (0, 0))
    )
    shrink_own = lax.all_gather(shrink_weight, "seq", tiled=True)
    cotangent_other = flip(cotangent_same, 1)
    cotangent_other, inward_own, token_low, lined, cross_gain, feed_gain = tie(
        cotangent_other, inward_own, token_low, lined, cross_gain, feed_gain
    )

    def weight_rows(first, count):
        start = frame_count + first * shard
        return lined[:, start : start + count * shard]

    first_state = plane_open(weight_rows(0, 2))
    row_latents = lined[:, :frame_count].reshape(row_length, D)
    row_norm, row_inverse = norm_forward(row_latents.astype(f32))
    row_low = jnp.concatenate([(row_norm * attend_gain).astype(bf16), token_low], axis=0)
    projected = dot(row_low, inward_own)
    projected, first_state, expand_blocks = tie(projected, first_state, expand_blocks)

    first_state = plane_relay(first_state)
    keyval_state = plane_open(weight_rows(2, 1))
    expand_part = lax.all_to_all(expand_blocks, "dp", 0, 0, tiled=True)
    attended, attended_wide, self_level, projected_low = self_forward(
        projected, cosine, sine, clip_column, clip_row, row_length
    )
    attended, first_state, keyval_state, shrink_own, expand_part = tie(
        attended, first_state, keyval_state, shrink_own, expand_part
    )

    attended_low = line_swap(attended[:, :own_width], 0, 1)
    first_same = plane_chips(first_state, chip_place)
    first_other = flip(first_same, 1)
    keyval_state = plane_relay(keyval_state)
    return_state = plane_open(weight_rows(3, 1))
    attended_low, first_same, first_other, keyval_state, return_state, expand_part = tie(
        attended_low, first_same, first_other, keyval_state, return_state, expand_part
    )

    expand_lined = lax.all_gather(expand_part, "seq")
    outward_full, query_full = [
        weight.reshape(D, D)
        for weight in both_cores(first_same, first_other, core_place, [shard] * 2)
    ]
    keyval_same = plane_chips(keyval_state, chip_place)
    keyval_other = flip(keyval_same, 1)
    return_state = plane_relay(return_state)
    after_self = latents[0].astype(f32) + dot(attended_low, outward_full)
    norm_two, inverse_two = norm_forward(after_self)
    normed_two = (norm_two * cross_gain).astype(bf16)
    cross_heads = dot(normed_two, query_full).astype(bf16)
    attended_other = flip(attended_low, 1)
    cross_heads, keyval_same, keyval_other, return_state, attended_other = tie(
        cross_heads, keyval_same, keyval_other, return_state, attended_other
    )

    keyval_full = both_cores(keyval_same, keyval_other, core_place, [shard])[0].reshape(D, D)
    return_same = plane_chips(return_state, chip_place)
    return_other = flip(return_same, 1)
    keyval = dot(context_spread, keyval_full).astype(bf16)
    crossed, crossed_wide, cross_level = cross_forward(
        cross_heads, keyval, own_clips[:, None], text_clips[None, :]
    )
    return_full = both_cores(return_same, return_other, core_place, [shard])[0].reshape(D, D)
    normed_two_other = flip(normed_two, 1)
    crossed, return_full, normed_two_other = tie(crossed, return_full, normed_two_other)

    after_cross = after_self + dot(crossed, return_full)
    norm_three, inverse_three = norm_forward(after_cross)
    normed_three = (norm_three * feed_gain).astype(bf16)
    crossed_other = flip(crossed, 1)
    frames_state = plane_relay(plane_open(normed_three))
    frames_same = plane_chips(frames_state)
    frames_same, expand_lined, crossed_other = tie(frames_same, expand_lined, crossed_other)

    if two_by_two():
        expand_own = assemble(
            [expand_lined],
            [(dp_count, seq_count, shard, 2 * hidden_width)],
            [(0, at(line), 0, at(slice(None), line)) for line in range(seq_count)],
            jnp.zeros((1,), jnp.int32),
        )[0]
    else:
        expand_own = expand_lined.transpose(1, 0, 2, 3)
    expand_own = expand_own.reshape(D, 2 * hidden_width)
    half_frames = chips * frame_count
    frames_other = flip(frames_same, 1)
    frames = [frames_same.reshape(half_frames, D), frames_other.reshape(half_frames, D)]
    tangents = [cotangent_same.reshape(half_frames, D), cotangent_other.reshape(half_frames, D)]
    hidden_low, expand_low = [], []
    for side in range(2):
        gate_up = dot(frames[side], expand_own)
        gate_part = gate_up[:, :hidden_width]
        upward = gate_up[:, hidden_width:]
        hidden_low.append((jax.nn.silu(gate_part) * upward).astype(bf16))
        hidden_grad = dot(tangents[side], shrink_own.T)
        expand_low.append(gated_back(hidden_grad, gate_part, upward))

    def sides(array):
        return array.astype(bf16).reshape(chips, frame_count, D)

    feed_other = sides(dot(expand_low[1], expand_own.T))
    feed_got = flip(feed_other, 1)
    feed_same = sides(dot(expand_low[0], expand_own.T))
    feed_same, feed_got, hidden_low, expand_low = tie(feed_same, feed_got, hidden_low, expand_low)
    feed_blocks = [feed_same[r].astype(f32) + feed_got[r].astype(f32) for r in range(chips)]
    feed_far = plane_far(feed_blocks)
    shrink_part = (
        dot(hidden_low[0].T, tangents[0]) + dot(hidden_low[1].T, tangents[1])
    ).astype(bf16)
    feed_far, shrink_part, expand_low = tie(feed_far, shrink_part, expand_low)
    grad_shrink = lax.psum_scatter(shrink_part, "seq", scatter_dimension=0, tiled=True)

    feed_near = plane_near(feed_blocks, feed_far)
    expand_grad = (dot(frames[0].T, expand_low[0]) + dot(frames[1].T, expand_low[1])).astype(bf16)
    expand_grad = expand_grad.reshape(dp_count, seq_count, shard, 2 * hidden_width)
    expand_grad = expand_grad.transpose(1, 0, 2, 3).reshape(D, 2 * hidden_width)
    feed_near, expand_grad, hidden_low = tie(feed_near, expand_grad, hidden_low)
    expand_sum = lax.psum_scatter(expand_grad, "seq", scatter_dimension=0, tiled=True)
    expand_sum = expand_sum.reshape(dp_count, shard, 2 * hidden_width)

    def open_grad(grad):
        grad = grad.astype(bf16).reshape(chips, 2, seq_count, shard, -1)
        return grad, flip(take(grad, 1 - core_place, 1), 1)

    def side_block(opened, r):
        return jnp.concatenate(
            [
                (
                    take(take(grad, core_place, 1), chip_place ^ r)[0, 0].astype(f32)
                    + take(got, chip_place ^ r)[0, 0].astype(f32)
                ).astype(bf16)
                for grad, got in opened
            ],
            axis=1,
        )

    def side_blocks(opened):
        return [side_block(opened, r) for r in range(chips)]

    def both_grad(left, left_other, right, right_other):
        return (dot(left.T, right) + dot(left_other.T, right_other)).astype(bf16)

    def own_core(grad):
        return take(grad.reshape(chips, 2, seq_count, shard, D), core_place, 1)[:, 0]

    feed_norm_grad = plane_total(feed_near)
    feed_term, feed_gain_part = norm_backward(
        feed_norm_grad, norm_three, inverse_three, feed_gain
    )
    after_cross_grad = cotangent[0].astype(f32) + feed_term
    return_low = after_cross_grad.astype(bf16)
    crossed_grad = dot(return_low, return_full.T).astype(bf16)
    return_other = flip(return_low, 1)
    crossed_grad, return_low, return_other = tie(crossed_grad, return_low, return_other)
    cross_query_low, cross_key_low, cross_value_low = cross_backward(
        cross_heads,
        keyval,
        crossed_grad,
        crossed_wide,
        cross_level,
        text_clips[:, None],
        own_clips[None, :],
    )
    cross_query_low, cross_key_low, cross_value_low = tie(
        cross_query_low, cross_key_low, cross_value_low
    )
    cross_norm_grad = dot(cross_query_low, query_full.T)
    cross_term, cross_gain_part = norm_backward(
        cross_norm_grad, norm_two, inverse_two, cross_gain
    )
    after_self_grad = after_cross_grad + cross_term
    outward_low = after_self_grad.astype(bf16)
    attended_grad = dot(outward_low, outward_full.T).astype(bf16)
    keyval_low = jnp.concatenate([cross_key_low, cross_value_low], axis=0)
    keyval_low_other = flip(keyval_low, 1)
    cross_query_other = flip(cross_query_low, 1)
    attended_grad, outward_low, keyval_low, keyval_low_other, cross_query_other, return_other = tie(
        attended_grad, outward_low, keyval_low, keyval_low_other, cross_query_other, return_other
    )

    attended_grad_own = line_swap(attended_grad, 1, 0)
    outward_other = flip(outward_low, 1)
    keyval_grad = both_grad(context_core[0], context_core[1], keyval_low, keyval_low_other)
    whole_grads = [
        own_core(both_grad(crossed, crossed_other, return_low, return_other)),
        keyval_grad.reshape(chips, seq_count, shard, D),
        own_core(both_grad(normed_two, normed_two_other, cross_query_low, cross_query_other)),
        own_core(both_grad(attended_low, attended_other, outward_low, outward_other)),
    ]
    halves = [
        [
            jnp.concatenate([take(grad, chip_place ^ r)[0] for grad in group], axis=1)
            for r in range(chips)
        ]
        for group in (whole_grads[:2], whole_grads[2:])
    ]
    half_far = [plane_far(blocks) for blocks in halves]
    attended_grad_own, half_far, grad_shrink = tie(attended_grad_own, half_far, grad_shrink)

    near_early = plane_near(halves[0], half_far[0])
    attended_grad_own = jnp.pad(attended_grad_own, ((0, 0), (0, padded - own_width)))
    inward_low = self_backward(
        projected_low,
        attended_grad_own,
        attended_wide,
        self_level,
        cosine,
        sine,
        clip_column,
        clip_row,
    )
    inward_low, near_early = tie(inward_low, near_early)

    near_late = plane_near(halves[1], half_far[1])
    attend_parts = dot(inward_low, inward_own.T)
    attend_low = attend_parts[:row_length].astype(bf16)
    attend_low, inward_low, attend_parts, near_late, expand_sum, hidden_low = tie(
        attend_low, inward_low, attend_parts, near_late, expand_sum, hidden_low
    )

    attend_sum = lax.psum_scatter(attend_low, "seq", scatter_dimension=0, tiled=True)
    expand_rows = lax.all_to_all(expand_sum, "dp", 0, 0, tiled=True)
    inward_blocks = side_blocks([open_grad(dot(row_low.T, inward_low))])
    inward_far = plane_far(inward_blocks)
    whole_column = jnp.concatenate(
        [plane_total(near_early).astype(bf16), plane_total(near_late).astype(bf16)], axis=1
    )
    token_term, token_gain_part = norm_backward(
        attend_parts[row_length : row_length + CLIPS], token_norm, token_inverse, attend_gain
    )
    attend_gain_part = jnp.sum(attend_parts[:row_length] * row_norm, axis=0) + token_gain_part
    feats_row = feats_low.astype(f32).reshape(-1)
    device_count = dp_count * seq_count
    gain_parts = jnp.stack([attend_gain_part, cross_gain_part, feed_gain_part], axis=0)
    gain_parts = gain_parts.reshape(3, device_count, shard).transpose(1, 0, 2)
    common = jnp.concatenate([token_term.reshape(-1), feats_row]).astype(bf16)
    small = jnp.concatenate(
        [
            jnp.broadcast_to(common[None], (device_count,) + common.shape),
            gain_parts.reshape(device_count, 3 * shard).astype(bf16),
        ],
        axis=1,
    )
    small = jnp.pad(small, ((0, 0), (0, -small.shape[1] % 2048)))
    small = small.reshape(device_count, -1, 128)
    fed_other = sides(dot(hidden_low[1], shrink_own))
    fed_got = flip(fed_other, 1)
    fed_same = sides(dot(hidden_low[0], shrink_own))
    inward_far, fed_got, fed_same, small, expand_rows, whole_column = tie(
        inward_far, fed_got, fed_same, small, expand_rows, whole_column
    )

    whole_sums = lax.psum_scatter(whole_column, "seq", scatter_dimension=0)
    small_all = lax.all_to_all(small, ("dp", "seq"), 0, 0, tiled=True).astype(f32)
    inward_near = plane_near(inward_blocks, inward_far)
    fed_blocks = [fed_same[r].astype(f32) + fed_got[r].astype(f32) for r in range(chips)]
    fed_far = plane_far(fed_blocks)
    inward_near, fed_far, expand_rows, small_all, attend_sum = tie(
        inward_near, fed_far, expand_rows, small_all, attend_sum
    )

    inward_rows = line_swap(plane_total(inward_near).astype(bf16))
    fed_near = plane_near(fed_blocks, fed_far)
    grad_expand = (
        expand_rows.reshape(dp_count, shard, 2, hidden_width)
        .transpose(1, 2, 0, 3)
        .reshape(shard, 2 * FF)
        .astype(f32)
    )
    inward_rows, fed_near, grad_expand, whole_sums = tie(
        inward_rows, fed_near, grad_expand, whole_sums
    )
    whole_sums = whole_sums.astype(f32)

    block_output = (after_cross + plane_total(fed_near)).astype(bf16)
    own_norm = lax.dynamic_slice_in_dim(row_norm, seq_place * frame_count, frame_count, axis=0)
    own_inverse = lax.dynamic_slice_in_dim(
        row_inverse, seq_place * frame_count, frame_count, axis=0
    )
    attend_term, _ = norm_backward(
        attend_sum.astype(f32), own_norm, own_inverse, attend_gain
    )
    latents_grad = (after_self_grad + attend_term)[None]
    grad_shrink = grad_shrink.astype(f32)
    grad_inward = (
        from_pairs(inward_rows).transpose(1, 2, 0, 3).reshape(shard, 3 * D).astype(f32)
    )
    grad_return = whole_sums[:shard]
    grad_keyval = jnp.concatenate(
        [whole_sums[shard : shard + shard // 2], whole_sums[shard + shard // 2 : 2 * shard]],
        axis=1,
    )
    grad_query = whole_sums[2 * shard : 3 * shard]
    grad_outward = whole_sums[3 * shard :]
    small_all = small_all.reshape(device_count, -1)
    token_count, feats_count = CLIPS * D, CLIPS * TFEAT
    token_sum = jnp.sum(
        small_all[:, :token_count].reshape(dp_count, seq_count, CLIPS, D), axis=1
    )
    feats_all = small_all.reshape(dp_count, seq_count, -1)[:, 0]
    feats_all = feats_all[:, token_count : token_count + feats_count]
    feats_all = feats_all.reshape(dp_count, CLIPS, TFEAT)
    feats_own = lax.dynamic_slice_in_dim(feats_all, place_all * time_shard, time_shard, axis=2)
    grad_time = jnp.einsum(
        "rct,rcn->tn",
        feats_own,
        token_sum,
        precision=PRECISE,
        preferred_element_type=f32,
    )
    gain_start = token_count + feats_count
    gain_sums = jnp.sum(small_all[:, gain_start : gain_start + 3 * shard], axis=0)
    gain_sums = gain_sums.reshape(3, shard)
    return (
        block_output[None],
        latents_grad,
        grad_inward,
        grad_outward,
        grad_query,
        grad_keyval,
        grad_return,
        grad_time,
        grad_expand,
        grad_shrink,
        gain_sums[0],
        gain_sums[1],
        gain_sums[2],
    )


def solution(mesh):
    return jax.shard_map(
        on_device,
        mesh=mesh,
        in_specs=(
            P("dp", "seq", None),
            P("dp", None, None),
            P("dp", None),
            P("dp", None),
            P(("dp", "seq"), None),
            P(("dp", "seq"), None),
            P(("dp", "seq"), None),
            P(("dp", "seq"), None),
            P(("dp", "seq"), None),
            P(("dp", "seq"), None),
            P(("dp", "seq"), None),
            P(("dp", "seq"), None),
            P(("dp", "seq")),
            P(("dp", "seq")),
            P(("dp", "seq")),
            P("dp", "seq", None),
        ),
        out_specs=(
            P("dp", "seq", None),
            P("dp", "seq", None),
            P(("dp", "seq"), None),
            P(("dp", "seq"), None),
            P(("dp", "seq"), None),
            P(("dp", "seq"), None),
            P(("dp", "seq"), None),
            P(("dp", "seq"), None),
            P(("dp", "seq"), None),
            P(("dp", "seq"), None),
            P(("dp", "seq")),
            P(("dp", "seq")),
            P(("dp", "seq")),
        ),
        check_vma=False,
    )
```

```python
import math

import jax
import jax.numpy as jnp
from jax import lax
from jax.experimental import pallas as pl
from jax.experimental.pallas import tpu as pltpu
from jax.sharding import PartitionSpec as P

D = 1536
HEADS = 24
HEAD_DIM = 64
FF = 6144
CTX_LEN = 128
TFEAT = 256
CLIPS = 3
TOKEN_ROWS = 128


EPSILON = 1e-05
SCORE_SCALE = 0.125
MASKED = -1e30
PRECISE = lax.Precision.HIGHEST


def contract_last(left, right):
    return lax.dot_general(left, right, (((1,), (1,)), ((), ())), preferred_element_type=jnp.float32)


def contract(left, right):
    return lax.dot_general(left, right, (((1,), (0,)), ((), ())), preferred_element_type=jnp.float32)


def lane_of(width=2 * HEAD_DIM):
    return lax.broadcasted_iota(jnp.int32, (1, width), 1)


def clip_features(clips):
    slot = (lane_of() % HEAD_DIM).astype(jnp.float32)
    used = slot < CLIPS + 1
    of_query = jnp.where(used & (slot != clips), MASKED, 0.0)
    of_key = jnp.where(used & (slot == jnp.where(clips < 0, float(CLIPS), clips)), 1.0, 0.0)
    return of_query.astype(jnp.bfloat16), of_key.astype(jnp.bfloat16)


def attend_rows(query, query_clips, key_pair, value_pair):
    first = lane_of() < HEAD_DIM
    outs, tops = [], []
    for head in range(2):
        mine = first if head == 0 else jnp.logical_not(first)
        scores = contract_last(jnp.where(mine, query, query_clips), key_pair[head])
        top = jnp.max(scores, axis=1, keepdims=True)
        weights = jnp.exp(scores - top).astype(jnp.bfloat16)
        mixed = contract(weights, value_pair[head])
        place_sum = HEAD_DIM if head == 0 else 0
        total = mixed[:, place_sum : place_sum + 1]
        outs.append(mixed / total)
        tops.append(top + jnp.log(total))
    mixture = jnp.where(first, outs[0], outs[1])
    return mixture, jnp.where(first, tops[0], tops[1])


def value_with_ones(values):
    first = lane_of() < HEAD_DIM
    one = jnp.ones((), values.dtype)
    return jnp.where(first, values, one), jnp.where(first, one, values)


def key_with_clips(keys, key_clips):
    first = lane_of() < HEAD_DIM
    return jnp.where(first, keys, key_clips), jnp.where(first, key_clips, keys)


def attend_rows_back(query, query_clips, key_pair, keys_turned, values, grads, mixture, level):
    first = lane_of() < HEAD_DIM
    zero = jnp.zeros((), query.dtype)
    product = jnp.transpose(grads.astype(jnp.float32) * mixture)
    level_turned = jnp.transpose(level)
    head_rows = lax.broadcasted_iota(jnp.int32, (2 * HEAD_DIM, 1), 0) < HEAD_DIM
    parts = []
    for head in range(2):
        mine = first if head == 0 else jnp.logical_not(first)
        low, high = head * HEAD_DIM, (head + 1) * HEAD_DIM
        query_own = jnp.where(mine, query, zero)
        grads_own = jnp.where(mine, grads, zero)
        scores = contract_last(key_pair[head], jnp.where(mine, query, query_clips))
        weights = jnp.exp(scores - level_turned[low : low + 1])
        grad_weights = contract_last(values, grads_own)
        diagonal = jnp.sum(product[low:high], axis=0, keepdims=True)
        grad_scores = (weights * (grad_weights - diagonal)).astype(jnp.bfloat16)
        key_grad = contract(grad_scores, query_own)
        value_grad = contract(weights.astype(jnp.bfloat16), grads_own)
        parts.append((contract(keys_turned, grad_scores), key_grad, value_grad))
    query_turned = jnp.where(head_rows, parts[0][0], parts[1][0])
    return query_turned, parts[0][1] + parts[1][1], parts[0][2] + parts[1][2]


def swap_halves(values):
    quarter = HEAD_DIM // 2
    down = pltpu.roll(values, 2 * HEAD_DIM - quarter, 1)
    up = pltpu.roll(values, quarter, 1)
    return jnp.where(lane_of() % HEAD_DIM < quarter, down, up)


def self_forward_kernel(
    projected, cosine, sine, clip_column, mixed, mixed_wide, level, low, key_pair, value_pair
):
    rows = mixed.shape[0]
    pair = 2 * HEAD_DIM
    block = min(256, rows)
    for part, scale in ((0, SCORE_SCALE), (1, 1.0)):
        values = projected[:, part * pair : (part + 1) * pair]
        turned = values * cosine[...] + swap_halves(values) * sine[...]
        low[:, part * pair : (part + 1) * pair] = turned.astype(jnp.bfloat16) * jnp.bfloat16(scale)
    values = projected[:, 2 * pair : 3 * pair].astype(jnp.bfloat16)
    low[:, 2 * pair : 3 * pair] = values
    value_pair[0], value_pair[1] = value_with_ones(values)
    _, key_clips = clip_features(clip_column[...])
    key_pair[0], key_pair[1] = key_with_clips(low[:, pair : 2 * pair], key_clips)

    def step(index, carry):
        place = pl.ds(pl.multiple_of(index * block, block), block)
        query_clips, _ = clip_features(clip_column[place, :])
        mixture, tops = attend_rows(
            low[place, 0:pair],
            query_clips,
            (key_pair[0], key_pair[1]),
            (value_pair[0], value_pair[1]),
        )
        mixed[place, :] = mixture.astype(jnp.bfloat16)
        mixed_wide[place, :] = mixture
        level[place, :] = tops
        return carry

    lax.fori_loop(0, rows // block, step, 0, unroll=True)


def self_backward_kernel(
    low, grads, mixed_wide, level, cosine, sine, clip_column, out, key_pair, keys_turned, totals
):
    rows = grads.shape[0]
    pair = 2 * HEAD_DIM
    block = min(256, rows)
    keys_turned[...] = jnp.transpose(low[:, pair : 2 * pair])
    _, key_clips = clip_features(clip_column[...])
    key_pair[0], key_pair[1] = key_with_clips(low[:, pair : 2 * pair], key_clips)
    totals[...] = jnp.zeros_like(totals)
    out[rows:, 0:pair] = jnp.zeros((out.shape[0] - rows, pair), jnp.bfloat16)

    def step(index, carry):
        start = pl.multiple_of(index * block, block)
        place = pl.ds(start, block)
        query_clips, _ = clip_features(clip_column[place, :])
        query_turned, key_grad, value_grad = attend_rows_back(
            low[place, 0:pair],
            query_clips,
            (key_pair[0], key_pair[1]),
            keys_turned[...],
            low[:, 2 * pair : 3 * pair],
            grads[place, :],
            mixed_wide[place, :],
            level[place, :],
        )
        query_grad = jnp.transpose(query_turned) * SCORE_SCALE
        back = query_grad * cosine[place, :] - swap_halves(query_grad) * sine[place, :]
        out[place, 0:pair] = back.astype(jnp.bfloat16)
        totals[0] += key_grad
        totals[1] += value_grad
        return carry

    lax.fori_loop(0, rows // block, step, 0, unroll=True)
    key_grad = totals[0]
    back = key_grad * cosine[...] - swap_halves(key_grad) * sine[...]
    out[:, pair : 2 * pair] = back.astype(jnp.bfloat16)
    out[:, 2 * pair : 3 * pair] = totals[1].astype(jnp.bfloat16)


def cross_forward_kernel(query, keys, values, clip_column, text_column, mixed, mixed_wide, level):
    pair = 2 * HEAD_DIM
    query_clips, _ = clip_features(clip_column[...])
    _, key_clips = clip_features(text_column[...])
    for start in range(0, query.shape[1], pair):
        part = slice(start, start + pair)
        mixture, tops = attend_rows(
            query[:, part] * jnp.bfloat16(SCORE_SCALE),
            query_clips,
            key_with_clips(keys[:, part], key_clips),
            value_with_ones(values[:, part]),
        )
        mixed[:, part] = mixture.astype(jnp.bfloat16)
        mixed_wide[:, part] = mixture
        level[:, part] = tops


def cross_backward_kernel(
    query, keys, values, grads, mixed_wide, level, clip_column, text_column, query_out, key_out, value_out
):
    pair = 2 * HEAD_DIM
    query_clips, _ = clip_features(clip_column[...])
    _, key_clips = clip_features(text_column[...])
    for start in range(0, query.shape[1], pair):
        part = slice(start, start + pair)
        query_turned, key_grad, value_grad = attend_rows_back(
            query[:, part] * jnp.bfloat16(SCORE_SCALE),
            query_clips,
            key_with_clips(keys[:, part], key_clips),
            jnp.transpose(keys[:, part]),
            values[:, part],
            grads[:, part],
            mixed_wide[:, part],
            level[:, part],
        )
        query_out[:, part] = (jnp.transpose(query_turned) * SCORE_SCALE).astype(jnp.bfloat16)
        key_out[:, part] = key_grad.astype(jnp.bfloat16)
        value_out[:, part] = value_grad.astype(jnp.bfloat16)


def whole(array):
    return pl.BlockSpec(array.shape, lambda p: (0,) * array.ndim)


def lanes(rows, width=2 * HEAD_DIM, second=False):
    return pl.BlockSpec((rows, width), lambda p: (1 if second else 0, p))


CROSS_PAIRS = 3
KERNEL_PARAMS = pltpu.CompilerParams(
    dimension_semantics=("arbitrary",), vmem_limit_bytes=48 * 1024 * 1024
)


def cost(microseconds):
    return pl.CostEstimate(
        flops=int(microseconds * 1e9), bytes_accessed=2**20, transcendentals=0
    )


def self_forward(projected, cosine, sine, clip_column, rows):
    total, width = projected.shape
    pair = 2 * HEAD_DIM
    pairs = width // (3 * pair)
    return pl.pallas_call(
        self_forward_kernel,
        grid=(pairs,),
        in_specs=[
            lanes(total, 3 * pair),
            whole(cosine),
            whole(sine),
            whole(clip_column),
        ],
        out_specs=[lanes(rows), lanes(rows), lanes(rows), lanes(total, 3 * pair)],
        out_shape=[
            jax.ShapeDtypeStruct((rows, pairs * pair), jnp.bfloat16),
            jax.ShapeDtypeStruct((rows, pairs * pair), jnp.float32),
            jax.ShapeDtypeStruct((rows, pairs * pair), jnp.float32),
            jax.ShapeDtypeStruct((total, width), jnp.bfloat16),
        ],
        scratch_shapes=[
            pltpu.VMEM((2, total, pair), jnp.bfloat16),
            pltpu.VMEM((2, total, pair), jnp.bfloat16),
        ],
        compiler_params=KERNEL_PARAMS,
        cost_estimate=cost(120),
    )(projected, cosine, sine, clip_column)


def self_backward(low, grads, mixed_wide, level, cosine, sine, clip_column):
    total, width = low.shape
    rows = grads.shape[0]
    pair = 2 * HEAD_DIM
    pairs = width // (3 * pair)
    return pl.pallas_call(
        self_backward_kernel,
        grid=(pairs,),
        in_specs=[
            lanes(total, 3 * pair),
            lanes(rows),
            lanes(rows),
            lanes(rows),
            whole(cosine),
            whole(sine),
            whole(clip_column),
        ],
        out_specs=lanes(total, 3 * pair),
        out_shape=jax.ShapeDtypeStruct((total, width), jnp.bfloat16),
        scratch_shapes=[
            pltpu.VMEM((2, total, pair), jnp.bfloat16),
            pltpu.VMEM((pair, total), jnp.bfloat16),
            pltpu.VMEM((2, total, pair), jnp.float32),
        ],
        compiler_params=KERNEL_PARAMS,
        cost_estimate=cost(2),
    )(low, grads, mixed_wide, level, cosine, sine, clip_column)


def cross_forward(query, keyval, clip_column, text_column):
    rows, width = query.shape
    keys = keyval.shape[0] // 2
    group = 2 * HEAD_DIM * CROSS_PAIRS
    steps = width // group
    return pl.pallas_call(
        cross_forward_kernel,
        grid=(steps,),
        in_specs=[
            lanes(rows, group),
            lanes(keys, group),
            lanes(keys, group, second=True),
            whole(clip_column),
            whole(text_column),
        ],
        out_specs=[lanes(rows, group), lanes(rows, group), lanes(rows, group)],
        out_shape=[
            jax.ShapeDtypeStruct((rows, width), jnp.bfloat16),
            jax.ShapeDtypeStruct((rows, width), jnp.float32),
            jax.ShapeDtypeStruct((rows, width), jnp.float32),
        ],
        compiler_params=KERNEL_PARAMS,
        cost_estimate=cost(20),
    )(query, keyval, keyval, clip_column, text_column)


def cross_backward(query, keyval, grads, mixed_wide, level, clip_column, text_column):
    rows, width = query.shape
    keys = keyval.shape[0] // 2
    group = 2 * HEAD_DIM * CROSS_PAIRS
    steps = width // group
    return pl.pallas_call(
        cross_backward_kernel,
        grid=(steps,),
        in_specs=[
            lanes(rows, group),
            lanes(keys, group),
            lanes(keys, group, second=True),
            lanes(rows, group),
            lanes(rows, group),
            lanes(rows, group),
            whole(clip_column),
            whole(text_column),
        ],
        out_specs=[lanes(rows, group), lanes(keys, group), lanes(keys, group)],
        out_shape=[
            jax.ShapeDtypeStruct((rows, width), jnp.bfloat16),
            jax.ShapeDtypeStruct((keys, width), jnp.bfloat16),
            jax.ShapeDtypeStruct((keys, width), jnp.bfloat16),
        ],
        compiler_params=KERNEL_PARAMS,
        cost_estimate=cost(120),
    )(query, keyval, keyval, grads, mixed_wide, level, clip_column, text_column)


def norm_forward(hidden):
    centre = jnp.mean(hidden, axis=-1, keepdims=True)
    centred = hidden - centre
    spread = jnp.mean(centred * centred, axis=-1, keepdims=True)
    scale_inv = lax.rsqrt(spread + EPSILON)
    return (centred * scale_inv, scale_inv)


def norm_backward(grad_norm, normalized, scale_inv, gain_vector):
    scaled = grad_norm * gain_vector
    gain_grad = jnp.sum(grad_norm * normalized, axis=0)
    inner = (
        scaled
        - jnp.mean(scaled, axis=-1, keepdims=True)
        - normalized * jnp.mean(scaled * normalized, axis=-1, keepdims=True)
    )
    return (scale_inv * inner, gain_grad)


def rotary_tables(positions):
    half_width = HEAD_DIM // 2
    frequencies = jnp.exp(
        -math.log(10000.0) * jnp.arange(half_width, dtype=jnp.float32) / half_width
    )
    angles = positions[:, None] * frequencies
    cosine, sine = jnp.cos(angles), jnp.sin(angles)
    return (
        jnp.concatenate([cosine, cosine, cosine, cosine], axis=1),
        jnp.concatenate([-sine, sine, -sine, sine], axis=1),
    )


def time_features(step_values):
    half_width = TFEAT // 2
    frequencies = jnp.exp(
        -math.log(10000.0) * jnp.arange(half_width, dtype=jnp.float32) / half_width
    )
    angles = step_values.astype(jnp.float32)[..., None] * frequencies
    return jnp.concatenate([jnp.cos(angles), jnp.sin(angles)], axis=-1)


def gated_back(hidden_grad, gate_part, upward):
    gate_sigmoid = jax.nn.sigmoid(gate_part)
    gate_grad = hidden_grad * upward * gate_sigmoid * (1.0 + gate_part * (1.0 - gate_sigmoid))
    upward_grad = hidden_grad * gate_part * gate_sigmoid
    return jnp.concatenate([gate_grad, upward_grad], axis=-1).astype(jnp.bfloat16)


def xor_pairs(count, bit):
    return [(k, k ^ bit) for k in range(count)]


def place(buffer, block, dim, index):
    starts = [0] * buffer.ndim
    starts[dim] = index
    return lax.dynamic_update_slice(buffer, block, tuple(starts))


def take(array, index, dim=0):
    return lax.dynamic_slice_in_dim(array, index, 1, axis=dim)


def plane_bits(count):
    return [1 << b for b in range(1, count.bit_length() - 1)]


def line_swap(blocks, split=0, join=0):
    return lax.all_to_all(blocks, "seq", split, join, tiled=True)


def dot(left, right):
    return jnp.dot(left, right, preferred_element_type=jnp.float32)


def tie(*values):
    return lax.optimization_barrier(values)


def flip(values, bit):
    return lax.ppermute(values, "dp", xor_pairs(lax.axis_size("dp"), bit))


def two_by_two():
    return lax.axis_size("dp") == 8


def assemble(pieces, shapes, moves, places):
    count = len(pieces)

    def kernel(places_ref, *refs):
        given, results, semaphores = refs[:count], refs[count:-1], refs[-1]
        copies = []
        for number, (piece, source, result, target) in enumerate(moves):
            copy = pltpu.make_async_copy(
                given[piece].at[source(places_ref)],
                results[result].at[target(places_ref)],
                semaphores.at[number],
            )
            copy.start()
            copies.append(copy)
        for copy in copies:
            copy.wait()

    size = sum(2 * math.prod(shape) for shape in shapes)
    return pl.pallas_call(
        kernel,
        in_specs=[pl.BlockSpec(memory_space=pltpu.SMEM)]
        + [pl.BlockSpec(memory_space=pl.ANY)] * count,
        out_specs=[pl.BlockSpec(memory_space=pltpu.VMEM)] * len(shapes),
        out_shape=[jax.ShapeDtypeStruct(shape, jnp.bfloat16) for shape in shapes],
        scratch_shapes=[pltpu.SemaphoreType.DMA((len(moves),))],
        compiler_params=pltpu.CompilerParams(vmem_limit_bytes=48 * 1024 * 1024),
        cost_estimate=pl.CostEstimate(flops=0, bytes_accessed=2 * size, transcendentals=0),
    )(places, *pieces)


def everything(places):
    return slice(None)


def at(*index):
    return lambda places: index


def plane_open(values):
    if not two_by_two():
        return (values,)
    return (values, flip(values, 2), flip(values, 4))


def plane_relay(state):
    if not two_by_two():
        return state
    values, by_first, by_second = state
    half = values.shape[0] // 2
    return state + (flip(by_first[:half], 4), flip(by_second[half:], 2))


def plane_chips(state, chip=None):
    values = state[0]
    chips = lax.axis_size("dp") // 2
    if not two_by_two():
        same = values[None]
        for bit in plane_bits(2 * chips):
            same = jnp.concatenate([same, flip(same, bit)], axis=0)
        if chip is None:
            return same
        ordered = jnp.zeros(same.shape, same.dtype)
        for r in range(chips):
            ordered = place(ordered, same[r : r + 1], 0, chip ^ r)
        return ordered
    half = values.shape[0] // 2
    rest = values.shape[0] - half

    def target(r, *more):
        if chip is None:
            return at(r, *more)
        return lambda places: (places[0] ^ r,) + more

    moves = [(r, everything, 0, target(r)) for r in range(3)]
    moves.append((3, everything, 0, target(3, pl.ds(0, half))))
    moves.append((4, everything, 0, target(3, pl.ds(half, rest))))
    places = jnp.zeros((1,), jnp.int32) if chip is None else chip.reshape(1).astype(jnp.int32)
    return assemble(state, [(chips,) + values.shape], moves, places)[0]


def both_cores(same, other, core, rows):
    chips, line, _, width = same.shape
    if two_by_two() and all(count % 16 == 0 for count in rows):
        moves, start = [], 0
        for result, count in enumerate(rows):
            part = at(slice(None), slice(None), pl.ds(start, count))
            moves.append((0, part, result, lambda places: (slice(None), places[0])))
            moves.append((1, part, result, lambda places: (slice(None), 1 - places[0])))
            start += count
        return assemble(
            [same, other],
            [(chips, 2, line, count, width) for count in rows],
            moves,
            core.reshape(1).astype(jnp.int32),
        )
    full = jnp.zeros((chips, 2) + same.shape[1:], same.dtype)
    full = place(place(full, same[:, None], 1, core), other[:, None], 1, 1 - core)
    results, start = [], 0
    for count in rows:
        results.append(full[:, :, :, start : start + count])
        start += count
    return results


def plane_far(blocks):
    if not two_by_two():
        return None
    half = blocks[3].shape[0] // 2
    low = jnp.bfloat16
    return (flip(blocks[3][:half].astype(low), 2), flip(blocks[3][half:].astype(low), 4))


def plane_near(blocks, far):
    low, wide = jnp.bfloat16, jnp.float32
    if not two_by_two():
        total = jnp.stack([block.astype(wide) for block in blocks], axis=0)
        for bit in reversed(plane_bits(lax.axis_size("dp"))):
            middle = total.shape[0] // 2
            got = flip(total[middle:].astype(low), bit)
            total = total[:middle] + got.astype(wide)
        return (total[0],)
    half = blocks[3].shape[0] // 2
    to_first = jnp.concatenate(
        [
            blocks[1][:half].astype(low),
            (blocks[1][half:].astype(wide) + far[1].astype(wide)).astype(low),
        ],
        axis=0,
    )
    to_second = jnp.concatenate(
        [
            (blocks[2][:half].astype(wide) + far[0].astype(wide)).astype(low),
            blocks[2][half:].astype(low),
        ],
        axis=0,
    )
    return (blocks[0], flip(to_first, 2), flip(to_second, 4))


def plane_total(near):
    total = near[0].astype(jnp.float32)
    for got in near[1:]:
        total = total + got.astype(jnp.float32)
    return total


def spread_pairs(blocks, own_width):
    line, rows, _ = blocks.shape
    pair = 2 * HEAD_DIM

    def kernel(given, result):
        for source in range(line):
            for number in range(own_width // pair):
                for part in range(3):
                    start = part * D + source * own_width + number * pair
                    taken = (3 * number + part) * pair
                    result[:, start : start + pair] = given[
                        source, :, taken : taken + pair
                    ].astype(jnp.float32)

    return pl.pallas_call(
        kernel,
        out_shape=jax.ShapeDtypeStruct((rows, 3 * D), jnp.float32),
        cost_estimate=cost(1),
    )(blocks)


def whole_grad_kernel(places, *refs):
    lefts, rights, outs = refs[:8], refs[8:16], refs[16:]
    for weight in range(4):
        total = None
        for side in range(2):
            left, right = lefts[2 * weight + side], rights[2 * weight + side]
            half = left.shape[1] // 2
            rows = jnp.where(places[1] == 0, left[:, :half], left[:, half:])
            part = lax.dot_general(
                rows, right[...], (((0,), (0,)), ((), ())), preferred_element_type=jnp.float32
            )
            total = part if total is None else total + part
        out = outs[weight // 2]
        line, count = out.shape[1], out.shape[2] // 2
        start = weight % 2 * count
        for place_of in range(line):
            out[0, place_of, start : start + count, :] = total[
                place_of * count : (place_of + 1) * count
            ].astype(jnp.bfloat16)


def whole_grad_blocks(lefts, rights, chip, core):
    chips, line = lax.axis_size("dp") // 2, lax.axis_size("seq")
    shard = D // (2 * chips * line)
    if two_by_two() and shard % 16 == 0:
        width = 2 * line * shard

        def left_spec(array):
            return pl.BlockSpec((array.shape[0], width), lambda r, places: (0, places[0] ^ r))

        def right_spec(array):
            return pl.BlockSpec(
                array.shape, lambda r, places: (0, 0), pipeline_mode=pl.Buffered(1)
            )

        flat_lefts = [side for pair in lefts for side in pair]
        flat_rights = [side for pair in rights for side in pair]
        out_shape = (chips, line, 2 * shard, D)
        outs = pl.pallas_call(
            whole_grad_kernel,
            grid_spec=pltpu.PrefetchScalarGridSpec(
                num_scalar_prefetch=1,
                grid=(chips,),
                in_specs=[left_spec(array) for array in flat_lefts]
                + [right_spec(array) for array in flat_rights],
                out_specs=[
                    pl.BlockSpec((1,) + out_shape[1:], lambda r, places: (r, 0, 0, 0))
                    for _ in range(2)
                ],
            ),
            out_shape=[jax.ShapeDtypeStruct(out_shape, jnp.bfloat16) for _ in range(2)],
            compiler_params=KERNEL_PARAMS,
            cost_estimate=cost(0.1),
        )(jnp.stack([chip, core]).astype(jnp.int32), *flat_lefts, *flat_rights)
        return [[out[r] for r in range(chips)] for out in outs]
    grads = []
    for (left, left_other), (right, right_other) in zip(lefts, rights):
        grad = (dot(left.T, right) + dot(left_other.T, right_other)).astype(jnp.bfloat16)
        grads.append(take(grad.reshape(chips, 2, line, shard, D), core, 1)[:, 0])
    return [
        [jnp.concatenate([take(grad, chip ^ r)[0] for grad in group], axis=1) for r in range(chips)]
        for group in (grads[:2], grads[2:])
    ]


def on_device(
    latents,
    context,
    clip_bounds,
    timesteps,
    self_inward,
    self_outward,
    cross_query,
    cross_keyval,
    cross_return,
    time_weight,
    expand_weight,
    shrink_weight,
    gain_attend,
    gain_cross,
    gain_feed,
    cotangent,
):
    f32, bf16 = jnp.float32, jnp.bfloat16
    frame_count = latents.shape[1]
    dp_count = lax.axis_size("dp")
    seq_count = lax.axis_size("seq")
    dp_place = lax.axis_index("dp")
    seq_place = lax.axis_index("seq")
    row_length = frame_count * seq_count
    text_count = context.shape[1]
    own_heads = HEADS // seq_count
    pairs = (own_heads + 1) // 2
    own_width = own_heads * HEAD_DIM
    pair_width = 2 * HEAD_DIM
    padded = pairs * pair_width
    hidden_width = FF // dp_count
    shard = D // (dp_count * seq_count)
    time_shard = TFEAT // (dp_count * seq_count)
    place_all = dp_place * seq_count + seq_place
    chip_place, core_place = dp_place // 2, dp_place % 2
    chips = dp_count // 2

    all_frames = jnp.arange(row_length, dtype=jnp.int32)
    second_start, third_start = clip_bounds[0, 0], clip_bounds[0, 1]
    frame_clips = (all_frames >= second_start).astype(jnp.int32) + (
        all_frames >= third_start
    ).astype(jnp.int32)
    clip_starts = jnp.where(
        frame_clips == 0, 0, jnp.where(frame_clips == 1, second_start, third_start)
    )
    token_slots = jnp.arange(TOKEN_ROWS, dtype=jnp.int32)
    clips = jnp.concatenate(
        [frame_clips, jnp.where(token_slots < CLIPS, token_slots, -1)]
    ).astype(f32)
    positions = jnp.concatenate(
        [all_frames - clip_starts + 1, jnp.zeros(TOKEN_ROWS, jnp.int32)]
    ).astype(f32)
    cosine, sine = rotary_tables(positions)
    clip_column = clips[:, None]
    own_clips = lax.dynamic_slice_in_dim(clips, seq_place * frame_count, frame_count)
    text_clips = (jnp.arange(text_count, dtype=jnp.int32) // CTX_LEN).astype(f32)

    def by_pairs(blocks):
        blocks = jnp.pad(blocks, ((0, 0),) * 3 + ((0, padded - own_width),))
        return (
            blocks.reshape(seq_count, shard, 3, pairs, pair_width)
            .transpose(0, 1, 3, 2, 4)
            .reshape(seq_count, shard, 3 * padded)
        )

    def from_pairs(blocks):
        return (
            blocks.reshape(seq_count, shard, pairs, 3, pair_width)
            .transpose(0, 1, 3, 2, 4)
            .reshape(seq_count, shard, 3, padded)[..., :own_width]
        )

    inward_blocks = by_pairs(
        self_inward.reshape(shard, 3, seq_count, own_width).transpose(2, 0, 1, 3)
    )
    extra = jnp.concatenate([time_weight.reshape(-1), gain_attend, gain_cross, gain_feed])
    extra_rows = -(-extra.shape[0] // (16 * 3 * padded)) * 16
    extra = jnp.pad(extra, (0, extra_rows * 3 * padded - extra.shape[0]))
    extra = jnp.broadcast_to(
        extra.reshape(1, extra_rows, 3 * padded), (seq_count, extra_rows, 3 * padded)
    )
    inward_send = jnp.concatenate([inward_blocks, extra], axis=1)
    expand_blocks = (
        expand_weight.reshape(shard, 2, dp_count, hidden_width)
        .transpose(2, 0, 1, 3)
        .reshape(dp_count, shard, 2 * hidden_width)
    )

    spread_rows = jnp.arange(D, dtype=jnp.int32)[None, :]
    context_rows = jnp.arange(D // 2, dtype=jnp.int32)[:, None]
    group, within = context_rows // (shard // 2), context_rows % (shard // 2)
    spread_keys = (spread_rows == group * shard + within).astype(bf16)
    spread_values = (spread_rows == group * shard + shard // 2 + within).astype(bf16)
    stacked = jnp.concatenate(
        [
            latents[0],
            self_outward,
            cross_query,
            cross_keyval[:, :D],
            cross_keyval[:, D:],
            cross_return,
        ],
        axis=0,
    )
    lined = lax.all_gather(stacked, "seq")
    inward_columns = line_swap(inward_send)
    context_spread = jnp.concatenate(
        [dot(context[0], spread_keys).astype(bf16), dot(context[0], spread_values).astype(bf16)],
        axis=0,
    )
    inward_columns, cotangent, expand_blocks, context_spread, cosine, sine = tie(
        inward_columns, cotangent, expand_blocks, context_spread, cosine, sine
    )

    inward_state = plane_open(inward_columns)
    cotangent_state = plane_open(cotangent[0])
    expand_part = lax.all_to_all(expand_blocks, "dp", 0, 0, tiled=True)
    inward_state, cotangent_state = tie(inward_state, cotangent_state)

    inward_state = plane_relay(inward_state)
    cotangent_state = plane_relay(cotangent_state)
    inward_same = plane_chips(inward_state, chip_place)
    inward_same, cotangent_state, expand_part = tie(inward_same, cotangent_state, expand_part)

    inward_other = flip(inward_same, 1)
    cotangent_same = plane_chips(cotangent_state)
    inward_other, cotangent_same = tie(inward_other, cotangent_same)

    inward_own, extra_all = both_cores(
        inward_same, inward_other, core_place, [shard, extra_rows]
    )
    inward_own = inward_own.reshape(D, 3 * padded)
    extra_all = extra_all.reshape(dp_count, seq_count, extra_rows * 3 * padded)
    time_full = extra_all[:, :, : time_shard * D].reshape(TFEAT, D)
    gains_all = extra_all[:, :, time_shard * D : time_shard * D + 3 * shard]
    gains_all = gains_all.reshape(dp_count, seq_count, 3, shard).astype(f32)
    attend_gain = gains_all[:, :, 0].reshape(D)
    cross_gain = gains_all[:, :, 1].reshape(D)
    feed_gain = gains_all[:, :, 2].reshape(D)
    feats_low = time_features(timesteps[0]).astype(bf16)
    token = dot(feats_low, time_full)
    token_norm, token_inverse = norm_forward(token)
    token_low = jnp.pad(
        (token_norm * attend_gain).astype(bf16), ((0, TOKEN_ROWS - CLIPS), (0, 0))
    )
    joined = two_by_two() and 2 * hidden_width == D and shard % 16 == 0
    early_parts = dp_count // 4 if joined else 0
    ffn_early = shrink_weight
    if joined:
        ffn_early = jnp.concatenate(
            [shrink_weight, expand_part[:early_parts].reshape(early_parts * shard, D)], axis=0
        )
    ffn_early = lax.all_gather(ffn_early, "seq")
    cotangent_other = flip(cotangent_same, 1)
    cotangent_other, inward_own, token_low, lined, cross_gain, feed_gain = tie(
        cotangent_other, inward_own, token_low, lined, cross_gain, feed_gain
    )

    def weight_rows(first, count):
        start = frame_count + first * shard
        return lined[:, start : start + count * shard]

    first_state = plane_open(weight_rows(0, 2))
    row_latents = lined[:, :frame_count].reshape(row_length, D)
    row_norm, row_inverse = norm_forward(row_latents.astype(f32))
    row_low = jnp.concatenate([(row_norm * attend_gain).astype(bf16), token_low], axis=0)
    projected = dot(row_low, inward_own)
    projected, first_state, lined = tie(projected, first_state, lined)

    first_state = plane_relay(first_state)
    second_state = plane_open(weight_rows(2, 2))
    attended, attended_wide, self_level, projected_low = self_forward(
        projected, cosine, sine, clip_column, row_length
    )
    attended, first_state, second_state, ffn_early = tie(
        attended, first_state, second_state, ffn_early
    )

    attended_low = line_swap(attended[:, :own_width], 0, 1)
    first_same = plane_chips(first_state, chip_place)
    first_other = flip(first_same, 1)
    second_state = plane_relay(second_state)
    attended_low, first_same, first_other, second_state, expand_part = tie(
        attended_low, first_same, first_other, second_state, expand_part
    )

    expand_lined = lax.all_gather(expand_part[early_parts:], "seq")
    outward_full, query_full = [
        weight.reshape(D, D)
        for weight in both_cores(first_same, first_other, core_place, [shard] * 2)
    ]
    second_same = plane_chips(second_state, chip_place)
    second_other = flip(second_same, 1)
    context_other = flip(context_spread, 1)
    after_self = latents[0].astype(f32) + dot(attended_low, outward_full)
    norm_two, inverse_two = norm_forward(after_self)
    normed_two = (norm_two * cross_gain).astype(bf16)
    cross_heads = dot(normed_two, query_full).astype(bf16)
    attended_other = flip(attended_low, 1)
    cross_heads, second_same, second_other, attended_other, context_other = tie(
        cross_heads, second_same, second_other, attended_other, context_other
    )

    keyval_full, return_full = [
        weight.reshape(D, D)
        for weight in both_cores(second_same, second_other, core_place, [shard] * 2)
    ]
    keyval = dot(context_spread, keyval_full).astype(bf16)
    crossed, crossed_wide, cross_level = cross_forward(
        cross_heads, keyval, own_clips[:, None], text_clips[:, None]
    )
    normed_two_other = flip(normed_two, 1)
    crossed, return_full, normed_two_other = tie(crossed, return_full, normed_two_other)

    after_cross = after_self + dot(crossed, return_full)
    norm_three, inverse_three = norm_forward(after_cross)
    normed_three = (norm_three * feed_gain).astype(bf16)
    crossed_other = flip(crossed, 1)
    frames_state = plane_relay(plane_open(normed_three))
    frames_same = plane_chips(frames_state)
    frames_same, expand_lined, crossed_other = tie(frames_same, expand_lined, crossed_other)

    if joined:
        moves = [(0, at(slice(None), pl.ds(0, hidden_width // seq_count)), 1, everything)]
        for line in range(seq_count):
            target = at(pl.ds(early_parts, dp_count - early_parts), line)
            moves.append((1, at(line), 0, target))
            for part in range(early_parts):
                rows = pl.ds(hidden_width // seq_count + part * shard, shard)
                moves.append((0, at(line, rows), 0, at(part, line)))
        expand_own, shrink_own = assemble(
            [ffn_early, expand_lined],
            [
                (dp_count, seq_count, shard, 2 * hidden_width),
                (seq_count, hidden_width // seq_count, D),
            ],
            moves,
            jnp.zeros((1,), jnp.int32),
        )
    else:
        expand_own, shrink_own = expand_lined.transpose(1, 0, 2, 3), ffn_early
    shrink_own = shrink_own.reshape(hidden_width, D)
    expand_own = expand_own.reshape(D, 2 * hidden_width)
    half_frames = chips * frame_count
    frames_other = flip(frames_same, 1)
    frames = [frames_same.reshape(half_frames, D), frames_other.reshape(half_frames, D)]
    tangents = [cotangent_same.reshape(half_frames, D), cotangent_other.reshape(half_frames, D)]
    hidden_low, expand_low = [], []
    for side in range(2):
        gate_up = dot(frames[side], expand_own)
        gate_part = gate_up[:, :hidden_width]
        upward = gate_up[:, hidden_width:]
        hidden_low.append((jax.nn.silu(gate_part) * upward).astype(bf16))
        hidden_grad = dot(tangents[side], shrink_own.T)
        expand_low.append(gated_back(hidden_grad, gate_part, upward))

    def sides(array):
        return array.astype(bf16).reshape(chips, frame_count, D)

    shrink_part = (
        dot(hidden_low[0].T, tangents[0]) + dot(hidden_low[1].T, tangents[1])
    ).astype(bf16)
    shrink_part, hidden_low, expand_low = tie(shrink_part, hidden_low, expand_low)
    grad_shrink = lax.psum_scatter(shrink_part, "seq", scatter_dimension=0, tiled=True)
    feed_other = sides(dot(expand_low[1], expand_own.T))
    feed_got = flip(feed_other, 1)
    feed_same = sides(dot(expand_low[0], expand_own.T))
    feed_same, feed_got, hidden_low, expand_low = tie(feed_same, feed_got, hidden_low, expand_low)
    feed_blocks = [feed_same[r].astype(f32) + feed_got[r].astype(f32) for r in range(chips)]
    feed_far = plane_far(feed_blocks)
    fed_other = sides(dot(hidden_low[1], shrink_own))
    fed_got = flip(fed_other, 1)
    fed_same = sides(dot(hidden_low[0], shrink_own))
    feed_far, fed_got, fed_same, expand_low = tie(feed_far, fed_got, fed_same, expand_low)

    feed_near = plane_near(feed_blocks, feed_far)
    expand_grad = (dot(frames[0].T, expand_low[0]) + dot(frames[1].T, expand_low[1])).astype(bf16)
    expand_grad = expand_grad.reshape(dp_count, seq_count, shard, 2 * hidden_width)
    expand_grad = expand_grad.transpose(1, 0, 2, 3).reshape(D, 2 * hidden_width)
    feed_near, expand_grad = tie(feed_near, expand_grad)
    expand_sum = lax.psum_scatter(expand_grad, "seq", scatter_dimension=0, tiled=True)
    expand_sum = expand_sum.reshape(dp_count, shard, 2 * hidden_width)

    def open_grad(grad):
        grad = grad.astype(bf16).reshape(chips, 2, seq_count, shard, -1)
        return grad, flip(take(grad, 1 - core_place, 1), 1)

    def side_block(opened, r):
        return jnp.concatenate(
            [
                (
                    take(take(grad, core_place, 1), chip_place ^ r)[0, 0].astype(f32)
                    + take(got, chip_place ^ r)[0, 0].astype(f32)
                ).astype(bf16)
                for grad, got in opened
            ],
            axis=1,
        )

    def side_blocks(opened):
        return [side_block(opened, r) for r in range(chips)]

    feed_norm_grad = plane_total(feed_near)
    feed_term, feed_gain_part = norm_backward(
        feed_norm_grad, norm_three, inverse_three, feed_gain
    )
    after_cross_grad = cotangent[0].astype(f32) + feed_term
    return_low = after_cross_grad.astype(bf16)
    crossed_grad = dot(return_low, return_full.T).astype(bf16)
    return_other = flip(return_low, 1)
    crossed_grad, return_low, return_other, grad_shrink = tie(
        crossed_grad, return_low, return_other, grad_shrink
    )
    cross_query_low, cross_key_low, cross_value_low = cross_backward(
        cross_heads,
        keyval,
        crossed_grad,
        crossed_wide,
        cross_level,
        own_clips[:, None],
        text_clips[:, None],
    )
    cross_query_low, cross_key_low, cross_value_low = tie(
        cross_query_low, cross_key_low, cross_value_low
    )
    cross_norm_grad = dot(cross_query_low, query_full.T)
    cross_term, cross_gain_part = norm_backward(
        cross_norm_grad, norm_two, inverse_two, cross_gain
    )
    after_self_grad = after_cross_grad + cross_term
    outward_low = after_self_grad.astype(bf16)
    attended_grad = dot(outward_low, outward_full.T).astype(bf16)
    keyval_low = jnp.concatenate([cross_key_low, cross_value_low], axis=0)
    keyval_low_other = flip(keyval_low, 1)
    cross_query_other = flip(cross_query_low, 1)
    queries_in, returns_in = (cross_query_low, cross_query_other), (return_low, return_other)
    attended_grad, outward_low, keyval_low, keyval_low_other, queries_in, returns_in = tie(
        attended_grad, outward_low, keyval_low, keyval_low_other, queries_in, returns_in
    )

    attended_grad_own = line_swap(attended_grad, 1, 0)
    outward_other = flip(outward_low, 1)
    halves = whole_grad_blocks(
        [(crossed, crossed_other), (context_spread, context_other)]
        + [(normed_two, normed_two_other), (attended_low, attended_other)],
        [returns_in, (keyval_low, keyval_low_other), queries_in, (outward_low, outward_other)],
        chip_place,
        core_place,
    )
    attended_grad_own, halves = tie(attended_grad_own, halves)
    half_far = [plane_far(blocks) for blocks in halves]

    attended_grad_own = jnp.pad(attended_grad_own, ((0, 0), (0, padded - own_width)))
    inward_low = self_backward(
        projected_low,
        attended_grad_own,
        attended_wide,
        self_level,
        cosine,
        sine,
        clip_column,
    )
    attend_parts = dot(inward_low, inward_own.T)
    attend_low = attend_parts[:row_length].astype(bf16)
    inward_low, attend_parts, attend_low, halves, half_far, expand_sum = tie(
        inward_low, attend_parts, attend_low, halves, half_far, expand_sum
    )

    near_early = plane_near(halves[0], half_far[0])
    attend_sum = lax.psum_scatter(attend_low, "seq", scatter_dimension=0, tiled=True)
    near_late = plane_near(halves[1], half_far[1])
    inward_grad = open_grad(dot(row_low.T, inward_low))
    inward_grad, attend_parts, near_early, near_late = tie(
        inward_grad, attend_parts, near_early, near_late
    )

    whole_column = jnp.concatenate(
        [plane_total(near_early).astype(bf16), plane_total(near_late).astype(bf16)], axis=1
    )
    whole_sums = lax.psum_scatter(whole_column, "seq", scatter_dimension=0)
    expand_rows = lax.all_to_all(expand_sum, "dp", 0, 0, tiled=True)
    inward_blocks = side_blocks([inward_grad])
    inward_far = plane_far(inward_blocks)
    token_term, token_gain_part = norm_backward(
        attend_parts[row_length : row_length + CLIPS], token_norm, token_inverse, attend_gain
    )
    attend_gain_part = jnp.sum(attend_parts[:row_length] * row_norm, axis=0) + token_gain_part
    feats_row = feats_low.astype(f32).reshape(-1)
    device_count = dp_count * seq_count
    gain_parts = jnp.stack([attend_gain_part, cross_gain_part, feed_gain_part], axis=0)
    gain_parts = gain_parts.reshape(3, device_count, shard).transpose(1, 0, 2)
    common = jnp.concatenate([token_term.reshape(-1), feats_row]).astype(bf16)
    small = jnp.concatenate(
        [
            jnp.broadcast_to(common[None], (device_count,) + common.shape),
            gain_parts.reshape(device_count, 3 * shard).astype(bf16),
        ],
        axis=1,
    )
    small = jnp.pad(small, ((0, 0), (0, -small.shape[1] % 2048)))
    small = small.reshape(device_count, -1, 128)
    inward_far, fed_got, fed_same, small, expand_rows = tie(
        inward_far, fed_got, fed_same, small, expand_rows
    )

    inward_near = plane_near(inward_blocks, inward_far)
    fed_blocks = [fed_same[r].astype(f32) + fed_got[r].astype(f32) for r in range(chips)]
    fed_far = plane_far(fed_blocks)
    inward_near, fed_far = tie(inward_near, fed_far)

    inward_rows = line_swap(plane_total(inward_near).astype(bf16))
    fed_near = plane_near(fed_blocks, fed_far)
    grad_expand = (
        expand_rows.reshape(dp_count, shard, 2, hidden_width)
        .transpose(1, 2, 0, 3)
        .reshape(shard, 2 * FF)
        .astype(f32)
    )
    inward_rows, fed_near, grad_expand, attend_sum, small = tie(
        inward_rows, fed_near, grad_expand, attend_sum, small
    )

    small_all = lax.all_to_all(small, ("dp", "seq"), 0, 0, tiled=True).astype(f32)
    block_output = (after_cross + plane_total(fed_near)).astype(bf16)
    own_norm = lax.dynamic_slice_in_dim(row_norm, seq_place * frame_count, frame_count, axis=0)
    own_inverse = lax.dynamic_slice_in_dim(
        row_inverse, seq_place * frame_count, frame_count, axis=0
    )
    attend_term, _ = norm_backward(
        attend_sum.astype(f32), own_norm, own_inverse, attend_gain
    )
    latents_grad = (after_self_grad + attend_term)[None]
    grad_shrink = grad_shrink.astype(f32)
    if own_width % pair_width == 0:
        grad_inward = spread_pairs(inward_rows, own_width)
    else:
        grad_inward = (
            from_pairs(inward_rows).transpose(1, 2, 0, 3).reshape(shard, 3 * D).astype(f32)
        )
    grad_inward, block_output, latents_grad, whole_sums = tie(
        grad_inward, block_output, latents_grad, whole_sums
    )
    whole_sums = whole_sums.astype(f32)
    grad_return = whole_sums[:shard]
    grad_keyval = jnp.concatenate(
        [whole_sums[shard : shard + shard // 2], whole_sums[shard + shard // 2 : 2 * shard]],
        axis=1,
    )
    grad_query = whole_sums[2 * shard : 3 * shard]
    grad_outward = whole_sums[3 * shard :]
    small_all = small_all.reshape(device_count, -1)
    token_count, feats_count = CLIPS * D, CLIPS * TFEAT
    token_sum = jnp.sum(
        small_all[:, :token_count].reshape(dp_count, seq_count, CLIPS, D), axis=1
    )
    feats_all = small_all.reshape(dp_count, seq_count, -1)[:, 0]
    feats_all = feats_all[:, token_count : token_count + feats_count]
    feats_all = feats_all.reshape(dp_count, CLIPS, TFEAT)
    feats_own = lax.dynamic_slice_in_dim(feats_all, place_all * time_shard, time_shard, axis=2)
    grad_time = jnp.einsum(
        "rct,rcn->tn",
        feats_own,
        token_sum,
        precision=PRECISE,
        preferred_element_type=f32,
    )
    gain_start = token_count + feats_count
    gain_sums = jnp.sum(small_all[:, gain_start : gain_start + 3 * shard], axis=0)
    gain_sums = gain_sums.reshape(3, shard)
    return (
        block_output[None],
        latents_grad,
        grad_inward,
        grad_outward,
        grad_query,
        grad_keyval,
        grad_return,
        grad_time,
        grad_expand,
        grad_shrink,
        gain_sums[0],
        gain_sums[1],
        gain_sums[2],
    )


def solution(mesh):
    return jax.shard_map(
        on_device,
        mesh=mesh,
        in_specs=(
            P("dp", "seq", None),
            P("dp", None, None),
            P("dp", None),
            P("dp", None),
            P(("dp", "seq"), None),
            P(("dp", "seq"), None),
            P(("dp", "seq"), None),
            P(("dp", "seq"), None),
            P(("dp", "seq"), None),
            P(("dp", "seq"), None),
            P(("dp", "seq"), None),
            P(("dp", "seq"), None),
            P(("dp", "seq")),
            P(("dp", "seq")),
            P(("dp", "seq")),
            P("dp", "seq", None),
        ),
        out_specs=(
            P("dp", "seq", None),
            P("dp", "seq", None),
            P(("dp", "seq"), None),
            P(("dp", "seq"), None),
            P(("dp", "seq"), None),
            P(("dp", "seq"), None),
            P(("dp", "seq"), None),
            P(("dp", "seq"), None),
            P(("dp", "seq"), None),
            P(("dp", "seq"), None),
            P(("dp", "seq")),
            P(("dp", "seq")),
            P(("dp", "seq")),
        ),
        check_vma=False,
    )
```

```python
import math

import jax
import jax.numpy as jnp
from jax import lax
from jax.experimental import pallas as pl
from jax.experimental.pallas import tpu as pltpu
from jax.sharding import PartitionSpec as P

D = 1536
HEADS = 24
HEAD_DIM = 64
FF = 6144
CTX_LEN = 128
TFEAT = 256
CLIPS = 3
TOKEN_ROWS = 128


EPSILON = 1e-05
SCORE_SCALE = 0.125
MASKED = -1e30
PRECISE = lax.Precision.HIGHEST


def contract_last(left, right):
    return lax.dot_general(left, right, (((1,), (1,)), ((), ())), preferred_element_type=jnp.float32)


def contract(left, right):
    return lax.dot_general(left, right, (((1,), (0,)), ((), ())), preferred_element_type=jnp.float32)


def lane_of(width=2 * HEAD_DIM):
    return lax.broadcasted_iota(jnp.int32, (1, width), 1)


def clip_features(clips):
    slot = (lane_of() % HEAD_DIM).astype(jnp.float32)
    used = slot < CLIPS + 1
    of_query = jnp.where(used & (slot != clips), MASKED, 0.0)
    of_key = jnp.where(used & (slot == jnp.where(clips < 0, float(CLIPS), clips)), 1.0, 0.0)
    return of_query.astype(jnp.bfloat16), of_key.astype(jnp.bfloat16)


def attend_rows(query, query_clips, key_pair, value_pair):
    first = lane_of() < HEAD_DIM
    outs, tops = [], []
    for head in range(2):
        mine = first if head == 0 else jnp.logical_not(first)
        scores = contract_last(jnp.where(mine, query, query_clips), key_pair[head])
        top = jnp.max(scores, axis=1, keepdims=True)
        weights = jnp.exp(scores - top).astype(jnp.bfloat16)
        mixed = contract(weights, value_pair[head])
        place_sum = HEAD_DIM if head == 0 else 0
        total = mixed[:, place_sum : place_sum + 1]
        outs.append(mixed / total)
        tops.append(top + jnp.log(total))
    mixture = jnp.where(first, outs[0], outs[1])
    return mixture, jnp.where(first, tops[0], tops[1])


def value_with_ones(values):
    first = lane_of() < HEAD_DIM
    one = jnp.ones((), values.dtype)
    return jnp.where(first, values, one), jnp.where(first, one, values)


def key_with_clips(keys, key_clips):
    first = lane_of() < HEAD_DIM
    return jnp.where(first, keys, key_clips), jnp.where(first, key_clips, keys)


def attend_rows_back(query, query_clips, key_pair, keys_turned, values, grads, mixture, level):
    first = lane_of() < HEAD_DIM
    zero = jnp.zeros((), query.dtype)
    product = jnp.transpose(grads.astype(jnp.float32) * mixture)
    level_turned = jnp.transpose(level)
    head_rows = lax.broadcasted_iota(jnp.int32, (2 * HEAD_DIM, 1), 0) < HEAD_DIM
    parts = []
    for head in range(2):
        mine = first if head == 0 else jnp.logical_not(first)
        low, high = head * HEAD_DIM, (head + 1) * HEAD_DIM
        query_own = jnp.where(mine, query, zero)
        grads_own = jnp.where(mine, grads, zero)
        scores = contract_last(key_pair[head], jnp.where(mine, query, query_clips))
        weights = jnp.exp(scores - level_turned[low : low + 1])
        grad_weights = contract_last(values, grads_own)
        diagonal = jnp.sum(product[low:high], axis=0, keepdims=True)
        grad_scores = (weights * (grad_weights - diagonal)).astype(jnp.bfloat16)
        key_grad = contract(grad_scores, query_own)
        value_grad = contract(weights.astype(jnp.bfloat16), grads_own)
        parts.append((contract(keys_turned, grad_scores), key_grad, value_grad))
    query_turned = jnp.where(head_rows, parts[0][0], parts[1][0])
    return query_turned, parts[0][1] + parts[1][1], parts[0][2] + parts[1][2]


def swap_halves(values):
    quarter = HEAD_DIM // 2
    down = pltpu.roll(values, 2 * HEAD_DIM - quarter, 1)
    up = pltpu.roll(values, quarter, 1)
    return jnp.where(lane_of() % HEAD_DIM < quarter, down, up)


def self_forward_kernel(
    projected, cosine, sine, clip_column, mixed, mixed_wide, level, low, key_pair, value_pair
):
    rows = mixed.shape[0]
    pair = 2 * HEAD_DIM
    block = min(256, rows)
    for part, scale in ((0, SCORE_SCALE), (1, 1.0)):
        values = projected[:, part * pair : (part + 1) * pair]
        turned = values * cosine[...] + swap_halves(values) * sine[...]
        low[:, part * pair : (part + 1) * pair] = turned.astype(jnp.bfloat16) * jnp.bfloat16(scale)
    values = projected[:, 2 * pair : 3 * pair].astype(jnp.bfloat16)
    low[:, 2 * pair : 3 * pair] = values
    value_pair[0], value_pair[1] = value_with_ones(values)
    _, key_clips = clip_features(clip_column[...])
    key_pair[0], key_pair[1] = key_with_clips(low[:, pair : 2 * pair], key_clips)

    def step(index, carry):
        place = pl.ds(pl.multiple_of(index * block, block), block)
        query_clips, _ = clip_features(clip_column[place, :])
        mixture, tops = attend_rows(
            low[place, 0:pair],
            query_clips,
            (key_pair[0], key_pair[1]),
            (value_pair[0], value_pair[1]),
        )
        mixed[place, :] = mixture.astype(jnp.bfloat16)
        mixed_wide[place, :] = mixture
        level[place, :] = tops
        return carry

    lax.fori_loop(0, rows // block, step, 0, unroll=True)


def self_backward_kernel(
    low, grads, mixed_wide, level, cosine, sine, clip_column, out, key_pair, keys_turned, totals
):
    rows = grads.shape[0]
    pair = 2 * HEAD_DIM
    block = min(256, rows)
    keys_turned[...] = jnp.transpose(low[:, pair : 2 * pair])
    _, key_clips = clip_features(clip_column[...])
    key_pair[0], key_pair[1] = key_with_clips(low[:, pair : 2 * pair], key_clips)
    totals[...] = jnp.zeros_like(totals)
    out[rows:, 0:pair] = jnp.zeros((out.shape[0] - rows, pair), jnp.bfloat16)

    def step(index, carry):
        start = pl.multiple_of(index * block, block)
        place = pl.ds(start, block)
        query_clips, _ = clip_features(clip_column[place, :])
        query_turned, key_grad, value_grad = attend_rows_back(
            low[place, 0:pair],
            query_clips,
            (key_pair[0], key_pair[1]),
            keys_turned[...],
            low[:, 2 * pair : 3 * pair],
            grads[place, :],
            mixed_wide[place, :],
            level[place, :],
        )
        query_grad = jnp.transpose(query_turned) * SCORE_SCALE
        back = query_grad * cosine[place, :] - swap_halves(query_grad) * sine[place, :]
        out[place, 0:pair] = back.astype(jnp.bfloat16)
        totals[0] += key_grad
        totals[1] += value_grad
        return carry

    lax.fori_loop(0, rows // block, step, 0, unroll=True)
    key_grad = totals[0]
    back = key_grad * cosine[...] - swap_halves(key_grad) * sine[...]
    out[:, pair : 2 * pair] = back.astype(jnp.bfloat16)
    out[:, 2 * pair : 3 * pair] = totals[1].astype(jnp.bfloat16)


def cross_forward_kernel(query, keys, values, clip_column, text_column, mixed, mixed_wide, level):
    pair = 2 * HEAD_DIM
    query_clips, _ = clip_features(clip_column[...])
    _, key_clips = clip_features(text_column[...])
    for start in range(0, query.shape[1], pair):
        part = slice(start, start + pair)
        mixture, tops = attend_rows(
            query[:, part] * jnp.bfloat16(SCORE_SCALE),
            query_clips,
            key_with_clips(keys[:, part], key_clips),
            value_with_ones(values[:, part]),
        )
        mixed[:, part] = mixture.astype(jnp.bfloat16)
        mixed_wide[:, part] = mixture
        level[:, part] = tops


def cross_backward_kernel(
    query, keys, values, grads, mixed_wide, level, clip_column, text_column, query_out, key_out, value_out
):
    pair = 2 * HEAD_DIM
    query_clips, _ = clip_features(clip_column[...])
    _, key_clips = clip_features(text_column[...])
    for start in range(0, query.shape[1], pair):
        part = slice(start, start + pair)
        query_turned, key_grad, value_grad = attend_rows_back(
            query[:, part] * jnp.bfloat16(SCORE_SCALE),
            query_clips,
            key_with_clips(keys[:, part], key_clips),
            jnp.transpose(keys[:, part]),
            values[:, part],
            grads[:, part],
            mixed_wide[:, part],
            level[:, part],
        )
        query_out[:, part] = (jnp.transpose(query_turned) * SCORE_SCALE).astype(jnp.bfloat16)
        key_out[:, part] = key_grad.astype(jnp.bfloat16)
        value_out[:, part] = value_grad.astype(jnp.bfloat16)


def whole(array):
    return pl.BlockSpec(array.shape, lambda p: (0,) * array.ndim)


def lanes(rows, width=2 * HEAD_DIM, second=False):
    return pl.BlockSpec((rows, width), lambda p: (1 if second else 0, p))


CROSS_PAIRS = 3
KERNEL_PARAMS = pltpu.CompilerParams(
    dimension_semantics=("arbitrary",), vmem_limit_bytes=48 * 1024 * 1024
)


def cost(microseconds):
    return pl.CostEstimate(
        flops=int(microseconds * 1e9), bytes_accessed=2**20, transcendentals=0
    )


def self_forward(projected, cosine, sine, clip_column, rows):
    total, width = projected.shape
    pair = 2 * HEAD_DIM
    pairs = width // (3 * pair)
    return pl.pallas_call(
        self_forward_kernel,
        grid=(pairs,),
        in_specs=[
            lanes(total, 3 * pair),
            whole(cosine),
            whole(sine),
            whole(clip_column),
        ],
        out_specs=[lanes(rows), lanes(rows), lanes(rows), lanes(total, 3 * pair)],
        out_shape=[
            jax.ShapeDtypeStruct((rows, pairs * pair), jnp.bfloat16),
            jax.ShapeDtypeStruct((rows, pairs * pair), jnp.float32),
            jax.ShapeDtypeStruct((rows, pairs * pair), jnp.float32),
            jax.ShapeDtypeStruct((total, width), jnp.bfloat16),
        ],
        scratch_shapes=[
            pltpu.VMEM((2, total, pair), jnp.bfloat16),
            pltpu.VMEM((2, total, pair), jnp.bfloat16),
        ],
        compiler_params=KERNEL_PARAMS,
        cost_estimate=cost(120),
    )(projected, cosine, sine, clip_column)


def self_backward(low, grads, mixed_wide, level, cosine, sine, clip_column):
    total, width = low.shape
    rows = grads.shape[0]
    pair = 2 * HEAD_DIM
    pairs = width // (3 * pair)
    return pl.pallas_call(
        self_backward_kernel,
        grid=(pairs,),
        in_specs=[
            lanes(total, 3 * pair),
            lanes(rows),
            lanes(rows),
            lanes(rows),
            whole(cosine),
            whole(sine),
            whole(clip_column),
        ],
        out_specs=lanes(total, 3 * pair),
        out_shape=jax.ShapeDtypeStruct((total, width), jnp.bfloat16),
        scratch_shapes=[
            pltpu.VMEM((2, total, pair), jnp.bfloat16),
            pltpu.VMEM((pair, total), jnp.bfloat16),
            pltpu.VMEM((2, total, pair), jnp.float32),
        ],
        compiler_params=KERNEL_PARAMS,
        cost_estimate=cost(2),
    )(low, grads, mixed_wide, level, cosine, sine, clip_column)


def cross_forward(query, keyval, clip_column, text_column):
    rows, width = query.shape
    keys = keyval.shape[0] // 2
    group = 2 * HEAD_DIM * CROSS_PAIRS
    steps = width // group
    return pl.pallas_call(
        cross_forward_kernel,
        grid=(steps,),
        in_specs=[
            lanes(rows, group),
            lanes(keys, group),
            lanes(keys, group, second=True),
            whole(clip_column),
            whole(text_column),
        ],
        out_specs=[lanes(rows, group), lanes(rows, group), lanes(rows, group)],
        out_shape=[
            jax.ShapeDtypeStruct((rows, width), jnp.bfloat16),
            jax.ShapeDtypeStruct((rows, width), jnp.float32),
            jax.ShapeDtypeStruct((rows, width), jnp.float32),
        ],
        compiler_params=KERNEL_PARAMS,
        cost_estimate=cost(20),
    )(query, keyval, keyval, clip_column, text_column)


def cross_backward(query, keyval, grads, mixed_wide, level, clip_column, text_column):
    rows, width = query.shape
    keys = keyval.shape[0] // 2
    group = 2 * HEAD_DIM * CROSS_PAIRS
    steps = width // group
    return pl.pallas_call(
        cross_backward_kernel,
        grid=(steps,),
        in_specs=[
            lanes(rows, group),
            lanes(keys, group),
            lanes(keys, group, second=True),
            lanes(rows, group),
            lanes(rows, group),
            lanes(rows, group),
            whole(clip_column),
            whole(text_column),
        ],
        out_specs=[lanes(rows, group), lanes(keys, group), lanes(keys, group)],
        out_shape=[
            jax.ShapeDtypeStruct((rows, width), jnp.bfloat16),
            jax.ShapeDtypeStruct((keys, width), jnp.bfloat16),
            jax.ShapeDtypeStruct((keys, width), jnp.bfloat16),
        ],
        compiler_params=KERNEL_PARAMS,
        cost_estimate=cost(120),
    )(query, keyval, keyval, grads, mixed_wide, level, clip_column, text_column)


def norm_forward(hidden):
    centre = jnp.mean(hidden, axis=-1, keepdims=True)
    centred = hidden - centre
    spread = jnp.mean(centred * centred, axis=-1, keepdims=True)
    scale_inv = lax.rsqrt(spread + EPSILON)
    return (centred * scale_inv, scale_inv)


def norm_backward(grad_norm, normalized, scale_inv, gain_vector):
    scaled = grad_norm * gain_vector
    gain_grad = jnp.sum(grad_norm * normalized, axis=0)
    inner = (
        scaled
        - jnp.mean(scaled, axis=-1, keepdims=True)
        - normalized * jnp.mean(scaled * normalized, axis=-1, keepdims=True)
    )
    return (scale_inv * inner, gain_grad)


def rotary_tables(positions):
    half_width = HEAD_DIM // 2
    frequencies = jnp.exp(
        -math.log(10000.0) * jnp.arange(half_width, dtype=jnp.float32) / half_width
    )
    angles = positions[:, None] * frequencies
    cosine, sine = jnp.cos(angles), jnp.sin(angles)
    return (
        jnp.concatenate([cosine, cosine, cosine, cosine], axis=1),
        jnp.concatenate([-sine, sine, -sine, sine], axis=1),
    )


def time_features(step_values):
    half_width = TFEAT // 2
    frequencies = jnp.exp(
        -math.log(10000.0) * jnp.arange(half_width, dtype=jnp.float32) / half_width
    )
    angles = step_values.astype(jnp.float32)[..., None] * frequencies
    return jnp.concatenate([jnp.cos(angles), jnp.sin(angles)], axis=-1)


def gated_back(hidden_grad, gate_part, upward):
    gate_sigmoid = jax.nn.sigmoid(gate_part)
    gate_grad = hidden_grad * upward * gate_sigmoid * (1.0 + gate_part * (1.0 - gate_sigmoid))
    upward_grad = hidden_grad * gate_part * gate_sigmoid
    return jnp.concatenate([gate_grad, upward_grad], axis=-1).astype(jnp.bfloat16)


def xor_pairs(count, bit):
    return [(k, k ^ bit) for k in range(count)]


def place(buffer, block, dim, index):
    starts = [0] * buffer.ndim
    starts[dim] = index
    return lax.dynamic_update_slice(buffer, block, tuple(starts))


def take(array, index, dim=0):
    return lax.dynamic_slice_in_dim(array, index, 1, axis=dim)


def plane_bits(count):
    return [1 << b for b in range(1, count.bit_length() - 1)]


def line_swap(blocks, split=0, join=0):
    return lax.all_to_all(blocks, "seq", split, join, tiled=True)


def dot(left, right):
    return jnp.dot(left, right, preferred_element_type=jnp.float32)


def tie(*values):
    return lax.optimization_barrier(values)


def flip(values, bit):
    return lax.ppermute(values, "dp", xor_pairs(lax.axis_size("dp"), bit))


def two_by_two():
    return lax.axis_size("dp") == 8


def assemble(pieces, shapes, moves, places):
    count = len(pieces)

    def kernel(places_ref, *refs):
        given, results, semaphores = refs[:count], refs[count:-1], refs[-1]
        copies = []
        for number, (piece, source, result, target) in enumerate(moves):
            copy = pltpu.make_async_copy(
                given[piece].at[source(places_ref)],
                results[result].at[target(places_ref)],
                semaphores.at[number],
            )
            copy.start()
            copies.append(copy)
        for copy in copies:
            copy.wait()

    size = sum(2 * math.prod(shape) for shape in shapes)
    return pl.pallas_call(
        kernel,
        in_specs=[pl.BlockSpec(memory_space=pltpu.SMEM)]
        + [pl.BlockSpec(memory_space=pl.ANY)] * count,
        out_specs=[pl.BlockSpec(memory_space=pltpu.VMEM)] * len(shapes),
        out_shape=[jax.ShapeDtypeStruct(shape, jnp.bfloat16) for shape in shapes],
        scratch_shapes=[pltpu.SemaphoreType.DMA((len(moves),))],
        compiler_params=pltpu.CompilerParams(vmem_limit_bytes=48 * 1024 * 1024),
        cost_estimate=pl.CostEstimate(flops=0, bytes_accessed=2 * size, transcendentals=0),
    )(places, *pieces)


def everything(places):
    return slice(None)


def at(*index):
    return lambda places: index


def plane_open(values):
    if not two_by_two():
        return (values,)
    return (values, flip(values, 2), flip(values, 4))


def plane_relay(state):
    if not two_by_two():
        return state
    values, by_first, by_second = state
    half = values.shape[0] // 2
    return state + (flip(by_first[:half], 4), flip(by_second[half:], 2))


def plane_chips(state, chip=None):
    values = state[0]
    chips = lax.axis_size("dp") // 2
    if not two_by_two():
        same = values[None]
        for bit in plane_bits(2 * chips):
            same = jnp.concatenate([same, flip(same, bit)], axis=0)
        if chip is None:
            return same
        ordered = jnp.zeros(same.shape, same.dtype)
        for r in range(chips):
            ordered = place(ordered, same[r : r + 1], 0, chip ^ r)
        return ordered
    half = values.shape[0] // 2
    rest = values.shape[0] - half

    def target(r, *more):
        if chip is None:
            return at(r, *more)
        return lambda places: (places[0] ^ r,) + more

    moves = [(r, everything, 0, target(r)) for r in range(3)]
    moves.append((3, everything, 0, target(3, pl.ds(0, half))))
    moves.append((4, everything, 0, target(3, pl.ds(half, rest))))
    places = jnp.zeros((1,), jnp.int32) if chip is None else chip.reshape(1).astype(jnp.int32)
    return assemble(state, [(chips,) + values.shape], moves, places)[0]


def both_cores(same, other, core, rows):
    chips, line, _, width = same.shape
    if two_by_two() and all(count % 16 == 0 for count in rows):
        moves, start = [], 0
        for result, count in enumerate(rows):
            part = at(slice(None), slice(None), pl.ds(start, count))
            moves.append((0, part, result, lambda places: (slice(None), places[0])))
            moves.append((1, part, result, lambda places: (slice(None), 1 - places[0])))
            start += count
        return assemble(
            [same, other],
            [(chips, 2, line, count, width) for count in rows],
            moves,
            core.reshape(1).astype(jnp.int32),
        )
    full = jnp.zeros((chips, 2) + same.shape[1:], same.dtype)
    full = place(place(full, same[:, None], 1, core), other[:, None], 1, 1 - core)
    results, start = [], 0
    for count in rows:
        results.append(full[:, :, :, start : start + count])
        start += count
    return results


def plane_far(blocks):
    if not two_by_two():
        return None
    half = blocks[3].shape[0] // 2
    low = jnp.bfloat16
    return (flip(blocks[3][:half].astype(low), 2), flip(blocks[3][half:].astype(low), 4))


def plane_near(blocks, far):
    low, wide = jnp.bfloat16, jnp.float32
    if not two_by_two():
        total = jnp.stack([block.astype(wide) for block in blocks], axis=0)
        for bit in reversed(plane_bits(lax.axis_size("dp"))):
            middle = total.shape[0] // 2
            got = flip(total[middle:].astype(low), bit)
            total = total[:middle] + got.astype(wide)
        return (total[0],)
    half = blocks[3].shape[0] // 2
    to_first = jnp.concatenate(
        [
            blocks[1][:half].astype(low),
            (blocks[1][half:].astype(wide) + far[1].astype(wide)).astype(low),
        ],
        axis=0,
    )
    to_second = jnp.concatenate(
        [
            (blocks[2][:half].astype(wide) + far[0].astype(wide)).astype(low),
            blocks[2][half:].astype(low),
        ],
        axis=0,
    )
    return (blocks[0], flip(to_first, 2), flip(to_second, 4))


def plane_total(near):
    total = near[0].astype(jnp.float32)
    for got in near[1:]:
        total = total + got.astype(jnp.float32)
    return total


def spread_pairs(blocks, own_width):
    line, rows, _ = blocks.shape
    pair = 2 * HEAD_DIM

    def kernel(given, result):
        for source in range(line):
            for number in range(own_width // pair):
                for part in range(3):
                    start = part * D + source * own_width + number * pair
                    taken = (3 * number + part) * pair
                    result[:, start : start + pair] = given[
                        source, :, taken : taken + pair
                    ].astype(jnp.float32)

    return pl.pallas_call(
        kernel,
        out_shape=jax.ShapeDtypeStruct((rows, 3 * D), jnp.float32),
        cost_estimate=cost(1),
    )(blocks)


def whole_grad_kernel(places, *refs):
    lefts, rights, outs = refs[:8], refs[8:16], refs[16:]
    for weight in range(4):
        total = None
        for side in range(2):
            left, right = lefts[2 * weight + side], rights[2 * weight + side]
            half = left.shape[1] // 2
            rows = jnp.where(places[1] == 0, left[:, :half], left[:, half:])
            part = lax.dot_general(
                rows, right[...], (((0,), (0,)), ((), ())), preferred_element_type=jnp.float32
            )
            total = part if total is None else total + part
        out = outs[weight // 2]
        line, count = out.shape[1], out.shape[2] // 2
        start = weight % 2 * count
        for place_of in range(line):
            out[0, place_of, start : start + count, :] = total[
                place_of * count : (place_of + 1) * count
            ].astype(jnp.bfloat16)


def whole_grad_blocks(lefts, rights, chip, core):
    chips, line = lax.axis_size("dp") // 2, lax.axis_size("seq")
    shard = D // (2 * chips * line)
    if two_by_two() and shard % 16 == 0:
        width = 2 * line * shard

        def left_spec(array):
            return pl.BlockSpec((array.shape[0], width), lambda r, places: (0, places[0] ^ r))

        def right_spec(array):
            return pl.BlockSpec(
                array.shape, lambda r, places: (0, 0), pipeline_mode=pl.Buffered(1)
            )

        flat_lefts = [side for pair in lefts for side in pair]
        flat_rights = [side for pair in rights for side in pair]
        out_shape = (chips, line, 2 * shard, D)
        outs = pl.pallas_call(
            whole_grad_kernel,
            grid_spec=pltpu.PrefetchScalarGridSpec(
                num_scalar_prefetch=1,
                grid=(chips,),
                in_specs=[left_spec(array) for array in flat_lefts]
                + [right_spec(array) for array in flat_rights],
                out_specs=[
                    pl.BlockSpec((1,) + out_shape[1:], lambda r, places: (r, 0, 0, 0))
                    for _ in range(2)
                ],
            ),
            out_shape=[jax.ShapeDtypeStruct(out_shape, jnp.bfloat16) for _ in range(2)],
            compiler_params=KERNEL_PARAMS,
            cost_estimate=cost(0.1),
        )(jnp.stack([chip, core]).astype(jnp.int32), *flat_lefts, *flat_rights)
        return [[out[r] for r in range(chips)] for out in outs]
    grads = []
    for (left, left_other), (right, right_other) in zip(lefts, rights):
        grad = (dot(left.T, right) + dot(left_other.T, right_other)).astype(jnp.bfloat16)
        grads.append(take(grad.reshape(chips, 2, line, shard, D), core, 1)[:, 0])
    return [
        [jnp.concatenate([take(grad, chip ^ r)[0] for grad in group], axis=1) for r in range(chips)]
        for group in (grads[:2], grads[2:])
    ]


def on_device(
    latents,
    context,
    clip_bounds,
    timesteps,
    self_inward,
    self_outward,
    cross_query,
    cross_keyval,
    cross_return,
    time_weight,
    expand_weight,
    shrink_weight,
    gain_attend,
    gain_cross,
    gain_feed,
    cotangent,
):
    f32, bf16 = jnp.float32, jnp.bfloat16
    frame_count = latents.shape[1]
    dp_count = lax.axis_size("dp")
    seq_count = lax.axis_size("seq")
    dp_place = lax.axis_index("dp")
    seq_place = lax.axis_index("seq")
    row_length = frame_count * seq_count
    text_count = context.shape[1]
    own_heads = HEADS // seq_count
    pairs = (own_heads + 1) // 2
    own_width = own_heads * HEAD_DIM
    pair_width = 2 * HEAD_DIM
    padded = pairs * pair_width
    hidden_width = FF // dp_count
    shard = D // (dp_count * seq_count)
    time_shard = TFEAT // (dp_count * seq_count)
    place_all = dp_place * seq_count + seq_place
    chip_place, core_place = dp_place // 2, dp_place % 2
    chips = dp_count // 2

    all_frames = jnp.arange(row_length, dtype=jnp.int32)
    second_start, third_start = clip_bounds[0, 0], clip_bounds[0, 1]
    frame_clips = (all_frames >= second_start).astype(jnp.int32) + (
        all_frames >= third_start
    ).astype(jnp.int32)
    clip_starts = jnp.where(
        frame_clips == 0, 0, jnp.where(frame_clips == 1, second_start, third_start)
    )
    token_slots = jnp.arange(TOKEN_ROWS, dtype=jnp.int32)
    clips = jnp.concatenate(
        [frame_clips, jnp.where(token_slots < CLIPS, token_slots, -1)]
    ).astype(f32)
    positions = jnp.concatenate(
        [all_frames - clip_starts + 1, jnp.zeros(TOKEN_ROWS, jnp.int32)]
    ).astype(f32)
    cosine, sine = rotary_tables(positions)
    clip_column = clips[:, None]
    own_clips = lax.dynamic_slice_in_dim(clips, seq_place * frame_count, frame_count)
    text_clips = (jnp.arange(text_count, dtype=jnp.int32) // CTX_LEN).astype(f32)

    def by_pairs(blocks):
        blocks = jnp.pad(blocks, ((0, 0),) * 3 + ((0, padded - own_width),))
        return (
            blocks.reshape(seq_count, shard, 3, pairs, pair_width)
            .transpose(0, 1, 3, 2, 4)
            .reshape(seq_count, shard, 3 * padded)
        )

    def from_pairs(blocks):
        return (
            blocks.reshape(seq_count, shard, pairs, 3, pair_width)
            .transpose(0, 1, 3, 2, 4)
            .reshape(seq_count, shard, 3, padded)[..., :own_width]
        )

    inward_blocks = by_pairs(
        self_inward.reshape(shard, 3, seq_count, own_width).transpose(2, 0, 1, 3)
    )
    extra = jnp.concatenate([time_weight.reshape(-1), gain_attend, gain_cross, gain_feed])
    extra_rows = -(-extra.shape[0] // (16 * 3 * padded)) * 16
    extra = jnp.pad(extra, (0, extra_rows * 3 * padded - extra.shape[0]))
    extra = jnp.broadcast_to(
        extra.reshape(1, extra_rows, 3 * padded), (seq_count, extra_rows, 3 * padded)
    )
    inward_send = jnp.concatenate([inward_blocks, extra], axis=1)
    expand_blocks = (
        expand_weight.reshape(shard, 2, dp_count, hidden_width)
        .transpose(2, 0, 1, 3)
        .reshape(dp_count, shard, 2 * hidden_width)
    )

    spread_rows = jnp.arange(D, dtype=jnp.int32)[None, :]
    context_rows = jnp.arange(D // 2, dtype=jnp.int32)[:, None]
    group, within = context_rows // (shard // 2), context_rows % (shard // 2)
    spread_keys = (spread_rows == group * shard + within).astype(bf16)
    spread_values = (spread_rows == group * shard + shard // 2 + within).astype(bf16)
    stacked = jnp.concatenate(
        [
            latents[0],
            self_outward,
            cross_query,
            cross_keyval[:, :D],
            cross_keyval[:, D:],
            cross_return,
        ],
        axis=0,
    )
    lined = lax.all_gather(stacked, "seq")
    inward_columns = line_swap(inward_send)
    context_spread = jnp.concatenate(
        [dot(context[0], spread_keys).astype(bf16), dot(context[0], spread_values).astype(bf16)],
        axis=0,
    )
    inward_columns, cotangent, expand_blocks, context_spread, cosine, sine = tie(
        inward_columns, cotangent, expand_blocks, context_spread, cosine, sine
    )

    inward_state = plane_open(inward_columns)
    cotangent_state = plane_open(cotangent[0])
    expand_part = lax.all_to_all(expand_blocks, "dp", 0, 0, tiled=True)
    inward_state, cotangent_state = tie(inward_state, cotangent_state)

    inward_state = plane_relay(inward_state)
    cotangent_state = plane_relay(cotangent_state)
    inward_same = plane_chips(inward_state, chip_place)
    inward_same, cotangent_state, expand_part = tie(inward_same, cotangent_state, expand_part)

    inward_other = flip(inward_same, 1)
    cotangent_same = plane_chips(cotangent_state)
    inward_other, cotangent_same = tie(inward_other, cotangent_same)

    inward_own, extra_all = both_cores(
        inward_same, inward_other, core_place, [shard, extra_rows]
    )
    inward_own = inward_own.reshape(D, 3 * padded)
    extra_all = extra_all.reshape(dp_count, seq_count, extra_rows * 3 * padded)
    time_full = extra_all[:, :, : time_shard * D].reshape(TFEAT, D)
    gains_all = extra_all[:, :, time_shard * D : time_shard * D + 3 * shard]
    gains_all = gains_all.reshape(dp_count, seq_count, 3, shard).astype(f32)
    attend_gain = gains_all[:, :, 0].reshape(D)
    cross_gain = gains_all[:, :, 1].reshape(D)
    feed_gain = gains_all[:, :, 2].reshape(D)
    feats_low = time_features(timesteps[0]).astype(bf16)
    token = dot(feats_low, time_full)
    token_norm, token_inverse = norm_forward(token)
    token_low = jnp.pad(
        (token_norm * attend_gain).astype(bf16), ((0, TOKEN_ROWS - CLIPS), (0, 0))
    )
    joined = two_by_two() and 2 * hidden_width == D and shard % 16 == 0
    early_parts = dp_count // 4 if joined else 0
    ffn_early = shrink_weight
    if joined:
        ffn_early = jnp.concatenate(
            [shrink_weight, expand_part[:early_parts].reshape(early_parts * shard, D)], axis=0
        )
    ffn_early = lax.all_gather(ffn_early, "seq")
    cotangent_other = flip(cotangent_same, 1)
    cotangent_other, inward_own, token_low, lined, cross_gain, feed_gain = tie(
        cotangent_other, inward_own, token_low, lined, cross_gain, feed_gain
    )

    def weight_rows(first, count):
        start = frame_count + first * shard
        return lined[:, start : start + count * shard]

    first_state = plane_open(weight_rows(0, 2))
    row_latents = lined[:, :frame_count].reshape(row_length, D)
    row_norm, row_inverse = norm_forward(row_latents.astype(f32))
    row_low = jnp.concatenate([(row_norm * attend_gain).astype(bf16), token_low], axis=0)
    projected = dot(row_low, inward_own)
    projected, first_state, lined = tie(projected, first_state, lined)

    first_state = plane_relay(first_state)
    second_state = plane_open(weight_rows(2, 2))
    attended, attended_wide, self_level, projected_low = self_forward(
        projected, cosine, sine, clip_column, row_length
    )
    attended, first_state, second_state, ffn_early = tie(
        attended, first_state, second_state, ffn_early
    )

    attended_low = line_swap(attended[:, :own_width], 0, 1)
    first_same = plane_chips(first_state, chip_place)
    first_other = flip(first_same, 1)
    second_state = plane_relay(second_state)
    attended_low, first_same, first_other, second_state, expand_part = tie(
        attended_low, first_same, first_other, second_state, expand_part
    )

    expand_lined = lax.all_gather(expand_part[early_parts:], "seq")
    outward_full, query_full = [
        weight.reshape(D, D)
        for weight in both_cores(first_same, first_other, core_place, [shard] * 2)
    ]
    second_same = plane_chips(second_state, chip_place)
    second_other = flip(second_same, 1)
    context_other = flip(context_spread, 1)
    after_self = latents[0].astype(f32) + dot(attended_low, outward_full)
    norm_two, inverse_two = norm_forward(after_self)
    normed_two = (norm_two * cross_gain).astype(bf16)
    cross_heads = dot(normed_two, query_full).astype(bf16)
    attended_other = flip(attended_low, 1)
    cross_heads, second_same, second_other, attended_other, context_other = tie(
        cross_heads, second_same, second_other, attended_other, context_other
    )

    keyval_full, return_full = [
        weight.reshape(D, D)
        for weight in both_cores(second_same, second_other, core_place, [shard] * 2)
    ]
    keyval = dot(context_spread, keyval_full).astype(bf16)
    crossed, crossed_wide, cross_level = cross_forward(
        cross_heads, keyval, own_clips[:, None], text_clips[:, None]
    )
    normed_two_other = flip(normed_two, 1)
    crossed, return_full, normed_two_other = tie(crossed, return_full, normed_two_other)

    after_cross = after_self + dot(crossed, return_full)
    norm_three, inverse_three = norm_forward(after_cross)
    normed_three = (norm_three * feed_gain).astype(bf16)
    crossed_other = flip(crossed, 1)
    frames_state = plane_relay(plane_open(normed_three))
    frames_same = plane_chips(frames_state)
    frames_same, expand_lined, crossed_other = tie(frames_same, expand_lined, crossed_other)

    if joined:
        moves = [(0, at(slice(None), pl.ds(0, hidden_width // seq_count)), 1, everything)]
        for line in range(seq_count):
            target = at(pl.ds(early_parts, dp_count - early_parts), line)
            moves.append((1, at(line), 0, target))
            for part in range(early_parts):
                rows = pl.ds(hidden_width // seq_count + part * shard, shard)
                moves.append((0, at(line, rows), 0, at(part, line)))
        expand_own, shrink_own = assemble(
            [ffn_early, expand_lined],
            [
                (dp_count, seq_count, shard, 2 * hidden_width),
                (seq_count, hidden_width // seq_count, D),
            ],
            moves,
            jnp.zeros((1,), jnp.int32),
        )
    else:
        expand_own, shrink_own = expand_lined.transpose(1, 0, 2, 3), ffn_early
    shrink_own = shrink_own.reshape(hidden_width, D)
    expand_own = expand_own.reshape(D, 2 * hidden_width)
    half_frames = chips * frame_count
    frames_other = flip(frames_same, 1)
    frames = [frames_same.reshape(half_frames, D), frames_other.reshape(half_frames, D)]
    tangents = [cotangent_same.reshape(half_frames, D), cotangent_other.reshape(half_frames, D)]
    hidden_low, expand_low = [], []
    for side in range(2):
        gate_up = dot(frames[side], expand_own)
        gate_part = gate_up[:, :hidden_width]
        upward = gate_up[:, hidden_width:]
        hidden_low.append((jax.nn.silu(gate_part) * upward).astype(bf16))
        hidden_grad = dot(tangents[side], shrink_own.T)
        expand_low.append(gated_back(hidden_grad, gate_part, upward))

    def sides(array):
        return array.astype(bf16).reshape(chips, frame_count, D)

    shrink_part = (
        dot(hidden_low[0].T, tangents[0]) + dot(hidden_low[1].T, tangents[1])
    ).astype(bf16)
    shrink_part, hidden_low, expand_low = tie(shrink_part, hidden_low, expand_low)
    grad_shrink = lax.psum_scatter(shrink_part, "seq", scatter_dimension=0, tiled=True)
    feed_other = sides(dot(expand_low[1], expand_own.T))
    feed_got = flip(feed_other, 1)
    feed_same = sides(dot(expand_low[0], expand_own.T))
    feed_same, feed_got, hidden_low, expand_low = tie(feed_same, feed_got, hidden_low, expand_low)
    feed_blocks = [feed_same[r].astype(f32) + feed_got[r].astype(f32) for r in range(chips)]
    feed_far = plane_far(feed_blocks)
    fed_other = sides(dot(hidden_low[1], shrink_own))
    fed_got = flip(fed_other, 1)
    fed_same = sides(dot(hidden_low[0], shrink_own))
    feed_far, fed_got, fed_same, expand_low = tie(feed_far, fed_got, fed_same, expand_low)

    feed_near = plane_near(feed_blocks, feed_far)
    expand_grad = (dot(frames[0].T, expand_low[0]) + dot(frames[1].T, expand_low[1])).astype(bf16)
    expand_grad = expand_grad.reshape(dp_count, seq_count, shard, 2 * hidden_width)
    expand_grad = expand_grad.transpose(1, 0, 2, 3).reshape(D, 2 * hidden_width)
    feed_near, expand_grad = tie(feed_near, expand_grad)
    expand_sum = lax.psum_scatter(expand_grad, "seq", scatter_dimension=0, tiled=True)
    expand_sum = expand_sum.reshape(dp_count, shard, 2 * hidden_width)

    def open_grad(grad):
        grad = grad.astype(bf16).reshape(chips, 2, seq_count, shard, -1)
        return grad, flip(take(grad, 1 - core_place, 1), 1)

    def side_block(opened, r):
        return jnp.concatenate(
            [
                (
                    take(take(grad, core_place, 1), chip_place ^ r)[0, 0].astype(f32)
                    + take(got, chip_place ^ r)[0, 0].astype(f32)
                ).astype(bf16)
                for grad, got in opened
            ],
            axis=1,
        )

    def side_blocks(opened):
        return [side_block(opened, r) for r in range(chips)]

    feed_norm_grad = plane_total(feed_near)
    feed_term, feed_gain_part = norm_backward(
        feed_norm_grad, norm_three, inverse_three, feed_gain
    )
    after_cross_grad = cotangent[0].astype(f32) + feed_term
    return_low = after_cross_grad.astype(bf16)
    crossed_grad = dot(return_low, return_full.T).astype(bf16)
    return_other = flip(return_low, 1)
    crossed_grad, return_low, return_other, grad_shrink = tie(
        crossed_grad, return_low, return_other, grad_shrink
    )
    cross_query_low, cross_key_low, cross_value_low = cross_backward(
        cross_heads,
        keyval,
        crossed_grad,
        crossed_wide,
        cross_level,
        own_clips[:, None],
        text_clips[:, None],
    )
    cross_query_low, cross_key_low, cross_value_low = tie(
        cross_query_low, cross_key_low, cross_value_low
    )
    cross_norm_grad = dot(cross_query_low, query_full.T)
    cross_term, cross_gain_part = norm_backward(
        cross_norm_grad, norm_two, inverse_two, cross_gain
    )
    after_self_grad = after_cross_grad + cross_term
    outward_low = after_self_grad.astype(bf16)
    attended_grad = dot(outward_low, outward_full.T).astype(bf16)
    keyval_low = jnp.concatenate([cross_key_low, cross_value_low], axis=0)
    keyval_low_other = flip(keyval_low, 1)
    cross_query_other = flip(cross_query_low, 1)
    queries_in, returns_in = (cross_query_low, cross_query_other), (return_low, return_other)
    attended_grad, outward_low, keyval_low, keyval_low_other, queries_in, returns_in = tie(
        attended_grad, outward_low, keyval_low, keyval_low_other, queries_in, returns_in
    )

    attended_grad_own = line_swap(attended_grad, 1, 0)
    outward_other = flip(outward_low, 1)
    halves = whole_grad_blocks(
        [(crossed, crossed_other), (context_spread, context_other)]
        + [(normed_two, normed_two_other), (attended_low, attended_other)],
        [returns_in, (keyval_low, keyval_low_other), queries_in, (outward_low, outward_other)],
        chip_place,
        core_place,
    )
    attended_grad_own, halves = tie(attended_grad_own, halves)
    half_far = [plane_far(blocks) for blocks in halves]

    attended_grad_own = jnp.pad(attended_grad_own, ((0, 0), (0, padded - own_width)))
    inward_low = self_backward(
        projected_low,
        attended_grad_own,
        attended_wide,
        self_level,
        cosine,
        sine,
        clip_column,
    )
    attend_parts = dot(inward_low, inward_own.T)
    attend_low = attend_parts[:row_length].astype(bf16)
    attend_sum = lax.psum_scatter(attend_low, "seq", scatter_dimension=0, tiled=True)
    inward_low, attend_parts, halves, half_far, expand_sum = tie(
        inward_low, attend_parts, halves, half_far, expand_sum
    )

    near_early = plane_near(halves[0], half_far[0])
    near_late = plane_near(halves[1], half_far[1])
    inward_grad = open_grad(dot(row_low.T, inward_low))
    token_term, token_gain_part = norm_backward(
        attend_parts[row_length : row_length + CLIPS], token_norm, token_inverse, attend_gain
    )
    attend_gain_part = jnp.sum(attend_parts[:row_length] * row_norm, axis=0) + token_gain_part
    feats_row = feats_low.astype(f32).reshape(-1)
    device_count = dp_count * seq_count
    gain_parts = jnp.stack([attend_gain_part, cross_gain_part, feed_gain_part], axis=0)
    gain_parts = gain_parts.reshape(3, device_count, shard).transpose(1, 0, 2)
    common = jnp.concatenate([token_term.reshape(-1), feats_row]).astype(bf16)
    small = jnp.concatenate(
        [
            jnp.broadcast_to(common[None], (device_count,) + common.shape),
            gain_parts.reshape(device_count, 3 * shard).astype(bf16),
        ],
        axis=1,
    )
    small = jnp.pad(small, ((0, 0), (0, -small.shape[1] % 2048)))
    small = small.reshape(device_count, -1, 128)
    inward_grad, small, near_early, near_late, attend_sum = tie(
        inward_grad, small, near_early, near_late, attend_sum
    )

    whole_column = jnp.concatenate(
        [plane_total(near_early).astype(bf16), plane_total(near_late).astype(bf16)], axis=1
    )
    whole_sums = lax.psum_scatter(whole_column, "seq", scatter_dimension=0)
    expand_rows = lax.all_to_all(expand_sum, "dp", 0, 0, tiled=True)
    inward_blocks = side_blocks([inward_grad])
    inward_far = plane_far(inward_blocks)
    inward_blocks, inward_far, small, expand_rows = tie(
        inward_blocks, inward_far, small, expand_rows
    )

    inward_near = plane_near(inward_blocks, inward_far)
    small_all = lax.all_to_all(small, ("dp", "seq"), 0, 0, tiled=True).astype(f32)
    fed_blocks = [fed_same[r].astype(f32) + fed_got[r].astype(f32) for r in range(chips)]
    fed_far = plane_far(fed_blocks)
    inward_near, small_all, fed_far, attend_sum = tie(
        inward_near, small_all, fed_far, attend_sum
    )

    inward_rows = line_swap(plane_total(inward_near).astype(bf16))
    fed_near = plane_near(fed_blocks, fed_far)
    grad_expand = (
        expand_rows.reshape(dp_count, shard, 2, hidden_width)
        .transpose(1, 2, 0, 3)
        .reshape(shard, 2 * FF)
        .astype(f32)
    )
    inward_rows, fed_near, grad_expand, whole_sums = tie(
        inward_rows, fed_near, grad_expand, whole_sums
    )

    block_output = (after_cross + plane_total(fed_near)).astype(bf16)
    own_norm = lax.dynamic_slice_in_dim(row_norm, seq_place * frame_count, frame_count, axis=0)
    own_inverse = lax.dynamic_slice_in_dim(
        row_inverse, seq_place * frame_count, frame_count, axis=0
    )
    attend_term, _ = norm_backward(
        attend_sum.astype(f32), own_norm, own_inverse, attend_gain
    )
    latents_grad = (after_self_grad + attend_term)[None]
    grad_shrink = grad_shrink.astype(f32)
    if own_width % pair_width == 0:
        grad_inward = spread_pairs(inward_rows, own_width)
    else:
        grad_inward = (
            from_pairs(inward_rows).transpose(1, 2, 0, 3).reshape(shard, 3 * D).astype(f32)
        )
    grad_inward, block_output, latents_grad, whole_sums = tie(
        grad_inward, block_output, latents_grad, whole_sums
    )
    whole_sums = whole_sums.astype(f32)
    grad_return = whole_sums[:shard]
    grad_keyval = jnp.concatenate(
        [whole_sums[shard : shard + shard // 2], whole_sums[shard + shard // 2 : 2 * shard]],
        axis=1,
    )
    grad_query = whole_sums[2 * shard : 3 * shard]
    grad_outward = whole_sums[3 * shard :]
    small_all = small_all.reshape(device_count, -1)
    token_count, feats_count = CLIPS * D, CLIPS * TFEAT
    token_sum = jnp.sum(
        small_all[:, :token_count].reshape(dp_count, seq_count, CLIPS, D), axis=1
    )
    feats_all = small_all.reshape(dp_count, seq_count, -1)[:, 0]
    feats_all = feats_all[:, token_count : token_count + feats_count]
    feats_all = feats_all.reshape(dp_count, CLIPS, TFEAT)
    feats_own = lax.dynamic_slice_in_dim(feats_all, place_all * time_shard, time_shard, axis=2)
    grad_time = jnp.einsum(
        "rct,rcn->tn",
        feats_own,
        token_sum,
        precision=PRECISE,
        preferred_element_type=f32,
    )
    gain_start = token_count + feats_count
    gain_sums = jnp.sum(small_all[:, gain_start : gain_start + 3 * shard], axis=0)
    gain_sums = gain_sums.reshape(3, shard)
    return (
        block_output[None],
        latents_grad,
        grad_inward,
        grad_outward,
        grad_query,
        grad_keyval,
        grad_return,
        grad_time,
        grad_expand,
        grad_shrink,
        gain_sums[0],
        gain_sums[1],
        gain_sums[2],
    )


def solution(mesh):
    return jax.shard_map(
        on_device,
        mesh=mesh,
        in_specs=(
            P("dp", "seq", None),
            P("dp", None, None),
            P("dp", None),
            P("dp", None),
            P(("dp", "seq"), None),
            P(("dp", "seq"), None),
            P(("dp", "seq"), None),
            P(("dp", "seq"), None),
            P(("dp", "seq"), None),
            P(("dp", "seq"), None),
            P(("dp", "seq"), None),
            P(("dp", "seq"), None),
            P(("dp", "seq")),
            P(("dp", "seq")),
            P(("dp", "seq")),
            P("dp", "seq", None),
        ),
        out_specs=(
            P("dp", "seq", None),
            P("dp", "seq", None),
            P(("dp", "seq"), None),
            P(("dp", "seq"), None),
            P(("dp", "seq"), None),
            P(("dp", "seq"), None),
            P(("dp", "seq"), None),
            P(("dp", "seq"), None),
            P(("dp", "seq"), None),
            P(("dp", "seq"), None),
            P(("dp", "seq")),
            P(("dp", "seq")),
            P(("dp", "seq")),
        ),
        check_vma=False,
    )
```

```python
import math

import jax
import jax.numpy as jnp
from jax import lax
from jax.experimental import pallas as pl
from jax.experimental.pallas import tpu as pltpu
from jax.sharding import PartitionSpec as P

D = 1536
HEADS = 24
HEAD_DIM = 64
FF = 6144
CTX_LEN = 128
TFEAT = 256
CLIPS = 3
TOKEN_ROWS = 128


EPSILON = 1e-05
SCORE_SCALE = 0.125
MASKED = -1e30
PRECISE = lax.Precision.HIGHEST


def contract_last(left, right):
    return lax.dot_general(left, right, (((1,), (1,)), ((), ())), preferred_element_type=jnp.float32)


def contract(left, right):
    return lax.dot_general(left, right, (((1,), (0,)), ((), ())), preferred_element_type=jnp.float32)


def lane_of(width=2 * HEAD_DIM):
    return lax.broadcasted_iota(jnp.int32, (1, width), 1)


def clip_features(clips):
    slot = (lane_of() % HEAD_DIM).astype(jnp.float32)
    used = slot < CLIPS + 1
    of_query = jnp.where(used & (slot != clips), MASKED, 0.0)
    of_key = jnp.where(used & (slot == jnp.where(clips < 0, float(CLIPS), clips)), 1.0, 0.0)
    return of_query.astype(jnp.bfloat16), of_key.astype(jnp.bfloat16)


def attend_rows(query, query_clips, key_pair, value_pair):
    first = lane_of() < HEAD_DIM
    outs, tops = [], []
    for head in range(2):
        mine = first if head == 0 else jnp.logical_not(first)
        scores = contract_last(jnp.where(mine, query, query_clips), key_pair[head])
        top = jnp.max(scores, axis=1, keepdims=True)
        weights = jnp.exp(scores - top).astype(jnp.bfloat16)
        mixed = contract(weights, value_pair[head])
        place_sum = HEAD_DIM if head == 0 else 0
        total = mixed[:, place_sum : place_sum + 1]
        outs.append(mixed / total)
        tops.append(top + jnp.log(total))
    mixture = jnp.where(first, outs[0], outs[1])
    return mixture, jnp.where(first, tops[0], tops[1])


def value_with_ones(values):
    first = lane_of() < HEAD_DIM
    one = jnp.ones((), values.dtype)
    return jnp.where(first, values, one), jnp.where(first, one, values)


def key_with_clips(keys, key_clips):
    first = lane_of() < HEAD_DIM
    return jnp.where(first, keys, key_clips), jnp.where(first, key_clips, keys)


def attend_rows_back(query, query_clips, key_pair, keys_turned, values, grads, mixture, level):
    first = lane_of() < HEAD_DIM
    zero = jnp.zeros((), query.dtype)
    product = jnp.transpose(grads.astype(jnp.float32) * mixture)
    level_turned = jnp.transpose(level)
    head_rows = lax.broadcasted_iota(jnp.int32, (2 * HEAD_DIM, 1), 0) < HEAD_DIM
    parts = []
    for head in range(2):
        mine = first if head == 0 else jnp.logical_not(first)
        low, high = head * HEAD_DIM, (head + 1) * HEAD_DIM
        query_own = jnp.where(mine, query, zero)
        grads_own = jnp.where(mine, grads, zero)
        scores = contract_last(key_pair[head], jnp.where(mine, query, query_clips))
        weights = jnp.exp(scores - level_turned[low : low + 1])
        grad_weights = contract_last(values, grads_own)
        diagonal = jnp.sum(product[low:high], axis=0, keepdims=True)
        grad_scores = (weights * (grad_weights - diagonal)).astype(jnp.bfloat16)
        key_grad = contract(grad_scores, query_own)
        value_grad = contract(weights.astype(jnp.bfloat16), grads_own)
        parts.append((contract(keys_turned, grad_scores), key_grad, value_grad))
    query_turned = jnp.where(head_rows, parts[0][0], parts[1][0])
    return query_turned, parts[0][1] + parts[1][1], parts[0][2] + parts[1][2]


def swap_halves(values):
    quarter = HEAD_DIM // 2
    down = pltpu.roll(values, 2 * HEAD_DIM - quarter, 1)
    up = pltpu.roll(values, quarter, 1)
    return jnp.where(lane_of() % HEAD_DIM < quarter, down, up)


def self_forward_kernel(
    projected, cosine, sine, clip_column, mixed, mixed_wide, level, low, key_pair, value_pair
):
    rows = mixed.shape[0]
    pair = 2 * HEAD_DIM
    block = min(256, rows)
    for part, scale in ((0, SCORE_SCALE), (1, 1.0)):
        values = projected[:, part * pair : (part + 1) * pair]
        turned = values * cosine[...] + swap_halves(values) * sine[...]
        low[:, part * pair : (part + 1) * pair] = turned.astype(jnp.bfloat16) * jnp.bfloat16(scale)
    values = projected[:, 2 * pair : 3 * pair].astype(jnp.bfloat16)
    low[:, 2 * pair : 3 * pair] = values
    value_pair[0], value_pair[1] = value_with_ones(values)
    _, key_clips = clip_features(clip_column[...])
    key_pair[0], key_pair[1] = key_with_clips(low[:, pair : 2 * pair], key_clips)

    def step(index, carry):
        place = pl.ds(pl.multiple_of(index * block, block), block)
        query_clips, _ = clip_features(clip_column[place, :])
        mixture, tops = attend_rows(
            low[place, 0:pair],
            query_clips,
            (key_pair[0], key_pair[1]),
            (value_pair[0], value_pair[1]),
        )
        mixed[place, :] = mixture.astype(jnp.bfloat16)
        mixed_wide[place, :] = mixture
        level[place, :] = tops
        return carry

    lax.fori_loop(0, rows // block, step, 0, unroll=True)


def self_backward_kernel(
    low, grads, mixed_wide, level, cosine, sine, clip_column, out, key_pair, keys_turned, totals
):
    rows = grads.shape[0]
    pair = 2 * HEAD_DIM
    block = min(256, rows)
    keys_turned[...] = jnp.transpose(low[:, pair : 2 * pair])
    _, key_clips = clip_features(clip_column[...])
    key_pair[0], key_pair[1] = key_with_clips(low[:, pair : 2 * pair], key_clips)
    totals[...] = jnp.zeros_like(totals)
    out[rows:, 0:pair] = jnp.zeros((out.shape[0] - rows, pair), jnp.bfloat16)

    def step(index, carry):
        start = pl.multiple_of(index * block, block)
        place = pl.ds(start, block)
        query_clips, _ = clip_features(clip_column[place, :])
        query_turned, key_grad, value_grad = attend_rows_back(
            low[place, 0:pair],
            query_clips,
            (key_pair[0], key_pair[1]),
            keys_turned[...],
            low[:, 2 * pair : 3 * pair],
            grads[place, :],
            mixed_wide[place, :],
            level[place, :],
        )
        query_grad = jnp.transpose(query_turned) * SCORE_SCALE
        back = query_grad * cosine[place, :] - swap_halves(query_grad) * sine[place, :]
        out[place, 0:pair] = back.astype(jnp.bfloat16)
        totals[0] += key_grad
        totals[1] += value_grad
        return carry

    lax.fori_loop(0, rows // block, step, 0, unroll=True)
    key_grad = totals[0]
    back = key_grad * cosine[...] - swap_halves(key_grad) * sine[...]
    out[:, pair : 2 * pair] = back.astype(jnp.bfloat16)
    out[:, 2 * pair : 3 * pair] = totals[1].astype(jnp.bfloat16)


def cross_forward_kernel(query, keys, values, clip_column, text_column, mixed, mixed_wide, level):
    pair = 2 * HEAD_DIM
    query_clips, _ = clip_features(clip_column[...])
    _, key_clips = clip_features(text_column[...])
    for start in range(0, query.shape[1], pair):
        part = slice(start, start + pair)
        mixture, tops = attend_rows(
            query[:, part] * jnp.bfloat16(SCORE_SCALE),
            query_clips,
            key_with_clips(keys[:, part], key_clips),
            value_with_ones(values[:, part]),
        )
        mixed[:, part] = mixture.astype(jnp.bfloat16)
        mixed_wide[:, part] = mixture
        level[:, part] = tops


def cross_backward_kernel(
    query, keys, values, grads, mixed_wide, level, clip_column, text_column, query_out, key_out, value_out
):
    pair = 2 * HEAD_DIM
    query_clips, _ = clip_features(clip_column[...])
    _, key_clips = clip_features(text_column[...])
    for start in range(0, query.shape[1], pair):
        part = slice(start, start + pair)
        query_turned, key_grad, value_grad = attend_rows_back(
            query[:, part] * jnp.bfloat16(SCORE_SCALE),
            query_clips,
            key_with_clips(keys[:, part], key_clips),
            jnp.transpose(keys[:, part]),
            values[:, part],
            grads[:, part],
            mixed_wide[:, part],
            level[:, part],
        )
        query_out[:, part] = (jnp.transpose(query_turned) * SCORE_SCALE).astype(jnp.bfloat16)
        key_out[:, part] = key_grad.astype(jnp.bfloat16)
        value_out[:, part] = value_grad.astype(jnp.bfloat16)


def whole(array):
    return pl.BlockSpec(array.shape, lambda p: (0,) * array.ndim)


def lanes(rows, width=2 * HEAD_DIM, second=False):
    return pl.BlockSpec((rows, width), lambda p: (1 if second else 0, p))


CROSS_PAIRS = 3
KERNEL_PARAMS = pltpu.CompilerParams(
    dimension_semantics=("arbitrary",), vmem_limit_bytes=48 * 1024 * 1024
)


def cost(microseconds):
    return pl.CostEstimate(
        flops=int(microseconds * 1e9), bytes_accessed=2**20, transcendentals=0
    )


def self_forward(projected, cosine, sine, clip_column, rows):
    total, width = projected.shape
    pair = 2 * HEAD_DIM
    pairs = width // (3 * pair)
    return pl.pallas_call(
        self_forward_kernel,
        grid=(pairs,),
        in_specs=[
            lanes(total, 3 * pair),
            whole(cosine),
            whole(sine),
            whole(clip_column),
        ],
        out_specs=[lanes(rows), lanes(rows), lanes(rows), lanes(total, 3 * pair)],
        out_shape=[
            jax.ShapeDtypeStruct((rows, pairs * pair), jnp.bfloat16),
            jax.ShapeDtypeStruct((rows, pairs * pair), jnp.float32),
            jax.ShapeDtypeStruct((rows, pairs * pair), jnp.float32),
            jax.ShapeDtypeStruct((total, width), jnp.bfloat16),
        ],
        scratch_shapes=[
            pltpu.VMEM((2, total, pair), jnp.bfloat16),
            pltpu.VMEM((2, total, pair), jnp.bfloat16),
        ],
        compiler_params=KERNEL_PARAMS,
        cost_estimate=cost(120),
    )(projected, cosine, sine, clip_column)


def self_backward(low, grads, mixed_wide, level, cosine, sine, clip_column):
    total, width = low.shape
    rows = grads.shape[0]
    pair = 2 * HEAD_DIM
    pairs = width // (3 * pair)
    return pl.pallas_call(
        self_backward_kernel,
        grid=(pairs,),
        in_specs=[
            lanes(total, 3 * pair),
            lanes(rows),
            lanes(rows),
            lanes(rows),
            whole(cosine),
            whole(sine),
            whole(clip_column),
        ],
        out_specs=lanes(total, 3 * pair),
        out_shape=jax.ShapeDtypeStruct((total, width), jnp.bfloat16),
        scratch_shapes=[
            pltpu.VMEM((2, total, pair), jnp.bfloat16),
            pltpu.VMEM((pair, total), jnp.bfloat16),
            pltpu.VMEM((2, total, pair), jnp.float32),
        ],
        compiler_params=KERNEL_PARAMS,
        cost_estimate=cost(2),
    )(low, grads, mixed_wide, level, cosine, sine, clip_column)


def cross_forward(query, keyval, clip_column, text_column):
    rows, width = query.shape
    keys = keyval.shape[0] // 2
    group = 2 * HEAD_DIM * CROSS_PAIRS
    steps = width // group
    return pl.pallas_call(
        cross_forward_kernel,
        grid=(steps,),
        in_specs=[
            lanes(rows, group),
            lanes(keys, group),
            lanes(keys, group, second=True),
            whole(clip_column),
            whole(text_column),
        ],
        out_specs=[lanes(rows, group), lanes(rows, group), lanes(rows, group)],
        out_shape=[
            jax.ShapeDtypeStruct((rows, width), jnp.bfloat16),
            jax.ShapeDtypeStruct((rows, width), jnp.float32),
            jax.ShapeDtypeStruct((rows, width), jnp.float32),
        ],
        compiler_params=KERNEL_PARAMS,
        cost_estimate=cost(20),
    )(query, keyval, keyval, clip_column, text_column)


def cross_backward(query, keyval, grads, mixed_wide, level, clip_column, text_column):
    rows, width = query.shape
    keys = keyval.shape[0] // 2
    group = 2 * HEAD_DIM * CROSS_PAIRS
    steps = width // group
    return pl.pallas_call(
        cross_backward_kernel,
        grid=(steps,),
        in_specs=[
            lanes(rows, group),
            lanes(keys, group),
            lanes(keys, group, second=True),
            lanes(rows, group),
            lanes(rows, group),
            lanes(rows, group),
            whole(clip_column),
            whole(text_column),
        ],
        out_specs=[lanes(rows, group), lanes(keys, group), lanes(keys, group)],
        out_shape=[
            jax.ShapeDtypeStruct((rows, width), jnp.bfloat16),
            jax.ShapeDtypeStruct((keys, width), jnp.bfloat16),
            jax.ShapeDtypeStruct((keys, width), jnp.bfloat16),
        ],
        compiler_params=KERNEL_PARAMS,
        cost_estimate=cost(120),
    )(query, keyval, keyval, grads, mixed_wide, level, clip_column, text_column)


def norm_forward(hidden):
    centre = jnp.mean(hidden, axis=-1, keepdims=True)
    centred = hidden - centre
    spread = jnp.mean(centred * centred, axis=-1, keepdims=True)
    scale_inv = lax.rsqrt(spread + EPSILON)
    return (centred * scale_inv, scale_inv)


def norm_backward(grad_norm, normalized, scale_inv, gain_vector):
    scaled = grad_norm * gain_vector
    gain_grad = jnp.sum(grad_norm * normalized, axis=0)
    inner = (
        scaled
        - jnp.mean(scaled, axis=-1, keepdims=True)
        - normalized * jnp.mean(scaled * normalized, axis=-1, keepdims=True)
    )
    return (scale_inv * inner, gain_grad)


def rotary_tables(positions):
    half_width = HEAD_DIM // 2
    frequencies = jnp.exp(
        -math.log(10000.0) * jnp.arange(half_width, dtype=jnp.float32) / half_width
    )
    angles = positions[:, None] * frequencies
    cosine, sine = jnp.cos(angles), jnp.sin(angles)
    return (
        jnp.concatenate([cosine, cosine, cosine, cosine], axis=1),
        jnp.concatenate([-sine, sine, -sine, sine], axis=1),
    )


def time_features(step_values):
    half_width = TFEAT // 2
    frequencies = jnp.exp(
        -math.log(10000.0) * jnp.arange(half_width, dtype=jnp.float32) / half_width
    )
    angles = step_values.astype(jnp.float32)[..., None] * frequencies
    return jnp.concatenate([jnp.cos(angles), jnp.sin(angles)], axis=-1)


def gated_back(hidden_grad, gate_part, upward):
    gate_sigmoid = jax.nn.sigmoid(gate_part)
    gate_grad = hidden_grad * upward * gate_sigmoid * (1.0 + gate_part * (1.0 - gate_sigmoid))
    upward_grad = hidden_grad * gate_part * gate_sigmoid
    return jnp.concatenate([gate_grad, upward_grad], axis=-1).astype(jnp.bfloat16)


def xor_pairs(count, bit):
    return [(k, k ^ bit) for k in range(count)]


def place(buffer, block, dim, index):
    starts = [0] * buffer.ndim
    starts[dim] = index
    return lax.dynamic_update_slice(buffer, block, tuple(starts))


def take(array, index, dim=0):
    return lax.dynamic_slice_in_dim(array, index, 1, axis=dim)


def plane_bits(count):
    return [1 << b for b in range(1, count.bit_length() - 1)]


def line_swap(blocks, split=0, join=0):
    return lax.all_to_all(blocks, "seq", split, join, tiled=True)


def dot(left, right):
    return jnp.dot(left, right, preferred_element_type=jnp.float32)


def tie(*values):
    return lax.optimization_barrier(values)


def flip(values, bit):
    return lax.ppermute(values, "dp", xor_pairs(lax.axis_size("dp"), bit))


def two_by_two():
    return lax.axis_size("dp") == 8


def assemble(pieces, shapes, moves, places):
    count = len(pieces)

    def kernel(places_ref, *refs):
        given, results, semaphores = refs[:count], refs[count:-1], refs[-1]
        copies = []
        for number, (piece, source, result, target) in enumerate(moves):
            copy = pltpu.make_async_copy(
                given[piece].at[source(places_ref)],
                results[result].at[target(places_ref)],
                semaphores.at[number],
            )
            copy.start()
            copies.append(copy)
        for copy in copies:
            copy.wait()

    size = sum(2 * math.prod(shape) for shape in shapes)
    return pl.pallas_call(
        kernel,
        in_specs=[pl.BlockSpec(memory_space=pltpu.SMEM)]
        + [pl.BlockSpec(memory_space=pl.ANY)] * count,
        out_specs=[pl.BlockSpec(memory_space=pltpu.VMEM)] * len(shapes),
        out_shape=[jax.ShapeDtypeStruct(shape, jnp.bfloat16) for shape in shapes],
        scratch_shapes=[pltpu.SemaphoreType.DMA((len(moves),))],
        compiler_params=pltpu.CompilerParams(vmem_limit_bytes=48 * 1024 * 1024),
        cost_estimate=pl.CostEstimate(flops=0, bytes_accessed=2 * size, transcendentals=0),
    )(places, *pieces)


def everything(places):
    return slice(None)


def at(*index):
    return lambda places: index


def plane_open(values):
    if not two_by_two():
        return (values,)
    return (values, flip(values, 2), flip(values, 4))


def plane_relay(state):
    if not two_by_two():
        return state
    values, by_first, by_second = state
    half = values.shape[0] // 2
    return state + (flip(by_first[:half], 4), flip(by_second[half:], 2))


def plane_chips(state, chip=None):
    values = state[0]
    chips = lax.axis_size("dp") // 2
    if not two_by_two():
        same = values[None]
        for bit in plane_bits(2 * chips):
            same = jnp.concatenate([same, flip(same, bit)], axis=0)
        if chip is None:
            return same
        ordered = jnp.zeros(same.shape, same.dtype)
        for r in range(chips):
            ordered = place(ordered, same[r : r + 1], 0, chip ^ r)
        return ordered
    half = values.shape[0] // 2
    rest = values.shape[0] - half

    def target(r, *more):
        if chip is None:
            return at(r, *more)
        return lambda places: (places[0] ^ r,) + more

    moves = [(r, everything, 0, target(r)) for r in range(3)]
    moves.append((3, everything, 0, target(3, pl.ds(0, half))))
    moves.append((4, everything, 0, target(3, pl.ds(half, rest))))
    places = jnp.zeros((1,), jnp.int32) if chip is None else chip.reshape(1).astype(jnp.int32)
    return assemble(state, [(chips,) + values.shape], moves, places)[0]


def both_cores(same, other, core, rows):
    chips, line, _, width = same.shape
    if two_by_two() and all(count % 16 == 0 for count in rows):
        moves, start = [], 0
        for result, count in enumerate(rows):
            part = at(slice(None), slice(None), pl.ds(start, count))
            moves.append((0, part, result, lambda places: (slice(None), places[0])))
            moves.append((1, part, result, lambda places: (slice(None), 1 - places[0])))
            start += count
        return assemble(
            [same, other],
            [(chips, 2, line, count, width) for count in rows],
            moves,
            core.reshape(1).astype(jnp.int32),
        )
    full = jnp.zeros((chips, 2) + same.shape[1:], same.dtype)
    full = place(place(full, same[:, None], 1, core), other[:, None], 1, 1 - core)
    results, start = [], 0
    for count in rows:
        results.append(full[:, :, :, start : start + count])
        start += count
    return results


def plane_far(blocks):
    if not two_by_two():
        return None
    half = blocks[3].shape[0] // 2
    low = jnp.bfloat16
    return (flip(blocks[3][:half].astype(low), 2), flip(blocks[3][half:].astype(low), 4))


def plane_near(blocks, far):
    low, wide = jnp.bfloat16, jnp.float32
    if not two_by_two():
        total = jnp.stack([block.astype(wide) for block in blocks], axis=0)
        for bit in reversed(plane_bits(lax.axis_size("dp"))):
            middle = total.shape[0] // 2
            got = flip(total[middle:].astype(low), bit)
            total = total[:middle] + got.astype(wide)
        return (total[0],)
    half = blocks[3].shape[0] // 2
    to_first = jnp.concatenate(
        [
            blocks[1][:half].astype(low),
            (blocks[1][half:].astype(wide) + far[1].astype(wide)).astype(low),
        ],
        axis=0,
    )
    to_second = jnp.concatenate(
        [
            (blocks[2][:half].astype(wide) + far[0].astype(wide)).astype(low),
            blocks[2][half:].astype(low),
        ],
        axis=0,
    )
    return (blocks[0], flip(to_first, 2), flip(to_second, 4))


def plane_total(near):
    total = near[0].astype(jnp.float32)
    for got in near[1:]:
        total = total + got.astype(jnp.float32)
    return total


def spread_pairs(blocks, own_width):
    line, rows, _ = blocks.shape
    pair = 2 * HEAD_DIM

    def kernel(given, result):
        for source in range(line):
            for number in range(own_width // pair):
                for part in range(3):
                    start = part * D + source * own_width + number * pair
                    taken = (3 * number + part) * pair
                    result[:, start : start + pair] = given[
                        source, :, taken : taken + pair
                    ].astype(jnp.float32)

    return pl.pallas_call(
        kernel,
        out_shape=jax.ShapeDtypeStruct((rows, 3 * D), jnp.float32),
        cost_estimate=cost(1),
    )(blocks)


def whole_grad_kernel(places, *refs):
    lefts, rights, outs = refs[:8], refs[8:16], refs[16:]
    for weight in range(4):
        total = None
        for side in range(2):
            left, right = lefts[2 * weight + side], rights[2 * weight + side]
            half = left.shape[1] // 2
            rows = jnp.where(places[1] == 0, left[:, :half], left[:, half:])
            part = lax.dot_general(
                rows, right[...], (((0,), (0,)), ((), ())), preferred_element_type=jnp.float32
            )
            total = part if total is None else total + part
        out = outs[weight // 2]
        line, count = out.shape[1], out.shape[2] // 2
        start = weight % 2 * count
        for place_of in range(line):
            out[0, place_of, start : start + count, :] = total[
                place_of * count : (place_of + 1) * count
            ].astype(jnp.bfloat16)


def whole_grad_blocks(lefts, rights, chip, core):
    chips, line = lax.axis_size("dp") // 2, lax.axis_size("seq")
    shard = D // (2 * chips * line)
    if two_by_two() and shard % 16 == 0:
        width = 2 * line * shard

        def left_spec(array):
            return pl.BlockSpec((array.shape[0], width), lambda r, places: (0, places[0] ^ r))

        def right_spec(array):
            return pl.BlockSpec(
                array.shape, lambda r, places: (0, 0), pipeline_mode=pl.Buffered(1)
            )

        flat_lefts = [side for pair in lefts for side in pair]
        flat_rights = [side for pair in rights for side in pair]
        out_shape = (chips, line, 2 * shard, D)
        outs = pl.pallas_call(
            whole_grad_kernel,
            grid_spec=pltpu.PrefetchScalarGridSpec(
                num_scalar_prefetch=1,
                grid=(chips,),
                in_specs=[left_spec(array) for array in flat_lefts]
                + [right_spec(array) for array in flat_rights],
                out_specs=[
                    pl.BlockSpec((1,) + out_shape[1:], lambda r, places: (r, 0, 0, 0))
                    for _ in range(2)
                ],
            ),
            out_shape=[jax.ShapeDtypeStruct(out_shape, jnp.bfloat16) for _ in range(2)],
            compiler_params=KERNEL_PARAMS,
            cost_estimate=cost(0.1),
        )(jnp.stack([chip, core]).astype(jnp.int32), *flat_lefts, *flat_rights)
        return [[out[r] for r in range(chips)] for out in outs]
    grads = []
    for (left, left_other), (right, right_other) in zip(lefts, rights):
        grad = (dot(left.T, right) + dot(left_other.T, right_other)).astype(jnp.bfloat16)
        grads.append(take(grad.reshape(chips, 2, line, shard, D), core, 1)[:, 0])
    return [
        [jnp.concatenate([take(grad, chip ^ r)[0] for grad in group], axis=1) for r in range(chips)]
        for group in (grads[:2], grads[2:])
    ]


def on_device(
    latents,
    context,
    clip_bounds,
    timesteps,
    self_inward,
    self_outward,
    cross_query,
    cross_keyval,
    cross_return,
    time_weight,
    expand_weight,
    shrink_weight,
    gain_attend,
    gain_cross,
    gain_feed,
    cotangent,
):
    f32, bf16 = jnp.float32, jnp.bfloat16
    frame_count = latents.shape[1]
    dp_count = lax.axis_size("dp")
    seq_count = lax.axis_size("seq")
    dp_place = lax.axis_index("dp")
    seq_place = lax.axis_index("seq")
    row_length = frame_count * seq_count
    text_count = context.shape[1]
    own_heads = HEADS // seq_count
    pairs = (own_heads + 1) // 2
    own_width = own_heads * HEAD_DIM
    pair_width = 2 * HEAD_DIM
    padded = pairs * pair_width
    hidden_width = FF // dp_count
    shard = D // (dp_count * seq_count)
    time_shard = TFEAT // (dp_count * seq_count)
    place_all = dp_place * seq_count + seq_place
    chip_place, core_place = dp_place // 2, dp_place % 2
    chips = dp_count // 2

    all_frames = jnp.arange(row_length, dtype=jnp.int32)
    second_start, third_start = clip_bounds[0, 0], clip_bounds[0, 1]
    frame_clips = (all_frames >= second_start).astype(jnp.int32) + (
        all_frames >= third_start
    ).astype(jnp.int32)
    clip_starts = jnp.where(
        frame_clips == 0, 0, jnp.where(frame_clips == 1, second_start, third_start)
    )
    token_slots = jnp.arange(TOKEN_ROWS, dtype=jnp.int32)
    clips = jnp.concatenate(
        [frame_clips, jnp.where(token_slots < CLIPS, token_slots, -1)]
    ).astype(f32)
    positions = jnp.concatenate(
        [all_frames - clip_starts + 1, jnp.zeros(TOKEN_ROWS, jnp.int32)]
    ).astype(f32)
    cosine, sine = rotary_tables(positions)
    clip_column = clips[:, None]
    own_clips = lax.dynamic_slice_in_dim(clips, seq_place * frame_count, frame_count)
    text_clips = (jnp.arange(text_count, dtype=jnp.int32) // CTX_LEN).astype(f32)

    def by_pairs(blocks):
        blocks = jnp.pad(blocks, ((0, 0),) * 3 + ((0, padded - own_width),))
        return (
            blocks.reshape(seq_count, shard, 3, pairs, pair_width)
            .transpose(0, 1, 3, 2, 4)
            .reshape(seq_count, shard, 3 * padded)
        )

    def from_pairs(blocks):
        return (
            blocks.reshape(seq_count, shard, pairs, 3, pair_width)
            .transpose(0, 1, 3, 2, 4)
            .reshape(seq_count, shard, 3, padded)[..., :own_width]
        )

    inward_blocks = by_pairs(
        self_inward.reshape(shard, 3, seq_count, own_width).transpose(2, 0, 1, 3)
    )
    extra = jnp.concatenate([time_weight.reshape(-1), gain_attend, gain_cross, gain_feed])
    extra_rows = -(-extra.shape[0] // (16 * 3 * padded)) * 16
    extra = jnp.pad(extra, (0, extra_rows * 3 * padded - extra.shape[0]))
    extra = jnp.broadcast_to(
        extra.reshape(1, extra_rows, 3 * padded), (seq_count, extra_rows, 3 * padded)
    )
    inward_send = jnp.concatenate([inward_blocks, extra], axis=1)
    expand_blocks = (
        expand_weight.reshape(shard, 2, dp_count, hidden_width)
        .transpose(2, 0, 1, 3)
        .reshape(dp_count, shard, 2 * hidden_width)
    )

    spread_rows = jnp.arange(D, dtype=jnp.int32)[None, :]
    context_rows = jnp.arange(D // 2, dtype=jnp.int32)[:, None]
    group, within = context_rows // (shard // 2), context_rows % (shard // 2)
    spread_keys = (spread_rows == group * shard + within).astype(bf16)
    spread_values = (spread_rows == group * shard + shard // 2 + within).astype(bf16)
    stacked = jnp.concatenate(
        [
            latents[0],
            self_outward,
            cross_query,
            cross_keyval[:, :D],
            cross_keyval[:, D:],
            cross_return,
        ],
        axis=0,
    )
    lined = lax.all_gather(stacked, "seq")
    inward_columns = line_swap(inward_send)
    context_spread = jnp.concatenate(
        [dot(context[0], spread_keys).astype(bf16), dot(context[0], spread_values).astype(bf16)],
        axis=0,
    )
    inward_columns, cotangent, expand_blocks, context_spread, cosine, sine = tie(
        inward_columns, cotangent, expand_blocks, context_spread, cosine, sine
    )

    inward_state = plane_open(inward_columns)
    cotangent_state = plane_open(cotangent[0])
    expand_part = lax.all_to_all(expand_blocks, "dp", 0, 0, tiled=True)
    inward_state, cotangent_state = tie(inward_state, cotangent_state)

    inward_state = plane_relay(inward_state)
    cotangent_state = plane_relay(cotangent_state)
    inward_same = plane_chips(inward_state, chip_place)
    inward_same, cotangent_state, expand_part = tie(inward_same, cotangent_state, expand_part)

    inward_other = flip(inward_same, 1)
    cotangent_same = plane_chips(cotangent_state)
    inward_other, cotangent_same = tie(inward_other, cotangent_same)

    inward_own, extra_all = both_cores(
        inward_same, inward_other, core_place, [shard, extra_rows]
    )
    inward_own = inward_own.reshape(D, 3 * padded)
    extra_all = extra_all.reshape(dp_count, seq_count, extra_rows * 3 * padded)
    time_full = extra_all[:, :, : time_shard * D].reshape(TFEAT, D)
    gains_all = extra_all[:, :, time_shard * D : time_shard * D + 3 * shard]
    gains_all = gains_all.reshape(dp_count, seq_count, 3, shard).astype(f32)
    attend_gain = gains_all[:, :, 0].reshape(D)
    cross_gain = gains_all[:, :, 1].reshape(D)
    feed_gain = gains_all[:, :, 2].reshape(D)
    feats_low = time_features(timesteps[0]).astype(bf16)
    token = dot(feats_low, time_full)
    token_norm, token_inverse = norm_forward(token)
    token_low = jnp.pad(
        (token_norm * attend_gain).astype(bf16), ((0, TOKEN_ROWS - CLIPS), (0, 0))
    )
    joined = two_by_two() and 2 * hidden_width == D and shard % 16 == 0
    early_parts = dp_count // 4 if joined else 0
    ffn_early = shrink_weight
    if joined:
        ffn_early = jnp.concatenate(
            [shrink_weight, expand_part[:early_parts].reshape(early_parts * shard, D)], axis=0
        )
    ffn_early = lax.all_gather(ffn_early, "seq")
    cotangent_other = flip(cotangent_same, 1)
    cotangent_other, inward_own, token_low, lined, cross_gain, feed_gain = tie(
        cotangent_other, inward_own, token_low, lined, cross_gain, feed_gain
    )

    def weight_rows(first, count):
        start = frame_count + first * shard
        return lined[:, start : start + count * shard]

    first_state = plane_open(weight_rows(0, 2))
    row_latents = lined[:, :frame_count].reshape(row_length, D)
    row_norm, row_inverse = norm_forward(row_latents.astype(f32))
    row_low = jnp.concatenate([(row_norm * attend_gain).astype(bf16), token_low], axis=0)
    projected = dot(row_low, inward_own)
    projected, first_state, lined = tie(projected, first_state, lined)

    first_state = plane_relay(first_state)
    second_state = plane_open(weight_rows(2, 2))
    attended, attended_wide, self_level, projected_low = self_forward(
        projected, cosine, sine, clip_column, row_length
    )
    attended, first_state, second_state, ffn_early = tie(
        attended, first_state, second_state, ffn_early
    )

    attended_low = line_swap(attended[:, :own_width], 0, 1)
    first_same = plane_chips(first_state, chip_place)
    first_other = flip(first_same, 1)
    second_state = plane_relay(second_state)
    attended_low, first_same, first_other, second_state, expand_part = tie(
        attended_low, first_same, first_other, second_state, expand_part
    )

    expand_lined = lax.all_gather(expand_part[early_parts:], "seq")
    outward_full, query_full = [
        weight.reshape(D, D)
        for weight in both_cores(first_same, first_other, core_place, [shard] * 2)
    ]
    second_same = plane_chips(second_state, chip_place)
    second_other = flip(second_same, 1)
    context_other = flip(context_spread, 1)
    after_self = latents[0].astype(f32) + dot(attended_low, outward_full)
    norm_two, inverse_two = norm_forward(after_self)
    normed_two = (norm_two * cross_gain).astype(bf16)
    cross_heads = dot(normed_two, query_full).astype(bf16)
    attended_other = flip(attended_low, 1)
    cross_heads, second_same, second_other, attended_other, context_other = tie(
        cross_heads, second_same, second_other, attended_other, context_other
    )

    keyval_full, return_full = [
        weight.reshape(D, D)
        for weight in both_cores(second_same, second_other, core_place, [shard] * 2)
    ]
    keyval = dot(context_spread, keyval_full).astype(bf16)
    crossed, crossed_wide, cross_level = cross_forward(
        cross_heads, keyval, own_clips[:, None], text_clips[:, None]
    )
    normed_two_other = flip(normed_two, 1)
    crossed, return_full, normed_two_other = tie(crossed, return_full, normed_two_other)

    after_cross = after_self + dot(crossed, return_full)
    norm_three, inverse_three = norm_forward(after_cross)
    normed_three = (norm_three * feed_gain).astype(bf16)
    crossed_other = flip(crossed, 1)
    normed_three, ffn_early, cotangent_same, cotangent_other = tie(
        normed_three, ffn_early, cotangent_same, cotangent_other
    )
    frames_state = plane_relay(plane_open(normed_three))
    half_frames = chips * frame_count
    tangents = [cotangent_same.reshape(half_frames, D), cotangent_other.reshape(half_frames, D)]
    shrink_own = ffn_early
    if joined:
        shrink_own = assemble(
            [ffn_early],
            [(seq_count, hidden_width // seq_count, D)],
            [(0, at(slice(None), pl.ds(0, hidden_width // seq_count)), 0, everything)],
            jnp.zeros((1,), jnp.int32),
        )[0]
    shrink_own = shrink_own.reshape(hidden_width, D)
    hidden_grads = [dot(side, shrink_own.T) for side in tangents]
    frames_same = plane_chips(frames_state)
    frames_same, expand_lined, crossed_other, hidden_grads = tie(
        frames_same, expand_lined, crossed_other, hidden_grads
    )

    if joined:
        moves = []
        for line in range(seq_count):
            target = at(pl.ds(early_parts, dp_count - early_parts), line)
            moves.append((1, at(line), 0, target))
            for part in range(early_parts):
                rows = pl.ds(hidden_width // seq_count + part * shard, shard)
                moves.append((0, at(line, rows), 0, at(part, line)))
        expand_own = assemble(
            [ffn_early, expand_lined],
            [(dp_count, seq_count, shard, 2 * hidden_width)],
            moves,
            jnp.zeros((1,), jnp.int32),
        )[0]
    else:
        expand_own = expand_lined.transpose(1, 0, 2, 3)
    expand_own = expand_own.reshape(D, 2 * hidden_width)
    half_frames = chips * frame_count
    frames_other = flip(frames_same, 1)
    frames = [frames_same.reshape(half_frames, D), frames_other.reshape(half_frames, D)]
    tangents = [cotangent_same.reshape(half_frames, D), cotangent_other.reshape(half_frames, D)]
    hidden_low, expand_low = [], []
    for side in range(2):
        gate_up = dot(frames[side], expand_own)
        gate_part = gate_up[:, :hidden_width]
        upward = gate_up[:, hidden_width:]
        hidden_low.append((jax.nn.silu(gate_part) * upward).astype(bf16))
        hidden_grad = hidden_grads[side]
        expand_low.append(gated_back(hidden_grad, gate_part, upward))

    def sides(array):
        return array.astype(bf16).reshape(chips, frame_count, D)

    shrink_part = (
        dot(hidden_low[0].T, tangents[0]) + dot(hidden_low[1].T, tangents[1])
    ).astype(bf16)
    shrink_part, hidden_low, expand_low = tie(shrink_part, hidden_low, expand_low)
    grad_shrink = lax.psum_scatter(shrink_part, "seq", scatter_dimension=0, tiled=True)
    feed_other = sides(dot(expand_low[1], expand_own.T))
    feed_got = flip(feed_other, 1)
    feed_same = sides(dot(expand_low[0], expand_own.T))
    feed_same, feed_got, hidden_low, expand_low = tie(feed_same, feed_got, hidden_low, expand_low)
    feed_blocks = [feed_same[r].astype(f32) + feed_got[r].astype(f32) for r in range(chips)]
    feed_far = plane_far(feed_blocks)
    fed_other = sides(dot(hidden_low[1], shrink_own))
    fed_got = flip(fed_other, 1)
    fed_same = sides(dot(hidden_low[0], shrink_own))
    feed_far, fed_got, fed_same, expand_low = tie(feed_far, fed_got, fed_same, expand_low)

    feed_near = plane_near(feed_blocks, feed_far)
    expand_grad = (dot(frames[0].T, expand_low[0]) + dot(frames[1].T, expand_low[1])).astype(bf16)
    expand_grad = expand_grad.reshape(dp_count, seq_count, shard, 2 * hidden_width)
    expand_grad = expand_grad.transpose(1, 0, 2, 3).reshape(D, 2 * hidden_width)
    feed_near, expand_grad = tie(feed_near, expand_grad)
    expand_sum = lax.psum_scatter(expand_grad, "seq", scatter_dimension=0, tiled=True)
    expand_sum = expand_sum.reshape(dp_count, shard, 2 * hidden_width)

    def open_grad(grad):
        grad = grad.astype(bf16).reshape(chips, 2, seq_count, shard, -1)
        return grad, flip(take(grad, 1 - core_place, 1), 1)

    def side_block(opened, r):
        return jnp.concatenate(
            [
                (
                    take(take(grad, core_place, 1), chip_place ^ r)[0, 0].astype(f32)
                    + take(got, chip_place ^ r)[0, 0].astype(f32)
                ).astype(bf16)
                for grad, got in opened
            ],
            axis=1,
        )

    def side_blocks(opened):
        return [side_block(opened, r) for r in range(chips)]

    feed_norm_grad = plane_total(feed_near)
    feed_term, feed_gain_part = norm_backward(
        feed_norm_grad, norm_three, inverse_three, feed_gain
    )
    after_cross_grad = cotangent[0].astype(f32) + feed_term
    return_low = after_cross_grad.astype(bf16)
    crossed_grad = dot(return_low, return_full.T).astype(bf16)
    return_other = flip(return_low, 1)
    crossed_grad, return_low, return_other, grad_shrink = tie(
        crossed_grad, return_low, return_other, grad_shrink
    )
    cross_query_low, cross_key_low, cross_value_low = cross_backward(
        cross_heads,
        keyval,
        crossed_grad,
        crossed_wide,
        cross_level,
        own_clips[:, None],
        text_clips[:, None],
    )
    cross_query_low, cross_key_low, cross_value_low = tie(
        cross_query_low, cross_key_low, cross_value_low
    )
    cross_norm_grad = dot(cross_query_low, query_full.T)
    cross_term, cross_gain_part = norm_backward(
        cross_norm_grad, norm_two, inverse_two, cross_gain
    )
    after_self_grad = after_cross_grad + cross_term
    outward_low = after_self_grad.astype(bf16)
    attended_grad = dot(outward_low, outward_full.T).astype(bf16)
    keyval_low = jnp.concatenate([cross_key_low, cross_value_low], axis=0)
    keyval_low_other = flip(keyval_low, 1)
    cross_query_other = flip(cross_query_low, 1)
    queries_in, returns_in = (cross_query_low, cross_query_other), (return_low, return_other)
    attended_grad, outward_low, keyval_low, keyval_low_other, queries_in, returns_in = tie(
        attended_grad, outward_low, keyval_low, keyval_low_other, queries_in, returns_in
    )

    attended_grad_own = line_swap(attended_grad, 1, 0)
    outward_other = flip(outward_low, 1)
    halves = whole_grad_blocks(
        [(crossed, crossed_other), (context_spread, context_other)]
        + [(normed_two, normed_two_other), (attended_low, attended_other)],
        [returns_in, (keyval_low, keyval_low_other), queries_in, (outward_low, outward_other)],
        chip_place,
        core_place,
    )
    attended_grad_own, halves = tie(attended_grad_own, halves)
    half_far = [plane_far(blocks) for blocks in halves]

    attended_grad_own = jnp.pad(attended_grad_own, ((0, 0), (0, padded - own_width)))
    inward_low = self_backward(
        projected_low,
        attended_grad_own,
        attended_wide,
        self_level,
        cosine,
        sine,
        clip_column,
    )
    attend_parts = dot(inward_low, inward_own.T)
    attend_low = attend_parts[:row_length].astype(bf16)
    attend_sum = lax.psum_scatter(attend_low, "seq", scatter_dimension=0, tiled=True)
    inward_low, attend_parts, halves, half_far, expand_sum = tie(
        inward_low, attend_parts, halves, half_far, expand_sum
    )

    near_early = plane_near(halves[0], half_far[0])
    near_late = plane_near(halves[1], half_far[1])
    inward_grad = open_grad(dot(row_low.T, inward_low))
    token_term, token_gain_part = norm_backward(
        attend_parts[row_length : row_length + CLIPS], token_norm, token_inverse, attend_gain
    )
    attend_gain_part = jnp.sum(attend_parts[:row_length] * row_norm, axis=0) + token_gain_part
    feats_row = feats_low.astype(f32).reshape(-1)
    device_count = dp_count * seq_count
    gain_parts = jnp.stack([attend_gain_part, cross_gain_part, feed_gain_part], axis=0)
    gain_parts = gain_parts.reshape(3, device_count, shard).transpose(1, 0, 2)
    common = jnp.concatenate([token_term.reshape(-1), feats_row]).astype(bf16)
    small = jnp.concatenate(
        [
            jnp.broadcast_to(common[None], (device_count,) + common.shape),
            gain_parts.reshape(device_count, 3 * shard).astype(bf16),
        ],
        axis=1,
    )
    small = jnp.pad(small, ((0, 0), (0, -small.shape[1] % 2048)))
    small = small.reshape(device_count, -1, 128)
    inward_grad, small, near_early, near_late, attend_sum = tie(
        inward_grad, small, near_early, near_late, attend_sum
    )

    whole_column = jnp.concatenate(
        [plane_total(near_early).astype(bf16), plane_total(near_late).astype(bf16)], axis=1
    )
    whole_sums = lax.psum_scatter(whole_column, "seq", scatter_dimension=0)
    expand_rows = lax.all_to_all(expand_sum, "dp", 0, 0, tiled=True)
    inward_blocks = side_blocks([inward_grad])
    inward_far = plane_far(inward_blocks)
    inward_blocks, inward_far, small, expand_rows = tie(
        inward_blocks, inward_far, small, expand_rows
    )

    inward_near = plane_near(inward_blocks, inward_far)
    small_all = lax.all_to_all(small, ("dp", "seq"), 0, 0, tiled=True).astype(f32)
    fed_blocks = [fed_same[r].astype(f32) + fed_got[r].astype(f32) for r in range(chips)]
    fed_far = plane_far(fed_blocks)
    inward_near, small_all, fed_far, attend_sum = tie(
        inward_near, small_all, fed_far, attend_sum
    )

    inward_rows = line_swap(plane_total(inward_near).astype(bf16))
    fed_near = plane_near(fed_blocks, fed_far)
    grad_expand = (
        expand_rows.reshape(dp_count, shard, 2, hidden_width)
        .transpose(1, 2, 0, 3)
        .reshape(shard, 2 * FF)
        .astype(f32)
    )
    inward_rows, fed_near, grad_expand, whole_sums = tie(
        inward_rows, fed_near, grad_expand, whole_sums
    )

    block_output = (after_cross + plane_total(fed_near)).astype(bf16)
    own_norm = lax.dynamic_slice_in_dim(row_norm, seq_place * frame_count, frame_count, axis=0)
    own_inverse = lax.dynamic_slice_in_dim(
        row_inverse, seq_place * frame_count, frame_count, axis=0
    )
    attend_term, _ = norm_backward(
        attend_sum.astype(f32), own_norm, own_inverse, attend_gain
    )
    latents_grad = (after_self_grad + attend_term)[None]
    grad_shrink = grad_shrink.astype(f32)
    if own_width % pair_width == 0:
        grad_inward = spread_pairs(inward_rows, own_width)
    else:
        grad_inward = (
            from_pairs(inward_rows).transpose(1, 2, 0, 3).reshape(shard, 3 * D).astype(f32)
        )
    grad_inward, block_output, latents_grad, whole_sums = tie(
        grad_inward, block_output, latents_grad, whole_sums
    )
    whole_sums = whole_sums.astype(f32)
    grad_return = whole_sums[:shard]
    grad_keyval = jnp.concatenate(
        [whole_sums[shard : shard + shard // 2], whole_sums[shard + shard // 2 : 2 * shard]],
        axis=1,
    )
    grad_query = whole_sums[2 * shard : 3 * shard]
    grad_outward = whole_sums[3 * shard :]
    small_all = small_all.reshape(device_count, -1)
    token_count, feats_count = CLIPS * D, CLIPS * TFEAT
    token_sum = jnp.sum(
        small_all[:, :token_count].reshape(dp_count, seq_count, CLIPS, D), axis=1
    )
    feats_all = small_all.reshape(dp_count, seq_count, -1)[:, 0]
    feats_all = feats_all[:, token_count : token_count + feats_count]
    feats_all = feats_all.reshape(dp_count, CLIPS, TFEAT)
    feats_own = lax.dynamic_slice_in_dim(feats_all, place_all * time_shard, time_shard, axis=2)
    grad_time = jnp.einsum(
        "rct,rcn->tn",
        feats_own,
        token_sum,
        precision=PRECISE,
        preferred_element_type=f32,
    )
    gain_start = token_count + feats_count
    gain_sums = jnp.sum(small_all[:, gain_start : gain_start + 3 * shard], axis=0)
    gain_sums = gain_sums.reshape(3, shard)
    return (
        block_output[None],
        latents_grad,
        grad_inward,
        grad_outward,
        grad_query,
        grad_keyval,
        grad_return,
        grad_time,
        grad_expand,
        grad_shrink,
        gain_sums[0],
        gain_sums[1],
        gain_sums[2],
    )


def solution(mesh):
    return jax.shard_map(
        on_device,
        mesh=mesh,
        in_specs=(
            P("dp", "seq", None),
            P("dp", None, None),
            P("dp", None),
            P("dp", None),
            P(("dp", "seq"), None),
            P(("dp", "seq"), None),
            P(("dp", "seq"), None),
            P(("dp", "seq"), None),
            P(("dp", "seq"), None),
            P(("dp", "seq"), None),
            P(("dp", "seq"), None),
            P(("dp", "seq"), None),
            P(("dp", "seq")),
            P(("dp", "seq")),
            P(("dp", "seq")),
            P("dp", "seq", None),
        ),
        out_specs=(
            P("dp", "seq", None),
            P("dp", "seq", None),
            P(("dp", "seq"), None),
            P(("dp", "seq"), None),
            P(("dp", "seq"), None),
            P(("dp", "seq"), None),
            P(("dp", "seq"), None),
            P(("dp", "seq"), None),
            P(("dp", "seq"), None),
            P(("dp", "seq"), None),
            P(("dp", "seq")),
            P(("dp", "seq")),
            P(("dp", "seq")),
        ),
        check_vma=False,
    )
```
